32 devices in a mesh: groups: 2 (over y), wide: 4 (over z), narrow: 4 (over x, core).
Axes of the slice: x: 2, y: 2, z: 4, core: 2. Of those that a mesh axis runs over, the one named last changes fastest.
Arguments:
- ssm_input: bfloat16 [4096, 2048], P(('groups', 'wide', 'narrow')), parts along dimension 0, may hold values from -6 to 6
- gate_input: bfloat16 [4096, 2048], P(('groups', 'wide', 'narrow')), parts along dimension 0, may hold values from -6 to 6
- b_proj: bfloat16 [4096, 128], P(('groups', 'wide', 'narrow')), parts along dimension 0, may hold values from -0.59765625 to 0.59765625
- c_proj: bfloat16 [4096, 128], P(('groups', 'wide', 'narrow')), parts along dimension 0, may hold values from -0.59765625 to 0.59765625
- dt_raw: float32 [4096, 32], P(('groups', 'wide', 'narrow')), parts along dimension 0, may hold values from -4 to 4
- a_log: float32 [32], replicated, may hold values from -5.3 to -0.7
- dt_bias: float32 [32], replicated, may hold values from -3.5 to -1.5
- d_skip: float32 [32], replicated, may hold values from 0.5 to 1.5
- norm_gain: float32 [2048], replicated, may hold values from 0.25 to 1.75
- state_in: float32 [32, 32, 64, 128], P(('groups', 'wide', 'narrow')), parts along dimension 0, may hold values from -6 to 6
- out_proj: bfloat16 [2048, 2048], P(None, 'narrow'), may hold values from -0.125 to 0.125
- expert_in: bfloat16 [16, 2048, 768], P(('wide', 'narrow')), may hold values from -0.125 to 0.125
- expert_out: bfloat16 [16, 384, 2048], P(('wide', 'narrow')), may hold values from -0.3125 to 0.3125
- route_ids: int32 [4096, 8], P(('groups', 'wide', 'narrow')), parts along dimension 0, may hold values from 0 to 15, all different within a row; in each aligned block of 128 rows (0 to 127, 128 to 255, ...) at most 80 rows name the same one
- route_weights: float32 [4096, 8], P(('groups', 'wide', 'narrow')), parts along dimension 0, may hold values from 0.05 to 0.3
Outputs:
- layer_out: bfloat16 [4096, 2048], P(('groups', 'wide', 'narrow')), parts along dimension 0
- state_out: float32 [32, 32, 64, 128], P(('groups', 'wide', 'narrow')), parts along dimension 0
The draws below stay inside these ranges and needn't reach their ends.
There are 2 independent parts, one for each index of `groups`. The reference program is written for one: setup_inputs(seed, part) draws one part's arguments, and reference() takes and returns one part's arrays. A program takes and returns all parts, laid end to end along the dimension named above; an argument that names none is the same for every part. Nothing has to cross between parts.
Inputs may be any that keep to these rules, and one draw needn't show every extreme that they name: `route_ids`: each row names 8 different experts; among the rows of one clip no expert is named more than 80 times, and that count is reached in some clip of every draw.
All inputs are finite; a program needn't handle non-finite values.
Results may differ from the reference program's by a relative error of at most 0.0063.
Values may be sent and summed in bfloat16 or wider, within the bound.
No kernel may reach another device: no remote copies, remote signals or barrier semaphores. Data moves between devices by JAX's collectives and lax.ppermute only.
A program may use at most 128 MiB of HBM per device.

```python
import math
import jax
import jax.numpy as jnp
import numpy as np
from jax import lax

D = 2048
H = 32
P_SIZE = 64
N = 128
DIN = 2048
FF_E = 384
TOPK = 8
EXPERTS = 16
TOK_DEV = 128
CLIPS = 16
TOKENS = 2048
CAP = 80


def block_scale(stream_key, dims, cuts, low, top_value):
    factor_of = 1.0
    for position, parts in cuts:
        draws = jax.random.uniform(jax.random.fold_in(jax.random.fold_in(stream_key, 6), position), (parts,), jnp.float32, low / len(cuts), top_value / len(cuts))
        factor_of = factor_of * jnp.repeat(jnp.exp(draws), dims[position] // parts).reshape((-1,) + (1,) * (len(dims) - 1 - position))
    return factor_of


def shared_out(own_key, own, number, rows, number_of, top, most, skew):
    ranking = jax.random.permutation(own_key, number_of)
    heavy_load, common = portions_of(number_of, rows * top, most, skew, True), portions_of(number_of, rows * top, most, skew, False)
    places = jnp.arange(number_of)

    def named(sizes, turn):
        used = int((sizes > 0).sum())
        fixed = max(1, used // 4)
        shifted = fixed + (places - fixed + turn * (used - fixed)) % max(1, number_of - fixed)
        return jnp.zeros((number_of,), jnp.int32).at[ranking[jnp.where(places < fixed, places, shifted)]].set(jnp.asarray(sizes, jnp.int32))

    sizes = jnp.where(number % 4 == 0, named(heavy_load, number // 4), named(common, number - number // 4 - 1))
    mixed = jax.random.permutation(jax.random.fold_in(own, 3), number_of)
    giver, receiver = mixed[0:number_of // 2 * 2:2], mixed[1:number_of // 2 * 2:2]
    room = jnp.minimum(sizes[giver] - 1, most - sizes[receiver]) // 2
    room = jnp.where((giver == ranking[0]) | (receiver == ranking[0]) | (sizes[receiver] == 0), 0, jnp.maximum(room, 0))
    shifted = jax.random.randint(jax.random.fold_in(own, 4), (number_of // 2,), 0, 1 << 20) % (room + 1)
    sizes = sizes.at[giver].add(-shifted).at[receiver].add(shifted)
    members = jnp.searchsorted(jnp.cumsum(sizes), jnp.arange(rows * top), side="right").astype(jnp.int32)
    table = members.reshape(top, rows).T
    table = table[jax.random.permutation(jax.random.fold_in(own, 1), rows)]
    turn = jax.random.randint(jax.random.fold_in(own, 2), (rows, 1), 0, top)
    return jnp.take_along_axis(table, (jnp.arange(top)[None, :] + turn) % top, axis=1)


def portions_of(amount, total, reach, slope, full):
    loads = [(1 << 20) // math.isqrt(standing ** slope) + 1 for standing in range(1, amount + 1)]
    largest = reach if full else min(reach, max(-(-total // amount), total * loads[0] // sum(loads)))
    least = 1 if total - largest >= amount - 1 else 0
    holding, surplus = [largest] + [least] * (amount - 1), total - largest - least * (amount - 1)
    while surplus > 0:
        movable = [i for i in range(1, amount) if holding[i] < largest] or [i for i in range(1, amount) if holding[i] < reach]
        pool, remaining = sum([loads[i] for i in movable]), surplus
        for i in movable:
            addition = min(reach - holding[i], max(1, remaining * loads[i] // pool), surplus)
            holding[i] = holding[i] + addition
            surplus = surplus - addition
    return np.array(holding)


def normal_values(stream_key, shape, scale, most, shards=(), kind=jnp.bfloat16):
    factor_of = block_scale(stream_key, shape, shards, -0.22, 0.18) if shards else 1.0
    values = jax.random.normal(stream_key, shape, jnp.float32) * scale * factor_of
    return jnp.minimum(jnp.maximum(values, -most), most).astype(kind)


def setup_inputs(seed: int = 0, part: int = 0) -> dict:
    arg_keys = jax.random.split(jax.random.key(seed), 16)
    own_keys = jax.random.split(jax.random.fold_in(arg_keys[15], part), 16)
    ssm_input = normal_values(own_keys[0], (TOKENS, DIN), 1.0, 6.0, ((0, 16),))
    gate_input = normal_values(own_keys[1], (TOKENS, DIN), 1.0, 6.0, ((0, 16),))
    b_proj = normal_values(own_keys[2], (TOKENS, N), 0.1, 0.59765625, ((0, 16),))
    c_proj = normal_values(own_keys[3], (TOKENS, N), 0.1, 0.59765625, ((0, 16),))
    dt_raw = normal_values(own_keys[4], (TOKENS, H), 0.7, 4.0, ((0, 16),), jnp.float32)
    a_log = jnp.clip(jax.random.uniform(arg_keys[5], (H,), jnp.float32, -5.3, -0.7), -5.3, -0.7)
    dt_bias = jnp.clip(jax.random.uniform(arg_keys[6], (H,), jnp.float32, -3.5, -1.5), -3.5, -1.5)
    d_skip = jnp.clip(jax.random.uniform(arg_keys[7], (H,), jnp.float32, 0.5, 1.5), 0.5, 1.5)
    norm_gain = jnp.clip(1.0 + 0.15 * jax.random.normal(arg_keys[8], (DIN,), jnp.float32), 0.25, 1.75)
    state_in = normal_values(own_keys[9], (CLIPS, H, P_SIZE, N), 1.0, 6.0, ((0, 16),), jnp.float32)
    out_proj = normal_values(arg_keys[10], (DIN, D), DIN ** -0.5, 0.125, ((1, 4),))
    expert_in = normal_values(arg_keys[11], (EXPERTS, D, 2 * FF_E), D ** -0.5, 0.125, ((0, 16),))
    expert_out = normal_values(arg_keys[12], (EXPERTS, FF_E, D), FF_E ** -0.5, 0.3125, ((0, 16),))
    route_ids_keys = jax.random.split(jax.random.fold_in(own_keys[13], 1), TOKENS // TOK_DEV)
    route_ids_turns = jax.random.permutation(jax.random.fold_in(own_keys[13], 3), TOKENS // TOK_DEV)
    route_ids = jax.vmap(lambda own, number: shared_out(jax.random.fold_in(own_keys[13], 2), own, number, TOK_DEV, EXPERTS, TOPK, CAP, 1))(route_ids_keys, route_ids_turns).reshape((TOKENS, TOPK))
    route_weights = jnp.clip(0.05 + 0.25 * jax.random.uniform(own_keys[14], (TOKENS, TOPK), jnp.float32) ** block_scale(own_keys[14], (TOKENS, TOPK), ((0, 16),), -0.2, 0.2), 0.05, 0.3)
    return {"ssm_input": ssm_input, "gate_input": gate_input, "b_proj": b_proj, "c_proj": c_proj, "dt_raw": dt_raw, "a_log": a_log, "dt_bias": dt_bias, "d_skip": d_skip, "norm_gain": norm_gain, "state_in": state_in, "out_proj": out_proj, "expert_in": expert_in, "expert_out": expert_out, "route_ids": route_ids, "route_weights": route_weights}


epsilon = 1e-05

def ssm_mixer(ssm_input, gate_input, b_proj, c_proj, dt_raw, a_log, dt_bias, d_skip, norm_gain, state_in):
    length = ssm_input.shape[0]
    head_count = dt_raw.shape[1]
    head_dim = ssm_input.shape[1] // head_count
    step_size = jax.nn.softplus(dt_raw + dt_bias[None, :])
    decay_log = jnp.cumsum(step_size * (-jnp.exp(a_log))[None, :], axis=0)
    decay_heads = decay_log.T
    causal = jnp.arange(length)[:, None] >= jnp.arange(length)[None, :]
    spread = decay_heads[:, :, None] - decay_heads[:, None, :]
    spread = jnp.where(causal[None], spread, 0.0)
    scores = jnp.dot(c_proj, b_proj.T, preferred_element_type=jnp.float32)
    mixing = jnp.where(causal[None], jnp.exp(spread), 0.0) * scores[None] * step_size.T[:, None, :]
    mixing = mixing.astype(jnp.bfloat16)
    values = ssm_input.reshape(length, head_count, head_dim)
    within = jnp.einsum('hts,shp->thp', mixing.astype(jnp.float32), values.astype(jnp.float32))
    carried = jnp.einsum('tn,hpn->thp', c_proj.astype(jnp.float32), state_in, precision=lax.Precision.HIGHEST)
    mixed_rows = within + jnp.exp(decay_log)[:, :, None] * carried + d_skip[None, :, None] * values.astype(jnp.float32)
    gated_rows = mixed_rows.reshape(length, -1) * jax.nn.silu(gate_input.astype(jnp.float32))
    normed = gated_rows * lax.rsqrt(lax.optimization_barrier(jnp.mean(gated_rows * gated_rows, axis=1, keepdims=True)) + epsilon) * norm_gain[None, :]
    normed = normed.astype(jnp.bfloat16)
    tail_weight = jnp.exp(decay_log[-1][None, :] - decay_log) * step_size
    scaled = (values.astype(jnp.float32) * tail_weight[:, :, None]).astype(jnp.bfloat16)
    state_next = jnp.exp(decay_log[-1])[:, None, None] * state_in + jnp.einsum('thp,tn->hpn', scaled.astype(jnp.float32), b_proj.astype(jnp.float32))
    return (normed, state_next)

def slot_positions(route_ids, experts):
    flat_ids = route_ids.reshape(-1)
    onehot = (flat_ids[:, None] == jnp.arange(experts, dtype=jnp.int32)[None, :]).astype(jnp.int32)
    earlier = jnp.cumsum(onehot, axis=0) - onehot
    return (flat_ids, lax.optimization_barrier(jnp.sum(earlier * onehot, axis=1)).astype(jnp.int32))

def expert_ffn(slot_rows, gate_up, down_proj):
    hidden_width = down_proj.shape[0]
    projected = jnp.dot(slot_rows, gate_up, preferred_element_type=jnp.float32)
    hidden = (jax.nn.silu(projected[:, :hidden_width]) * projected[:, hidden_width:]).astype(jnp.bfloat16)
    return jnp.dot(hidden, down_proj, preferred_element_type=jnp.float32).astype(jnp.bfloat16)

def reference(ssm_input, gate_input, b_proj, c_proj, dt_raw, a_log, dt_bias, d_skip, norm_gain, state_in, out_proj, expert_in, expert_out, route_ids, route_weights):

    def one_clip(clip_index):
        begin = (clip_index * TOK_DEV).astype(jnp.int32)
        pieces = [lax.dynamic_slice_in_dim(item, begin, TOK_DEV, 0) for item in (ssm_input, gate_input, b_proj, c_proj, dt_raw)]
        normed, state_next = ssm_mixer(pieces[0], pieces[1], pieces[2], pieces[3], pieces[4], a_log, dt_bias, d_skip, norm_gain, state_in[clip_index])
        return (jnp.dot(normed, out_proj, preferred_element_type=jnp.float32).astype(jnp.bfloat16), state_next)
    mixer_rows, state_out = lax.map(one_clip, jnp.arange(CLIPS, dtype=jnp.int32))
    mixer_rows = mixer_rows.reshape(TOKENS, D)
    clip_ids = route_ids.reshape(CLIPS, TOK_DEV, TOPK)
    flat_ids, positions = jax.vmap(lambda block_ids: slot_positions(block_ids, EXPERTS))(clip_ids)
    per_clip = TOK_DEV * TOPK
    owners = jnp.arange(CLIPS * per_clip, dtype=jnp.int32)
    columns = owners // per_clip * CAP + positions.reshape(-1)
    flat_all = flat_ids.reshape(-1)
    slot_table = jnp.full((EXPERTS, CLIPS * CAP), TOKENS, jnp.int32).at[flat_all, columns].set(owners // TOPK)
    slot_weights = jnp.zeros((EXPERTS, CLIPS * CAP), jnp.float32).at[flat_all, columns].set(route_weights.reshape(-1))
    padded = jnp.concatenate([mixer_rows, jnp.zeros((1, D), jnp.bfloat16)], axis=0)

    def add_expert(running, pieces):
        slot_rows, slot_gate, gate_up, down_proj = pieces
        result = expert_ffn(padded[slot_rows], gate_up, down_proj)
        return (running.at[slot_rows].add(slot_gate[:, None] * result.astype(jnp.float32), mode='drop'), None)
    expert_sum, _ = lax.scan(add_expert, jnp.zeros((TOKENS, D), jnp.float32), (slot_table, slot_weights, expert_in, expert_out))
    layer_out = (mixer_rows.astype(jnp.float32) + expert_sum).astype(jnp.bfloat16)
    return (layer_out, state_out)
```

```python
import jax
import jax.numpy as jnp
from jax import lax
from jax.sharding import PartitionSpec as P

epsilon = 1e-05


def ssm_mixer(
    ssm_input, gate_input, b_proj, c_proj, dt_raw, a_log, dt_bias, d_skip, norm_gain, state_in
):
    length = ssm_input.shape[0]
    head_count = dt_raw.shape[1]
    head_dim = ssm_input.shape[1] // head_count
    step_size = jax.nn.softplus(dt_raw + dt_bias[None, :])
    decay_log = jnp.cumsum(step_size * (-jnp.exp(a_log))[None, :], axis=0)
    decay_heads = decay_log.T
    causal = jnp.arange(length)[:, None] >= jnp.arange(length)[None, :]
    spread = decay_heads[:, :, None] - decay_heads[:, None, :]
    spread = jnp.where(causal[None], spread, 0.0)
    scores = jnp.dot(c_proj, b_proj.T, preferred_element_type=jnp.float32)
    mixing = jnp.where(causal[None], jnp.exp(spread), 0.0) * scores[None] * step_size.T[:, None, :]
    mixing = mixing.astype(jnp.bfloat16)
    values = ssm_input.reshape(length, head_count, head_dim)
    within = jnp.einsum("hts,shp->thp", mixing, values, preferred_element_type=jnp.float32)
    carried = jnp.einsum(
        "tn,hpn->thp", c_proj.astype(jnp.float32), state_in, precision=lax.Precision.HIGHEST
    )
    mixed_rows = (
        within
        + jnp.exp(decay_log)[:, :, None] * carried
        + d_skip[None, :, None] * values.astype(jnp.float32)
    )
    gated_rows = mixed_rows.reshape(length, -1) * jax.nn.silu(gate_input.astype(jnp.float32))
    normed = (
        gated_rows
        * lax.rsqrt(jnp.mean(gated_rows * gated_rows, axis=1, keepdims=True) + epsilon)
        * norm_gain[None, :]
    )
    normed = normed.astype(jnp.bfloat16)
    tail_weight = jnp.exp(decay_log[-1][None, :] - decay_log) * step_size
    scaled = (values.astype(jnp.float32) * tail_weight[:, :, None]).astype(jnp.bfloat16)
    state_next = jnp.exp(decay_log[-1])[:, None, None] * state_in + jnp.einsum(
        "thp,tn->hpn", scaled, b_proj, preferred_element_type=jnp.float32
    )
    return (normed, state_next)


def slot_positions(route_ids, experts):
    flat_ids = route_ids.reshape(-1)
    onehot = (flat_ids[:, None] == jnp.arange(experts, dtype=jnp.int32)[None, :]).astype(jnp.int32)
    earlier = jnp.cumsum(onehot, axis=0) - onehot
    return (flat_ids, jnp.sum(earlier * onehot, axis=1))


def body(
    ssm_input,
    gate_input,
    b_proj,
    c_proj,
    dt_raw,
    a_log,
    dt_bias,
    d_skip,
    norm_gain,
    state_in,
    out_proj,
    expert_in,
    expert_out,
    route_ids,
    route_weights,
):
    normed, state_next = ssm_mixer(
        ssm_input,
        gate_input,
        b_proj,
        c_proj,
        dt_raw,
        a_log,
        dt_bias,
        d_skip,
        norm_gain,
        state_in[0],
    )
    frames_here, topk_count = route_ids.shape
    local_experts = expert_in.shape[0]
    experts = local_experts * lax.axis_size(("wide", "narrow"))
    if experts <= 4 * topk_count:
        layer_out = dense_experts(normed, out_proj, expert_in, expert_out, route_ids, route_weights)
    else:
        layer_out = routed_experts(normed, out_proj, expert_in, expert_out, route_ids, route_weights)
    return (layer_out, state_next[None])


def dense_experts(normed, out_proj, expert_in, expert_out, route_ids, route_weights):
    frames_here, topk_count = route_ids.shape
    local_experts = expert_in.shape[0]
    model_width = expert_in.shape[1]
    wide, narrow = lax.axis_size("wide"), lax.axis_size("narrow")
    devices = wide * narrow
    me = lax.axis_index(("wide", "narrow"))
    row_norms = lax.all_gather(normed, "narrow", axis=0, tiled=True)
    columns = jnp.dot(row_norms, out_proj, preferred_element_type=jnp.float32).astype(jnp.bfloat16)
    width = columns.shape[1]
    all_rows = lax.all_gather(columns, ("wide", "narrow"), axis=0, tiled=False)
    all_rows = all_rows.reshape(wide, narrow, narrow * frames_here, width)
    ids_all = lax.all_gather(route_ids, ("wide", "narrow"), axis=0, tiled=True)
    weights_all = lax.all_gather(route_weights, ("wide", "narrow"), axis=0, tiled=True)
    total = None
    for local in range(local_experts):
        gate = jnp.sum(
            jnp.where(ids_all == me * local_experts + local, weights_all, 0.0), axis=1, keepdims=True
        )
        projected = None
        for block in range(narrow):
            part = jnp.dot(
                all_rows[:, block].reshape(devices * frames_here, width),
                expert_in[local, block * width : (block + 1) * width],
                preferred_element_type=jnp.float32,
            )
            projected = part if projected is None else projected + part
        hidden_width = expert_out.shape[1]
        hidden = (jax.nn.silu(projected[:, :hidden_width]) * projected[:, hidden_width:]).astype(
            jnp.bfloat16
        )
        result = gate * jnp.dot(hidden, expert_out[local], preferred_element_type=jnp.float32)
        total = result if total is None else total + result
    summed = lax.psum_scatter(
        total.astype(jnp.bfloat16), ("wide", "narrow"), scatter_dimension=0, tiled=True
    )
    mine = lax.dynamic_slice_in_dim(all_rows, lax.axis_index("wide"), 1, 0)[0]
    mine = lax.dynamic_slice_in_dim(mine, lax.axis_index("narrow") * frames_here, frames_here, 1)
    mine = mine.transpose(1, 0, 2).reshape(frames_here, model_width)
    return (mine.astype(jnp.float32) + summed.astype(jnp.float32)).astype(jnp.bfloat16)


def routed_experts(normed, out_proj, expert_in, expert_out, route_ids, route_weights):
    mixer_rows = jnp.dot(
        normed,
        lax.all_gather(out_proj, "narrow", axis=1, tiled=True),
        preferred_element_type=jnp.float32,
    ).astype(jnp.bfloat16)
    frames_here = mixer_rows.shape[0]
    model_width = mixer_rows.shape[1]
    topk_count = route_ids.shape[1]
    local_experts = expert_in.shape[0]
    devices = lax.axis_size(("wide", "narrow"))
    experts = local_experts * devices
    capacity = max(2, frames_here * topk_count * 5 // (4 * experts))
    flat_ids, positions = slot_positions(route_ids, experts)
    owners = jnp.arange(frames_here * topk_count, dtype=jnp.int32) // topk_count
    slot_table = (
        jnp.full((experts, capacity), frames_here, jnp.int32).at[flat_ids, positions].set(owners)
    )
    padded = jnp.concatenate([mixer_rows, jnp.zeros((1, model_width), jnp.bfloat16)], axis=0)
    outgoing = padded[slot_table]
    hidden_width = expert_out.shape[1]
    projected = jnp.einsum(
        "nlcd,ldf->nlcf",
        lax.all_to_all(
            outgoing.reshape(devices, local_experts, capacity, model_width),
            ("wide", "narrow"),
            split_axis=0,
            concat_axis=0,
            tiled=True,
        ),
        expert_in,
        preferred_element_type=jnp.float32,
    )
    hidden = (jax.nn.silu(projected[..., :hidden_width]) * projected[..., hidden_width:]).astype(
        jnp.bfloat16
    )
    returned = lax.all_to_all(
        jnp.einsum("nlcf,lfd->nlcd", hidden, expert_out, preferred_element_type=jnp.float32).astype(
            jnp.bfloat16
        ),
        ("wide", "narrow"),
        split_axis=0,
        concat_axis=0,
        tiled=True,
    )
    returned = returned.reshape(experts, capacity, model_width)
    picked = returned[flat_ids, positions].reshape(frames_here, topk_count, model_width)
    expert_sum = jnp.einsum("tk,tkd->td", route_weights, picked.astype(jnp.float32))
    layer_out = (mixer_rows.astype(jnp.float32) + expert_sum).astype(jnp.bfloat16)
    return layer_out


def solution(mesh):
    placed = (
        P(("groups", "wide", "narrow"), None),
        P(("groups", "wide", "narrow"), None),
        P(("groups", "wide", "narrow"), None),
        P(("groups", "wide", "narrow"), None),
        P(("groups", "wide", "narrow"), None),
        P(),
        P(),
        P(),
        P(),
        P(("groups", "wide", "narrow"), None, None, None),
        P(None, "narrow"),
        P(("wide", "narrow"), None, None),
        P(("wide", "narrow"), None, None),
        P(("groups", "wide", "narrow"), None),
        P(("groups", "wide", "narrow"), None),
    )
    return jax.shard_map(
        body,
        mesh=mesh,
        in_specs=placed,
        out_specs=(
            P(("groups", "wide", "narrow"), None),
            P(("groups", "wide", "narrow"), None, None, None),
        ),
        check_vma=False,
    )
```

```python
import jax
import jax.numpy as jnp
from jax import lax
from jax.sharding import PartitionSpec as P

epsilon = 1e-05


def ssm_mixer(
    ssm_input, gate_input, b_proj, c_proj, dt_raw, a_log, dt_bias, d_skip, norm_gain, state_in
):
    length = ssm_input.shape[0]
    head_count = dt_raw.shape[1]
    head_dim = ssm_input.shape[1] // head_count
    step_size = jax.nn.softplus(dt_raw + dt_bias[None, :])
    decay_log = jnp.cumsum(step_size * (-jnp.exp(a_log))[None, :], axis=0)
    decay_heads = decay_log.T
    causal = jnp.arange(length)[:, None] >= jnp.arange(length)[None, :]
    spread = decay_heads[:, :, None] - decay_heads[:, None, :]
    spread = jnp.where(causal[None], spread, 0.0)
    scores = jnp.dot(c_proj, b_proj.T, preferred_element_type=jnp.float32)
    mixing = jnp.where(causal[None], jnp.exp(spread), 0.0) * scores[None] * step_size.T[:, None, :]
    mixing = mixing.astype(jnp.bfloat16)
    values = ssm_input.reshape(length, head_count, head_dim)
    within = jnp.einsum("hts,shp->thp", mixing, values, preferred_element_type=jnp.float32)
    carried = jnp.einsum(
        "tn,hpn->thp", c_proj.astype(jnp.float32), state_in, precision=lax.Precision.HIGHEST
    )
    mixed_rows = (
        within
        + jnp.exp(decay_log)[:, :, None] * carried
        + d_skip[None, :, None] * values.astype(jnp.float32)
    )
    gated_rows = mixed_rows.reshape(length, -1) * jax.nn.silu(gate_input.astype(jnp.float32))
    normed = (
        gated_rows
        * lax.rsqrt(jnp.mean(gated_rows * gated_rows, axis=1, keepdims=True) + epsilon)
        * norm_gain[None, :]
    )
    normed = normed.astype(jnp.bfloat16)
    tail_weight = jnp.exp(decay_log[-1][None, :] - decay_log) * step_size
    scaled = (values.astype(jnp.float32) * tail_weight[:, :, None]).astype(jnp.bfloat16)
    state_next = jnp.exp(decay_log[-1])[:, None, None] * state_in + jnp.einsum(
        "thp,tn->hpn", scaled, b_proj, preferred_element_type=jnp.float32
    )
    return (normed, state_next)


def slot_positions(route_ids, experts):
    flat_ids = route_ids.reshape(-1)
    onehot = (flat_ids[:, None] == jnp.arange(experts, dtype=jnp.int32)[None, :]).astype(jnp.int32)
    earlier = jnp.cumsum(onehot, axis=0) - onehot
    return (flat_ids, jnp.sum(earlier * onehot, axis=1))


def body(
    ssm_input,
    gate_input,
    b_proj,
    c_proj,
    dt_raw,
    a_log,
    dt_bias,
    d_skip,
    norm_gain,
    state_in,
    out_proj,
    expert_in,
    expert_out,
    route_ids,
    route_weights,
):
    normed, state_next = ssm_mixer(
        ssm_input,
        gate_input,
        b_proj,
        c_proj,
        dt_raw,
        a_log,
        dt_bias,
        d_skip,
        norm_gain,
        state_in[0],
    )
    frames_here, topk_count = route_ids.shape
    local_experts = expert_in.shape[0]
    experts = local_experts * lax.axis_size(("wide", "narrow"))
    wide, narrow = lax.axis_size("wide"), lax.axis_size("narrow")
    if experts <= 4 * topk_count and narrow == 4 and wide & (wide - 1) == 0 and local_experts == 1:
        layer_out = dense_experts(
            normed, out_proj, expert_in[0], expert_out[0], route_ids, route_weights
        )
    else:
        layer_out = routed_experts(normed, out_proj, expert_in, expert_out, route_ids, route_weights)
    return (layer_out, state_next[None])


def routes(wide, move):
    pairs = []
    for z in range(wide):
        for x in range(2):
            for core in range(2):
                to = move(z, x, core)
                if to is not None:
                    pairs.append(((z * 2 + x) * 2 + core, (to[0] * 2 + to[1]) * 2 + to[2]))
    return pairs


def pick(index, table, arrays):
    used = sorted(set(table))
    out = arrays[used[0]]
    for name in used[1:]:
        here = [i for i, entry in enumerate(table) if entry == name]
        test = index == here[0]
        for i in here[1:]:
            test = test | (index == i)
        out = jnp.where(test, arrays[name], out)
    return out


def dense_experts(normed, out_proj, expert_in, expert_out, route_ids, route_weights):
    frames = route_ids.shape[0]
    wide = lax.axis_size("wide")
    z = lax.axis_index("wide")
    x, core = lax.axis_index("narrow") // 2, lax.axis_index("narrow") % 2
    axes = ("wide", "narrow")

    def send(value, move):
        return lax.ppermute(value, axes, routes(wide, move))

    def to_core(value):
        return send(value, lambda z, x, c: (z, x, 1 - c))

    def to_x(value):
        return send(value, lambda z, x, c: (z, 1 - x, c))

    out_other, in_other, down_other = to_core(out_proj), to_core(expert_in), to_core(expert_out)

    experts = wide * 4
    gates = jnp.sum(
        jnp.where(route_ids[:, :, None] == jnp.arange(experts), route_weights[:, :, None], 0.0), axis=1
    )
    other = to_x(gates)
    gates = jnp.stack([jnp.where(x == 0, gates, other), jnp.where(x == 0, other, gates)])[None]
    step = 1
    while step < wide:
        gates = jnp.concatenate([gates, send(gates, lambda z, x, c: (z ^ step, x, c))], axis=0)
        step *= 2
    mine = (z * 2 + x) * 2 + core
    pair = jnp.stack([mine, mine + 1 - 2 * core])
    gates = jnp.sum(
        jnp.where(pair[:, None] == jnp.arange(experts), gates[..., None, :], 0.0), axis=-1
    ).reshape(wide, 2 * frames, 2)

    def project(rows):
        first = jnp.dot(rows, out_proj, preferred_element_type=jnp.float32).astype(jnp.bfloat16)
        second = jnp.dot(rows, out_other, preferred_element_type=jnp.float32).astype(jnp.bfloat16)
        return jnp.where(
            core == 0,
            jnp.concatenate([first, second], axis=1),
            jnp.concatenate([second, first], axis=1),
        )

    own = project(normed)
    peer = project(to_x(normed))
    block = jnp.where(x == 0, jnp.concatenate([own, peer]), jnp.concatenate([peer, own]))

    order = [sorted((o for o in range(wide) if o != p), key=lambda o: (abs(o - p), o)) for p in range(wide)]
    came = {}
    up = down = block
    for k in range(1, wide):
        up = send(up, lambda z, x, c: (z + 1, x, c) if z + 1 < wide and z + 1 >= k else None)
        down = send(down, lambda z, x, c: (z - 1, x, c) if z >= 1 and z - 1 + k < wide else None)
        came[-k], came[k] = up, down
    slots = [block]
    for s in range(wide - 1):
        slots.append(pick(z, [order[p][s] - p for p in range(wide)], came))
    across = [to_x(slot) for slot in slots]

    half = block.shape[1]
    hidden_width = expert_out.shape[0]
    partial = []
    for s in range(wide):
        rows = jnp.where(
            x == 0,
            jnp.concatenate([slots[s], across[s]], axis=1),
            jnp.concatenate([across[s], slots[s]], axis=1),
        )
        if s == 0:
            mixer_rows = lax.dynamic_slice_in_dim(rows, x * frames, frames, 0)
            gate = gates[0]
        else:
            where_from = jnp.asarray([p ^ order[p][s - 1] for p in range(wide)])[z]
            gate = lax.dynamic_index_in_dim(gates, where_from, 0, keepdims=False)
        total = None
        for e, (w_in, w_down) in enumerate(((expert_in, expert_out), (in_other, down_other))):
            v = jnp.dot(rows, w_in, preferred_element_type=jnp.float32)
            hidden = jax.nn.silu(v[:, :hidden_width]) * v[:, hidden_width:] * gate[:, e : e + 1]
            part = jnp.dot(hidden.astype(jnp.bfloat16), w_down, preferred_element_type=jnp.float32)
            total = part if total is None else total + part
        partial.append(total)

    sums = [None] * wide
    for s in reversed(range(wide)):
        away = lax.dynamic_slice_in_dim(partial[s], (1 - x) * frames, frames, 0)
        kept = lax.dynamic_slice_in_dim(partial[s], x * frames, frames, 0)
        sums[s] = kept + to_x(away.astype(jnp.bfloat16)).astype(jnp.float32)
    got_down = got_up = None
    for k in range(wide - 1, 0, -1):
        for side in (-1, 1):
            table = [1 + order[p].index(p + side * k) if 0 <= p + side * k < wide else None for p in range(wide)]
            some = next(t for t in table if t is not None)
            load = pick(z, [some if t is None else t for t in table], sums)
            got = got_down if side < 0 else got_up
            if got is not None:
                load = load + got.astype(jnp.float32)
            load = load.astype(jnp.bfloat16)
            if side < 0:
                got_down = send(load, lambda z, x, c: (z - 1, x, c) if z >= k else None)
            else:
                got_up = send(load, lambda z, x, c: (z + 1, x, c) if z + k < wide else None)
    total = sums[0]
    if wide > 1:
        total = total + got_down.astype(jnp.float32) + got_up.astype(jnp.float32)
    return (mixer_rows.astype(jnp.float32) + total).astype(jnp.bfloat16)


def routed_experts(normed, out_proj, expert_in, expert_out, route_ids, route_weights):
    mixer_rows = jnp.dot(
        normed,
        lax.all_gather(out_proj, "narrow", axis=1, tiled=True),
        preferred_element_type=jnp.float32,
    ).astype(jnp.bfloat16)
    frames_here = mixer_rows.shape[0]
    model_width = mixer_rows.shape[1]
    topk_count = route_ids.shape[1]
    local_experts = expert_in.shape[0]
    devices = lax.axis_size(("wide", "narrow"))
    experts = local_experts * devices
    capacity = max(2, frames_here * topk_count * 5 // (4 * experts))
    flat_ids, positions = slot_positions(route_ids, experts)
    owners = jnp.arange(frames_here * topk_count, dtype=jnp.int32) // topk_count
    slot_table = (
        jnp.full((experts, capacity), frames_here, jnp.int32).at[flat_ids, positions].set(owners)
    )
    padded = jnp.concatenate([mixer_rows, jnp.zeros((1, model_width), jnp.bfloat16)], axis=0)
    outgoing = padded[slot_table]
    hidden_width = expert_out.shape[1]
    projected = jnp.einsum(
        "nlcd,ldf->nlcf",
        lax.all_to_all(
            outgoing.reshape(devices, local_experts, capacity, model_width),
            ("wide", "narrow"),
            split_axis=0,
            concat_axis=0,
            tiled=True,
        ),
        expert_in,
        preferred_element_type=jnp.float32,
    )
    hidden = (jax.nn.silu(projected[..., :hidden_width]) * projected[..., hidden_width:]).astype(
        jnp.bfloat16
    )
    returned = lax.all_to_all(
        jnp.einsum("nlcf,lfd->nlcd", hidden, expert_out, preferred_element_type=jnp.float32).astype(
            jnp.bfloat16
        ),
        ("wide", "narrow"),
        split_axis=0,
        concat_axis=0,
        tiled=True,
    )
    returned = returned.reshape(experts, capacity, model_width)
    picked = returned[flat_ids, positions].reshape(frames_here, topk_count, model_width)
    expert_sum = jnp.einsum("tk,tkd->td", route_weights, picked.astype(jnp.float32))
    layer_out = (mixer_rows.astype(jnp.float32) + expert_sum).astype(jnp.bfloat16)
    return layer_out


def solution(mesh):
    placed = (
        P(("groups", "wide", "narrow"), None),
        P(("groups", "wide", "narrow"), None),
        P(("groups", "wide", "narrow"), None),
        P(("groups", "wide", "narrow"), None),
        P(("groups", "wide", "narrow"), None),
        P(),
        P(),
        P(),
        P(),
        P(("groups", "wide", "narrow"), None, None, None),
        P(None, "narrow"),
        P(("wide", "narrow"), None, None),
        P(("wide", "narrow"), None, None),
        P(("groups", "wide", "narrow"), None),
        P(("groups", "wide", "narrow"), None),
    )
    return jax.shard_map(
        body,
        mesh=mesh,
        in_specs=placed,
        out_specs=(
            P(("groups", "wide", "narrow"), None),
            P(("groups", "wide", "narrow"), None, None, None),
        ),
        check_vma=False,
    )
```

```python
import jax
import jax.numpy as jnp
from jax import lax
from jax.sharding import PartitionSpec as P

epsilon = 1e-05


def ssm_mixer(
    ssm_input, gate_input, b_proj, c_proj, dt_raw, a_log, dt_bias, d_skip, norm_gain, state_in
):
    length = ssm_input.shape[0]
    head_count = dt_raw.shape[1]
    head_dim = ssm_input.shape[1] // head_count
    step_size = jax.nn.softplus(dt_raw + dt_bias[None, :])
    decay_log = jnp.cumsum(step_size * (-jnp.exp(a_log))[None, :], axis=0)
    decay_heads = decay_log.T
    causal = jnp.arange(length)[:, None] >= jnp.arange(length)[None, :]
    spread = decay_heads[:, :, None] - decay_heads[:, None, :]
    spread = jnp.where(causal[None], spread, 0.0)
    scores = jnp.dot(c_proj, b_proj.T, preferred_element_type=jnp.float32)
    mixing = jnp.where(causal[None], jnp.exp(spread), 0.0) * scores[None] * step_size.T[:, None, :]
    mixing = mixing.astype(jnp.bfloat16)
    values = ssm_input.reshape(length, head_count, head_dim)
    within = jnp.einsum("hts,shp->thp", mixing, values, preferred_element_type=jnp.float32)
    carried = jnp.einsum(
        "tn,hpn->thp", c_proj.astype(jnp.float32), state_in, precision=lax.Precision.HIGHEST
    )
    mixed_rows = (
        within
        + jnp.exp(decay_log)[:, :, None] * carried
        + d_skip[None, :, None] * values.astype(jnp.float32)
    )
    gated_rows = mixed_rows.reshape(length, -1) * jax.nn.silu(gate_input.astype(jnp.float32))
    normed = (
        gated_rows
        * lax.rsqrt(jnp.mean(gated_rows * gated_rows, axis=1, keepdims=True) + epsilon)
        * norm_gain[None, :]
    )
    normed = normed.astype(jnp.bfloat16)
    tail_weight = jnp.exp(decay_log[-1][None, :] - decay_log) * step_size
    scaled = (values.astype(jnp.float32) * tail_weight[:, :, None]).astype(jnp.bfloat16)
    state_next = jnp.exp(decay_log[-1])[:, None, None] * state_in + jnp.einsum(
        "thp,tn->hpn", scaled, b_proj, preferred_element_type=jnp.float32
    )
    return (normed, state_next)


def slot_positions(route_ids, experts):
    flat_ids = route_ids.reshape(-1)
    onehot = (flat_ids[:, None] == jnp.arange(experts, dtype=jnp.int32)[None, :]).astype(jnp.int32)
    earlier = jnp.cumsum(onehot, axis=0) - onehot
    return (flat_ids, jnp.sum(earlier * onehot, axis=1))


def body(
    ssm_input,
    gate_input,
    b_proj,
    c_proj,
    dt_raw,
    a_log,
    dt_bias,
    d_skip,
    norm_gain,
    state_in,
    out_proj,
    expert_in,
    expert_out,
    route_ids,
    route_weights,
):
    normed, state_next = ssm_mixer(
        ssm_input,
        gate_input,
        b_proj,
        c_proj,
        dt_raw,
        a_log,
        dt_bias,
        d_skip,
        norm_gain,
        state_in[0],
    )
    frames_here, topk_count = route_ids.shape
    local_experts = expert_in.shape[0]
    experts = local_experts * lax.axis_size(("wide", "narrow"))
    wide, narrow = lax.axis_size("wide"), lax.axis_size("narrow")
    if experts <= 4 * topk_count and narrow == 4 and wide & (wide - 1) == 0 and local_experts == 1:
        layer_out = dense_experts(
            normed, out_proj, expert_in[0], expert_out[0], route_ids, route_weights
        )
    else:
        layer_out = routed_experts(normed, out_proj, expert_in, expert_out, route_ids, route_weights)
    return (layer_out, state_next[None])


def routes(wide, move):
    pairs = []
    for z in range(wide):
        for x in range(2):
            for core in range(2):
                to = move(z, x, core)
                pairs.append(((z * 2 + x) * 2 + core, (to[0] * 2 + to[1]) * 2 + to[2]))
    return pairs


def dense_experts(normed, out_proj, expert_in, expert_out, route_ids, route_weights):
    frames = route_ids.shape[0]
    wide = lax.axis_size("wide")
    ring = 2 * wide
    z = lax.axis_index("wide")
    x, core = lax.axis_index("narrow") // 2, lax.axis_index("narrow") % 2
    place = jnp.where(x == 0, z, ring - 1 - z)
    axes = ("wide", "narrow")

    def send(value, move):
        return lax.ppermute(value, axes, routes(wide, move))

    def to_core(value):
        return send(value, lambda z, x, c: (z, x, 1 - c))

    def to_x(value):
        return send(value, lambda z, x, c: (z, 1 - x, c))

    def along(value, step):
        def move(z, x, c):
            p = ((z if x == 0 else ring - 1 - z) + step) % ring
            return (p, 0, c) if p < wide else (ring - 1 - p, 1, c)

        return send(value, move)

    out_other, in_other, down_other = to_core(out_proj), to_core(expert_in), to_core(expert_out)

    experts = wide * 4
    gates = jnp.sum(
        jnp.where(route_ids[:, :, None] == jnp.arange(experts), route_weights[:, :, None], 0.0), axis=1
    )
    other = to_x(gates)
    gates = jnp.where(x == 0, jnp.stack([gates, other]), jnp.stack([other, gates]))[:, None]
    step = 1
    while step < wide:
        other = send(gates, lambda z, x, c: (z ^ step, x, c))
        low = z & step == 0
        gates = jnp.where(
            low, jnp.concatenate([gates, other], axis=1), jnp.concatenate([other, gates], axis=1)
        )
        step *= 2
    normed, gates = lax.optimization_barrier((normed, gates))
    mine = (z * 2 + x) * 2 + core
    pair = jnp.stack([mine, mine + 1 - 2 * core])
    gates = jnp.sum(
        jnp.where(pair[:, None] == jnp.arange(experts), gates[..., None, :], 0.0), axis=-1
    )
    gates = jnp.concatenate([gates[0], gates[1, ::-1]])
    gates = lax.dynamic_slice_in_dim(jnp.concatenate([gates, gates]), place, ring, 0)

    def project(rows):
        first = jnp.dot(rows, out_proj, preferred_element_type=jnp.float32).astype(jnp.bfloat16)
        second = jnp.dot(rows, out_other, preferred_element_type=jnp.float32).astype(jnp.bfloat16)
        return jnp.where(
            core == 0,
            jnp.concatenate([first, second], axis=1),
            jnp.concatenate([second, first], axis=1),
        )

    halves = range(2)
    size = frames // 2
    sent = [to_x(normed[h * size : (h + 1) * size]) for h in halves]
    own = project(normed)
    rows = []
    for h in halves:
        back = to_x(project(sent[h]))
        here = own[h * size : (h + 1) * size]
        rows.append(
            jnp.where(
                x == 0,
                jnp.concatenate([here, back], axis=1),
                jnp.concatenate([back, here], axis=1),
            )
        )

    *rows, in_other, down_other = lax.optimization_barrier((*rows, in_other, down_other))
    hidden_width = expert_out.shape[0]

    def run_experts(rows, gate):
        total = None
        for e, (w_in, w_down) in enumerate(((expert_in, expert_out), (in_other, down_other))):
            v = jnp.dot(rows, w_in, preferred_element_type=jnp.float32)
            hidden = jax.nn.silu(v[:, :hidden_width]) * v[:, hidden_width:] * gate[:, e : e + 1]
            part = jnp.dot(hidden.astype(jnp.bfloat16), w_down, preferred_element_type=jnp.float32)
            total = part if total is None else total + part
        return total

    fore, back = list(rows), list(rows)
    total = run_experts(jnp.concatenate(rows), gates[0])
    mixer_rows = rows
    ahead, behind = {}, {}
    for h in halves:
        ahead[0, h] = total[h * size : (h + 1) * size]
    far = ring // 2
    for k in range(1, far):
        for h in halves:
            fore[h] = along(fore[h], 1)
            back[h] = along(back[h], -1)
        total = run_experts(
            jnp.concatenate([back[0], back[1], fore[0], fore[1]]),
            jnp.concatenate([gates[k], gates[ring - k]]),
        )
        for h in halves:
            ahead[k, h] = total[h * size : (h + 1) * size]
            behind[k, h] = total[frames + h * size : frames + (h + 1) * size]
    last = [along(fore[0], 1), along(back[1], -1)]
    total = run_experts(jnp.concatenate(last), gates[far])

    fore = [along(total[:size].astype(jnp.bfloat16), 1), None]
    back = [None, along(total[size:].astype(jnp.bfloat16), -1)]
    for k in range(far - 1, 0, -1):
        for h in halves:
            load = ahead[k, h]
            if fore[h] is not None:
                load = load + fore[h].astype(jnp.float32)
            fore[h] = along(load.astype(jnp.bfloat16), 1)
            load = behind[k, h]
            if back[h] is not None:
                load = load + back[h].astype(jnp.float32)
            back[h] = along(load.astype(jnp.bfloat16), -1)
    out = []
    for h in halves:
        total = ahead[0, h] + fore[h].astype(jnp.float32) + back[h].astype(jnp.float32)
        out.append((mixer_rows[h].astype(jnp.float32) + total).astype(jnp.bfloat16))
    return jnp.concatenate(out)


def routed_experts(normed, out_proj, expert_in, expert_out, route_ids, route_weights):
    mixer_rows = jnp.dot(
        normed,
        lax.all_gather(out_proj, "narrow", axis=1, tiled=True),
        preferred_element_type=jnp.float32,
    ).astype(jnp.bfloat16)
    frames_here = mixer_rows.shape[0]
    model_width = mixer_rows.shape[1]
    topk_count = route_ids.shape[1]
    local_experts = expert_in.shape[0]
    devices = lax.axis_size(("wide", "narrow"))
    experts = local_experts * devices
    capacity = max(2, frames_here * topk_count * 5 // (4 * experts))
    flat_ids, positions = slot_positions(route_ids, experts)
    owners = jnp.arange(frames_here * topk_count, dtype=jnp.int32) // topk_count
    slot_table = (
        jnp.full((experts, capacity), frames_here, jnp.int32).at[flat_ids, positions].set(owners)
    )
    padded = jnp.concatenate([mixer_rows, jnp.zeros((1, model_width), jnp.bfloat16)], axis=0)
    outgoing = padded[slot_table]
    hidden_width = expert_out.shape[1]
    projected = jnp.einsum(
        "nlcd,ldf->nlcf",
        lax.all_to_all(
            outgoing.reshape(devices, local_experts, capacity, model_width),
            ("wide", "narrow"),
            split_axis=0,
            concat_axis=0,
            tiled=True,
        ),
        expert_in,
        preferred_element_type=jnp.float32,
    )
    hidden = (jax.nn.silu(projected[..., :hidden_width]) * projected[..., hidden_width:]).astype(
        jnp.bfloat16
    )
    returned = lax.all_to_all(
        jnp.einsum("nlcf,lfd->nlcd", hidden, expert_out, preferred_element_type=jnp.float32).astype(
            jnp.bfloat16
        ),
        ("wide", "narrow"),
        split_axis=0,
        concat_axis=0,
        tiled=True,
    )
    returned = returned.reshape(experts, capacity, model_width)
    picked = returned[flat_ids, positions].reshape(frames_here, topk_count, model_width)
    expert_sum = jnp.einsum("tk,tkd->td", route_weights, picked.astype(jnp.float32))
    layer_out = (mixer_rows.astype(jnp.float32) + expert_sum).astype(jnp.bfloat16)
    return layer_out


def solution(mesh):
    placed = (
        P(("groups", "wide", "narrow"), None),
        P(("groups", "wide", "narrow"), None),
        P(("groups", "wide", "narrow"), None),
        P(("groups", "wide", "narrow"), None),
        P(("groups", "wide", "narrow"), None),
        P(),
        P(),
        P(),
        P(),
        P(("groups", "wide", "narrow"), None, None, None),
        P(None, "narrow"),
        P(("wide", "narrow"), None, None),
        P(("wide", "narrow"), None, None),
        P(("groups", "wide", "narrow"), None),
        P(("groups", "wide", "narrow"), None),
    )
    return jax.shard_map(
        body,
        mesh=mesh,
        in_specs=placed,
        out_specs=(
            P(("groups", "wide", "narrow"), None),
            P(("groups", "wide", "narrow"), None, None, None),
        ),
        check_vma=False,
    )
```

```python
import functools

import jax
import jax.numpy as jnp
from jax import lax
from jax.experimental import pallas as pl
from jax.experimental.pallas import tpu as pltpu
from jax.sharding import PartitionSpec as P

epsilon = 1e-05


CHUNK = 8
NT = (((1,), (1,)), ((), ()))
TN = (((0,), (0,)), ((), ()))


def decays(dt_ref, bias_ref, a_ref):
    frames = dt_ref.shape[1]
    step_size = jax.nn.softplus(dt_ref[...] + bias_ref[...])
    rise = step_size * -jnp.exp(a_ref[...])
    s = lax.broadcasted_iota(jnp.int32, (frames, frames), 0)
    t = lax.broadcasted_iota(jnp.int32, (frames, frames), 1)
    upto = jnp.where(s <= t, 1.0, 0.0)
    decay = jnp.dot(rise, upto, precision=lax.Precision.HIGHEST, preferred_element_type=jnp.float32)
    return step_size, decay


def mixer_kernel(
    x_ref, z_ref, b_ref, c_ref, dt_ref, bias_ref, a_ref, skip_ref, gain_ref, state_ref, out_ref, g_ref, ss_ref
):
    i = pl.program_id(0)
    frames, width = x_ref.shape
    head = width // CHUNK
    step_size, decay = decays(dt_ref, bias_ref, a_ref)
    decay_col = decay.T
    carry_col = jnp.exp(decay_col)
    t = lax.broadcasted_iota(jnp.int32, (frames, frames), 0)
    s = lax.broadcasted_iota(jnp.int32, (frames, frames), 1)
    c = c_ref[...]
    scores = lax.dot_general(c, b_ref[...], NT, preferred_element_type=jnp.float32)
    scores = jnp.where(s <= t, scores, 0.0)
    cc = jnp.concatenate([c, c], axis=1)
    left = lax.broadcasted_iota(jnp.int32, (frames, 2 * head), 1) < head
    squares = None
    for pair in range(CHUNK // 2):
        mixes = []
        for h in (2 * pair, 2 * pair + 1):
            spread = jnp.exp(jnp.minimum(decay_col[:, h : h + 1] - decay[h : h + 1, :], 0.0))
            mixes.append((spread * (scores * step_size[h : h + 1, :])).astype(jnp.bfloat16))
        at = slice(2 * head * pair, 2 * head * (pair + 1))
        x = x_ref[:, at]
        zero = jnp.zeros_like(x)
        y = jnp.dot(
            jnp.concatenate(mixes, axis=1),
            jnp.concatenate([jnp.where(left, x, zero), jnp.where(left, zero, x)], axis=0),
            preferred_element_type=jnp.float32,
        )
        state = state_ref[at, :]
        high = state.astype(jnp.bfloat16)
        low = (state - high.astype(jnp.float32)).astype(jnp.bfloat16)
        carried = lax.dot_general(
            cc, jnp.concatenate([high, low], axis=1), NT, preferred_element_type=jnp.float32
        )
        factor = jnp.where(
            left, carry_col[:, 2 * pair : 2 * pair + 1], carry_col[:, 2 * pair + 1 : 2 * pair + 2]
        )
        mixed = y + factor * carried + skip_ref[:, at] * x.astype(jnp.float32)
        z = z_ref[:, at].astype(jnp.float32)
        g = mixed * jax.nn.silu(z)
        g_ref[i, :, at] = g
        squares = g * g if squares is None else squares + g * g

    @pl.when(i == 0)
    def _():
        ss_ref[...] = squares

    @pl.when(i > 0)
    def _():
        ss_ref[...] += squares

    steps = g_ref.shape[0]

    @pl.when(i == steps - 1)
    def _():
        mean = jnp.sum(ss_ref[...], axis=1, keepdims=True) / (steps * width)
        scale = lax.rsqrt(mean + epsilon)
        for j in range(steps):
            at = slice(j * width, (j + 1) * width)
            out_ref[:, at] = (g_ref[j] * scale * gain_ref[:, at]).astype(jnp.bfloat16)


def state_kernel(x_ref, b_ref, dt_ref, bias_ref, a_ref, state_ref, out_ref):
    frames, width = x_ref.shape
    head = width // CHUNK
    step_size, decay = decays(dt_ref, bias_ref, a_ref)
    end = decay[:, frames - 1 : frames]
    tail = (jnp.exp(end - decay) * step_size).T
    kept = jnp.exp(end)
    left = lax.broadcasted_iota(jnp.int32, (frames, 2 * head), 1) < head
    upper = lax.broadcasted_iota(jnp.int32, (2 * head, b_ref.shape[1]), 0) < head
    for pair in range(CHUNK // 2):
        at = slice(2 * head * pair, 2 * head * (pair + 1))
        factor = jnp.where(left, tail[:, 2 * pair : 2 * pair + 1], tail[:, 2 * pair + 1 : 2 * pair + 2])
        scaled = (x_ref[:, at].astype(jnp.float32) * factor).astype(jnp.bfloat16)
        added = lax.dot_general(scaled, b_ref[...], TN, preferred_element_type=jnp.float32)
        keep = jnp.where(upper, kept[2 * pair : 2 * pair + 1, :], kept[2 * pair + 1 : 2 * pair + 2, :])
        out_ref[at, :] = keep * state_ref[at, :] + added


def ssm_mixer(
    ssm_input, gate_input, b_proj, c_proj, dt_raw, a_log, dt_bias, d_skip, norm_gain, state_in
):
    frames, width = ssm_input.shape
    heads, head, inner = state_in.shape
    steps = heads // CHUNK
    part = width // steps
    dt = dt_raw.T
    state = state_in.reshape(width, inner)
    column = pl.BlockSpec((frames, part), lambda i: (0, i))
    whole = pl.BlockSpec((frames, inner), lambda i: (0, 0))
    per_head = pl.BlockSpec((CHUNK, frames), lambda i: (i, 0))
    scalar = pl.BlockSpec((CHUNK, 1), lambda i: (i, 0))
    rows = pl.BlockSpec((part, inner), lambda i: (i, 0))
    full_row = pl.BlockSpec((1, width), lambda i: (0, 0))
    normed = pl.pallas_call(
        mixer_kernel,
        grid=(steps,),
        in_specs=[
            column,
            column,
            whole,
            whole,
            per_head,
            scalar,
            scalar,
            pl.BlockSpec((1, part), lambda i: (0, i)),
            full_row,
            rows,
        ],
        out_specs=pl.BlockSpec((frames, width), lambda i: (0, 0)),
        out_shape=jax.ShapeDtypeStruct((frames, width), jnp.bfloat16),
        scratch_shapes=[
            pltpu.VMEM((steps, frames, part), jnp.float32),
            pltpu.VMEM((frames, 2 * head), jnp.float32),
        ],
        compiler_params=pltpu.CompilerParams(vmem_limit_bytes=24 << 20),
        cost_estimate=pl.CostEstimate(flops=400_000_000, bytes_accessed=6_000_000, transcendentals=2_000_000),
        name="mixer",
    )(
        ssm_input,
        gate_input,
        b_proj,
        c_proj,
        dt,
        dt_bias[:, None],
        a_log[:, None],
        jnp.repeat(d_skip, head)[None, :],
        norm_gain[None, :],
        state,
    )

    def state_next(ssm_input):
        out = pl.pallas_call(
            state_kernel,
            grid=(steps,),
            in_specs=[column, whole, per_head, scalar, scalar, rows],
            out_specs=rows,
            out_shape=jax.ShapeDtypeStruct((width, inner), jnp.float32),
            compiler_params=pltpu.CompilerParams(vmem_limit_bytes=16 << 20),
            cost_estimate=pl.CostEstimate(flops=70_000_000, bytes_accessed=3_000_000, transcendentals=20_000),
            name="state",
        )(ssm_input, b_proj, dt, dt_bias[:, None], a_log[:, None], state)
        return out.reshape(heads, head, inner)

    return (normed, state_next)


def project_kernel(core_ref, rows_ref, mine_ref, other_ref, out_ref):
    i = pl.program_id(0)
    steps = pl.num_programs(0) // 2

    @pl.when(i < steps)
    def _():
        out_ref[...] = jnp.dot(
            rows_ref[...], mine_ref[...], preferred_element_type=jnp.float32
        ).astype(jnp.bfloat16)

    @pl.when(i >= steps)
    def _():
        out_ref[...] = jnp.dot(
            rows_ref[...], other_ref[...], preferred_element_type=jnp.float32
        ).astype(jnp.bfloat16)


def project(core, rows, mine, other):
    count, depth = rows.shape
    width = mine.shape[1]
    wide = min(width, 256)
    steps = width // wide
    return pl.pallas_call(
        project_kernel,
        grid_spec=pltpu.PrefetchScalarGridSpec(
            num_scalar_prefetch=1,
            grid=(2 * steps,),
            in_specs=[
                pl.BlockSpec((count, depth), lambda i, c: (0, 0)),
                pl.BlockSpec((depth, wide), lambda i, c: (0, jnp.minimum(i, steps - 1))),
                pl.BlockSpec((depth, wide), lambda i, c: (0, jnp.maximum(i - steps, 0))),
            ],
            out_specs=pl.BlockSpec(
                (count, wide),
                lambda i, c: (0, jnp.where(i < steps, c[0], 1 - c[0]) * steps + i % steps),
            ),
        ),
        out_shape=jax.ShapeDtypeStruct((count, 2 * width), jnp.bfloat16),
        compiler_params=pltpu.CompilerParams(vmem_limit_bytes=16 << 20),
        cost_estimate=pl.CostEstimate(
            flops=4 * count * depth * width, bytes_accessed=4 * depth * width, transcendentals=0
        ),
        name="project",
    )(core[None], rows, mine, other)


def experts_kernel(parts, gate_ref, *refs):
    row_refs, refs = refs[:parts], refs[parts:]
    weights, refs = (refs[0:3], refs[3:6]), refs[6:]
    outs, (rows, total) = refs[:-2], refs[-2:]
    i = pl.program_id(0)
    steps = pl.num_programs(0) // 2
    size = row_refs[0].shape[0]

    @pl.when(i == 0)
    def _():
        for p in range(parts):
            rows[p * size : (p + 1) * size, :] = row_refs[p][...]
        total[...] = jnp.zeros_like(total)

    def add(e):
        gate_in, up_in, down = weights[e]
        r = rows[...]
        gated = jnp.dot(r, gate_in[...], preferred_element_type=jnp.float32)
        up = jnp.dot(r, up_in[...], preferred_element_type=jnp.float32)
        hidden = (jax.nn.silu(gated) * up * gate_ref[:, e : e + 1]).astype(jnp.bfloat16)
        total[...] += jnp.dot(hidden, down[...], preferred_element_type=jnp.float32)

    pl.when(i < steps)(functools.partial(add, 0))
    pl.when(i >= steps)(functools.partial(add, 1))

    @pl.when(i == 2 * steps - 1)
    def _():
        for p in range(parts):
            outs[p][...] = total[p * size : (p + 1) * size, :].astype(outs[p].dtype)


def run_experts(parts, gate, mine, other, out_type):
    size, depth = parts[0].shape
    hidden, width = mine[1].shape
    count = len(parts) * size
    cut = 128 if hidden % 128 == 0 else hidden
    steps = hidden // cut
    first = lambda i: jnp.minimum(i, steps - 1)
    second = lambda i: jnp.maximum(i - steps, 0)
    in_specs = [pl.BlockSpec((count, 2), lambda i: (0, 0))]
    in_specs += [pl.BlockSpec((size, depth), lambda i: (0, 0)) for _ in parts]
    operands = [gate, *parts]
    for pick, (w_in, w_down) in ((first, mine), (second, other)):
        in_specs += [
            pl.BlockSpec((depth, cut), lambda i, pick=pick: (0, pick(i))),
            pl.BlockSpec((depth, cut), lambda i, pick=pick: (0, steps + pick(i))),
            pl.BlockSpec((cut, width), lambda i, pick=pick: (pick(i), 0)),
        ]
        operands += [w_in, w_in, w_down]
    return pl.pallas_call(
        functools.partial(experts_kernel, len(parts)),
        grid=(2 * steps,),
        in_specs=in_specs,
        out_specs=[pl.BlockSpec((size, width), lambda i: (0, 0)) for _ in parts],
        out_shape=[jax.ShapeDtypeStruct((size, width), out_type) for _ in parts],
        scratch_shapes=[
            pltpu.VMEM((count, depth), jnp.bfloat16),
            pltpu.VMEM((count, width), jnp.float32),
        ],
        compiler_params=pltpu.CompilerParams(vmem_limit_bytes=32 << 20),
        cost_estimate=pl.CostEstimate(
            flops=12 * count * depth * hidden, bytes_accessed=12 * depth * hidden, transcendentals=2 * count * hidden
        ),
        name="experts",
    )(*operands)


def add_kernel(total_ref, got_ref, out_ref):
    out_ref[...] = (total_ref[...] + got_ref[...].astype(jnp.float32)).astype(jnp.bfloat16)


def add_on(total, got):
    return pl.pallas_call(
        add_kernel,
        out_shape=jax.ShapeDtypeStruct(got.shape, jnp.bfloat16),
        cost_estimate=pl.CostEstimate(flops=got.size, bytes_accessed=8 * got.size, transcendentals=0),
        name="add_on",
    )(total, got)


def slot_positions(route_ids, experts):
    flat_ids = route_ids.reshape(-1)
    onehot = (flat_ids[:, None] == jnp.arange(experts, dtype=jnp.int32)[None, :]).astype(jnp.int32)
    earlier = jnp.cumsum(onehot, axis=0) - onehot
    return (flat_ids, jnp.sum(earlier * onehot, axis=1))


def body(
    ssm_input,
    gate_input,
    b_proj,
    c_proj,
    dt_raw,
    a_log,
    dt_bias,
    d_skip,
    norm_gain,
    state_in,
    out_proj,
    expert_in,
    expert_out,
    route_ids,
    route_weights,
):
    normed, state_next = ssm_mixer(
        ssm_input,
        gate_input,
        b_proj,
        c_proj,
        dt_raw,
        a_log,
        dt_bias,
        d_skip,
        norm_gain,
        state_in[0],
    )
    frames_here, topk_count = route_ids.shape
    local_experts = expert_in.shape[0]
    experts = local_experts * lax.axis_size(("wide", "narrow"))
    wide, narrow = lax.axis_size("wide"), lax.axis_size("narrow")
    if experts <= 4 * topk_count and narrow == 4 and wide & (wide - 1) == 0 and local_experts == 1:
        layer_out, ssm_input = dense_experts(
            normed, out_proj, expert_in[0], expert_out[0], route_ids, route_weights, ssm_input
        )
    else:
        layer_out = routed_experts(normed, out_proj, expert_in, expert_out, route_ids, route_weights)
    state = state_next(ssm_input)
    return (layer_out, state[None])


def routes(wide, move):
    pairs = []
    for z in range(wide):
        for x in range(2):
            for core in range(2):
                to = move(z, x, core)
                pairs.append(((z * 2 + x) * 2 + core, (to[0] * 2 + to[1]) * 2 + to[2]))
    return pairs


def dense_experts(normed, out_proj, expert_in, expert_out, route_ids, route_weights, held):
    frames = route_ids.shape[0]
    wide = lax.axis_size("wide")
    ring = 2 * wide
    z = lax.axis_index("wide")
    x, core = lax.axis_index("narrow") // 2, lax.axis_index("narrow") % 2
    place = jnp.where(x == 0, z, ring - 1 - z)
    axes = ("wide", "narrow")

    def send(value, move):
        return lax.ppermute(value, axes, routes(wide, move))

    def to_core(value):
        return send(value, lambda z, x, c: (z, x, 1 - c))

    def to_x(value):
        return send(value, lambda z, x, c: (z, 1 - x, c))

    def along(value, step):
        def move(z, x, c):
            p = ((z if x == 0 else ring - 1 - z) + step) % ring
            return (p, 0, c) if p < wide else (ring - 1 - p, 1, c)

        return send(value, move)

    out_other, in_other, down_other = to_core(out_proj), to_core(expert_in), to_core(expert_out)

    experts = wide * 4
    gates = jnp.sum(
        jnp.where(route_ids[:, :, None] == jnp.arange(experts), route_weights[:, :, None], 0.0), axis=1
    )
    other = to_x(gates)
    gates = jnp.where(x == 0, jnp.stack([gates, other]), jnp.stack([other, gates]))[:, None]
    step = 1
    while step < wide:
        other = send(gates, lambda z, x, c: (z ^ step, x, c))
        low = z & step == 0
        gates = jnp.where(
            low, jnp.concatenate([gates, other], axis=1), jnp.concatenate([other, gates], axis=1)
        )
        step *= 2
    mine = (z * 2 + x) * 2 + core
    pair = jnp.stack([mine, mine + 1 - 2 * core])
    gates = jnp.sum(
        jnp.where(pair[:, None] == jnp.arange(experts), gates[..., None, :], 0.0), axis=-1
    )
    gates = jnp.concatenate([gates[0], gates[1, ::-1]])
    gates = lax.dynamic_slice_in_dim(jnp.concatenate([gates, gates]), place, ring, 0)

    halves = range(2)
    size = frames // 2
    sent = [to_x(normed[h * size : (h + 1) * size]) for h in halves]
    own = project(core, normed, out_proj, out_other)
    rows = []
    for h in halves:
        back = to_x(project(core, sent[h], out_proj, out_other))
        here = own[h * size : (h + 1) * size]
        rows.append(
            jnp.where(
                x == 0,
                jnp.concatenate([here, back], axis=1),
                jnp.concatenate([back, here], axis=1),
            )
        )
    *rows, in_other, down_other, gates, held = lax.optimization_barrier(
        (*rows, in_other, down_other, gates, held)
    )
    first, second = (expert_in, expert_out), (in_other, down_other)

    fore, back = list(rows), list(rows)
    ahead, behind = {}, {}
    ahead[0, 0], ahead[0, 1] = run_experts(rows, gates[0], first, second, jnp.float32)
    far = ring // 2
    for k in range(1, far):
        for h in halves:
            fore[h] = along(fore[h], 1)
            back[h] = along(back[h], -1)
        ahead[k, 0], ahead[k, 1], behind[k, 0], behind[k, 1] = run_experts(
            [back[0], back[1], fore[0], fore[1]],
            jnp.concatenate([gates[k], gates[ring - k]]),
            first,
            second,
            jnp.float32,
        )
    last = [along(fore[0], 1), along(back[1], -1)]
    last = run_experts(last, gates[far], first, second, jnp.bfloat16)

    fore, back = [along(last[0], 1), None], [None, along(last[1], -1)]
    for k in range(far - 1, 0, -1):
        for h in halves:
            for way, step, totals in ((fore, 1, ahead), (back, -1, behind)):
                if way[h] is None:
                    load = totals[k, h].astype(jnp.bfloat16)
                else:
                    load = add_on(totals[k, h], way[h])
                way[h] = along(load, step)
    out = []
    for h in halves:
        total = ahead[0, h] + fore[h].astype(jnp.float32) + back[h].astype(jnp.float32)
        out.append((rows[h].astype(jnp.float32) + total).astype(jnp.bfloat16))
    return jnp.concatenate(out), held


def routed_experts(normed, out_proj, expert_in, expert_out, route_ids, route_weights):
    mixer_rows = jnp.dot(
        normed,
        lax.all_gather(out_proj, "narrow", axis=1, tiled=True),
        preferred_element_type=jnp.float32,
    ).astype(jnp.bfloat16)
    frames_here = mixer_rows.shape[0]
    model_width = mixer_rows.shape[1]
    topk_count = route_ids.shape[1]
    local_experts = expert_in.shape[0]
    devices = lax.axis_size(("wide", "narrow"))
    experts = local_experts * devices
    capacity = max(2, frames_here * topk_count * 5 // (4 * experts))
    flat_ids, positions = slot_positions(route_ids, experts)
    owners = jnp.arange(frames_here * topk_count, dtype=jnp.int32) // topk_count
    slot_table = (
        jnp.full((experts, capacity), frames_here, jnp.int32).at[flat_ids, positions].set(owners)
    )
    padded = jnp.concatenate([mixer_rows, jnp.zeros((1, model_width), jnp.bfloat16)], axis=0)
    outgoing = padded[slot_table]
    hidden_width = expert_out.shape[1]
    projected = jnp.einsum(
        "nlcd,ldf->nlcf",
        lax.all_to_all(
            outgoing.reshape(devices, local_experts, capacity, model_width),
            ("wide", "narrow"),
            split_axis=0,
            concat_axis=0,
            tiled=True,
        ),
        expert_in,
        preferred_element_type=jnp.float32,
    )
    hidden = (jax.nn.silu(projected[..., :hidden_width]) * projected[..., hidden_width:]).astype(
        jnp.bfloat16
    )
    returned = lax.all_to_all(
        jnp.einsum("nlcf,lfd->nlcd", hidden, expert_out, preferred_element_type=jnp.float32).astype(
            jnp.bfloat16
        ),
        ("wide", "narrow"),
        split_axis=0,
        concat_axis=0,
        tiled=True,
    )
    returned = returned.reshape(experts, capacity, model_width)
    picked = returned[flat_ids, positions].reshape(frames_here, topk_count, model_width)
    expert_sum = jnp.einsum("tk,tkd->td", route_weights, picked.astype(jnp.float32))
    layer_out = (mixer_rows.astype(jnp.float32) + expert_sum).astype(jnp.bfloat16)
    return layer_out


def solution(mesh):
    placed = (
        P(("groups", "wide", "narrow"), None),
        P(("groups", "wide", "narrow"), None),
        P(("groups", "wide", "narrow"), None),
        P(("groups", "wide", "narrow"), None),
        P(("groups", "wide", "narrow"), None),
        P(),
        P(),
        P(),
        P(),
        P(("groups", "wide", "narrow"), None, None, None),
        P(None, "narrow"),
        P(("wide", "narrow"), None, None),
        P(("wide", "narrow"), None, None),
        P(("groups", "wide", "narrow"), None),
        P(("groups", "wide", "narrow"), None),
    )
    return jax.shard_map(
        body,
        mesh=mesh,
        in_specs=placed,
        out_specs=(
            P(("groups", "wide", "narrow"), None),
            P(("groups", "wide", "narrow"), None, None, None),
        ),
        check_vma=False,
    )
```

```python
import functools

import jax
import jax.numpy as jnp
from jax import lax
from jax.experimental import pallas as pl
from jax.experimental.pallas import tpu as pltpu
from jax.sharding import PartitionSpec as P

epsilon = 1e-05


CHUNK = 8
NT = (((1,), (1,)), ((), ()))
TN = (((0,), (0,)), ((), ()))


def decays(dt_ref, bias_ref, a_ref, step_ref, decay_ref):
    frames, heads = dt_ref.shape
    step_size = jax.nn.softplus(dt_ref[...] + bias_ref[...])
    rise = step_size * -jnp.exp(a_ref[...])
    s = lax.broadcasted_iota(jnp.int32, (frames, frames), 0)
    t = lax.broadcasted_iota(jnp.int32, (frames, frames), 1)
    upto = jnp.where(s <= t, 1.0, 0.0)
    step_ref[...] = step_size.T
    decay_ref[...] = jnp.dot(
        rise.T, upto, precision=lax.Precision.HIGHEST, preferred_element_type=jnp.float32
    )


def mixer_kernel(
    skip_ref,
    x_ref,
    z_ref,
    b_ref,
    c_ref,
    dt_ref,
    bias_ref,
    a_ref,
    gain_ref,
    state_ref,
    out_ref,
    g_ref,
    ss_ref,
    step_ref,
    decay_ref,
):
    i = pl.program_id(0)
    frames, width = x_ref.shape
    head = width // CHUNK
    pl.when(i == 0)(lambda: decays(dt_ref, bias_ref, a_ref, step_ref, decay_ref))
    chunk = pl.ds(pl.multiple_of(i * CHUNK, CHUNK), CHUNK)
    step_size, decay = step_ref[chunk, :], decay_ref[chunk, :]
    decay_col = decay.T
    carry_col = jnp.exp(decay_col)
    t = lax.broadcasted_iota(jnp.int32, (frames, frames), 0)
    s = lax.broadcasted_iota(jnp.int32, (frames, frames), 1)
    c = c_ref[...]
    scores = lax.dot_general(c, b_ref[...], NT, preferred_element_type=jnp.float32)
    scores = jnp.where(s <= t, scores, 0.0)
    cc = jnp.concatenate([c, c], axis=1)
    left = lax.broadcasted_iota(jnp.int32, (frames, 2 * head), 1) < head
    squares = None
    for pair in range(CHUNK // 2):
        mixes = []
        for h in (2 * pair, 2 * pair + 1):
            spread = jnp.exp(jnp.minimum(decay_col[:, h : h + 1] - decay[h : h + 1, :], 0.0))
            mixes.append((spread * (scores * step_size[h : h + 1, :])).astype(jnp.bfloat16))
        at = slice(2 * head * pair, 2 * head * (pair + 1))
        x = x_ref[:, at]
        zero = jnp.zeros_like(x)
        y = jnp.dot(
            jnp.concatenate(mixes, axis=1),
            jnp.concatenate([jnp.where(left, x, zero), jnp.where(left, zero, x)], axis=0),
            preferred_element_type=jnp.float32,
        )
        state = state_ref[at, :]
        high = state.astype(jnp.bfloat16)
        low = (state - high.astype(jnp.float32)).astype(jnp.bfloat16)
        carried = lax.dot_general(
            cc, jnp.concatenate([high, low], axis=1), NT, preferred_element_type=jnp.float32
        )
        factor = jnp.where(
            left, carry_col[:, 2 * pair : 2 * pair + 1], carry_col[:, 2 * pair + 1 : 2 * pair + 2]
        )
        skip = jnp.where(left[:1], skip_ref[i * CHUNK + 2 * pair], skip_ref[i * CHUNK + 2 * pair + 1])
        mixed = y + factor * carried + skip * x.astype(jnp.float32)
        z = z_ref[:, at].astype(jnp.float32)
        g = mixed * jax.nn.silu(z)
        g_ref[i, :, at] = g
        squares = g * g if squares is None else squares + g * g

    @pl.when(i == 0)
    def _():
        ss_ref[...] = squares

    @pl.when(i > 0)
    def _():
        ss_ref[...] += squares

    steps = g_ref.shape[0]

    @pl.when(i == steps - 1)
    def _():
        mean = jnp.sum(ss_ref[...], axis=1, keepdims=True) / (steps * width)
        scale = lax.rsqrt(mean + epsilon)
        for j in range(steps):
            at = slice(j * width, (j + 1) * width)
            out_ref[:, at] = (g_ref[j] * scale * gain_ref[:, at]).astype(jnp.bfloat16)


def state_kernel(x_ref, b_ref, dt_ref, bias_ref, a_ref, state_ref, out_ref, step_ref, decay_ref):
    i = pl.program_id(0)
    frames, width = x_ref.shape
    head = width // CHUNK
    pl.when(i == 0)(lambda: decays(dt_ref, bias_ref, a_ref, step_ref, decay_ref))
    chunk = pl.ds(pl.multiple_of(i * CHUNK, CHUNK), CHUNK)
    step_size, decay = step_ref[chunk, :], decay_ref[chunk, :]
    end = decay[:, frames - 1 : frames]
    tail = (jnp.exp(end - decay) * step_size).T
    kept = jnp.exp(end)
    left = lax.broadcasted_iota(jnp.int32, (frames, 2 * head), 1) < head
    upper = lax.broadcasted_iota(jnp.int32, (2 * head, b_ref.shape[1]), 0) < head
    for pair in range(CHUNK // 2):
        at = slice(2 * head * pair, 2 * head * (pair + 1))
        factor = jnp.where(left, tail[:, 2 * pair : 2 * pair + 1], tail[:, 2 * pair + 1 : 2 * pair + 2])
        scaled = (x_ref[:, at].astype(jnp.float32) * factor).astype(jnp.bfloat16)
        added = lax.dot_general(scaled, b_ref[...], TN, preferred_element_type=jnp.float32)
        keep = jnp.where(upper, kept[2 * pair : 2 * pair + 1, :], kept[2 * pair + 1 : 2 * pair + 2, :])
        out_ref[at, :] = keep * state_ref[at, :] + added


def ssm_mixer(
    ssm_input, gate_input, b_proj, c_proj, dt_raw, a_log, dt_bias, d_skip, norm_gain, state_in
):
    frames, width = ssm_input.shape
    heads, head, inner = state_in.shape
    steps = heads // CHUNK
    part = width // steps
    state = state_in.reshape(width, inner)
    column = pl.BlockSpec((frames, part), lambda i: (0, i))
    whole = pl.BlockSpec((frames, inner), lambda i: (0, 0))
    per_head = pl.BlockSpec((frames, heads), lambda i: (0, 0))
    scalar = pl.BlockSpec((1, heads), lambda i: (0, 0))
    rows = pl.BlockSpec((part, inner), lambda i: (i, 0))
    full_row = pl.BlockSpec((1, width), lambda i: (0, 0))
    tables = [pltpu.VMEM((heads, frames), jnp.float32)] * 2
    normed = pl.pallas_call(
        mixer_kernel,
        grid=(steps,),
        in_specs=[
            pl.BlockSpec(memory_space=pltpu.SMEM),
            column,
            column,
            whole,
            whole,
            per_head,
            scalar,
            scalar,
            full_row,
            rows,
        ],
        out_specs=pl.BlockSpec((frames, width), lambda i: (0, 0)),
        out_shape=jax.ShapeDtypeStruct((frames, width), jnp.bfloat16),
        scratch_shapes=[
            pltpu.VMEM((steps, frames, part), jnp.float32),
            pltpu.VMEM((frames, 2 * head), jnp.float32),
            *tables,
        ],
        compiler_params=pltpu.CompilerParams(vmem_limit_bytes=56 << 20),
        cost_estimate=pl.CostEstimate(flops=400_000_000, bytes_accessed=6_000_000, transcendentals=2_000_000),
        name="mixer",
    )(
        d_skip,
        ssm_input,
        gate_input,
        b_proj,
        c_proj,
        dt_raw,
        dt_bias[None, :],
        a_log[None, :],
        norm_gain[None, :],
        state,
    )

    def state_next(ssm_input):
        out = pl.pallas_call(
            state_kernel,
            grid=(steps,),
            in_specs=[column, whole, per_head, scalar, scalar, rows],
            out_specs=rows,
            out_shape=jax.ShapeDtypeStruct((width, inner), jnp.float32),
            scratch_shapes=tables,
            compiler_params=pltpu.CompilerParams(vmem_limit_bytes=16 << 20),
            cost_estimate=pl.CostEstimate(flops=70_000_000, bytes_accessed=3_000_000, transcendentals=20_000),
            name="state",
        )(ssm_input, b_proj, dt_raw, dt_bias[None, :], a_log[None, :], state)
        return out.reshape(heads, head, inner)

    return (normed, state_next)


def slot_positions(route_ids, experts):
    flat_ids = route_ids.reshape(-1)
    onehot = (flat_ids[:, None] == jnp.arange(experts, dtype=jnp.int32)[None, :]).astype(jnp.int32)
    earlier = jnp.cumsum(onehot, axis=0) - onehot
    return (flat_ids, jnp.sum(earlier * onehot, axis=1))


def body(
    ssm_input,
    gate_input,
    b_proj,
    c_proj,
    dt_raw,
    a_log,
    dt_bias,
    d_skip,
    norm_gain,
    state_in,
    out_proj,
    expert_in,
    expert_out,
    route_ids,
    route_weights,
):
    normed, state_next = ssm_mixer(
        ssm_input,
        gate_input,
        b_proj,
        c_proj,
        dt_raw,
        a_log,
        dt_bias,
        d_skip,
        norm_gain,
        state_in[0],
    )
    frames_here, topk_count = route_ids.shape
    local_experts = expert_in.shape[0]
    experts = local_experts * lax.axis_size(("wide", "narrow"))
    wide, narrow = lax.axis_size("wide"), lax.axis_size("narrow")
    if experts <= 4 * topk_count and narrow == 4 and wide & (wide - 1) == 0 and local_experts == 1:
        layer_out, state = dense_experts(
            normed,
            out_proj,
            expert_in[0],
            expert_out[0],
            route_ids,
            route_weights,
            functools.partial(state_next, ssm_input),
        )
    else:
        layer_out = routed_experts(normed, out_proj, expert_in, expert_out, route_ids, route_weights)
        state = state_next(ssm_input)
    return (layer_out, state[None])


def routes(wide, move):
    pairs = []
    for z in range(wide):
        for x in range(2):
            for core in range(2):
                to = move(z, x, core)
                pairs.append(((z * 2 + x) * 2 + core, (to[0] * 2 + to[1]) * 2 + to[2]))
    return pairs


def dense_experts(normed, out_proj, expert_in, expert_out, route_ids, route_weights, state_next):
    frames = route_ids.shape[0]
    wide = lax.axis_size("wide")
    ring = 2 * wide
    z = lax.axis_index("wide")
    x, core = lax.axis_index("narrow") // 2, lax.axis_index("narrow") % 2
    place = jnp.where(x == 0, z, ring - 1 - z)
    axes = ("wide", "narrow")

    def send(value, move):
        return lax.ppermute(value, axes, routes(wide, move))

    def to_core(value):
        return send(value, lambda z, x, c: (z, x, 1 - c))

    def to_x(value):
        return send(value, lambda z, x, c: (z, 1 - x, c))

    def along(value, step):
        def move(z, x, c):
            p = ((z if x == 0 else ring - 1 - z) + step) % ring
            return (p, 0, c) if p < wide else (ring - 1 - p, 1, c)

        return send(value, move)

    out_other, in_other, down_other = to_core(out_proj), to_core(expert_in), to_core(expert_out)

    halves = range(2)
    size = frames // 2
    sent = [to_x(normed[h * size : (h + 1) * size]) for h in halves]

    columns = lax.optimization_barrier(
        jnp.where(
            core == 0,
            jnp.concatenate([out_proj, out_other], axis=1),
            jnp.concatenate([out_other, out_proj], axis=1),
        )
    )

    def project(rows):
        return jnp.dot(rows, columns, preferred_element_type=jnp.float32).astype(jnp.bfloat16)

    own = project(normed)
    rows, backs = [], []
    for h in halves:
        backs.append(to_x(project(sent[h])))
        here = own[h * size : (h + 1) * size]
        rows.append(
            jnp.where(
                x == 0,
                jnp.concatenate([here, backs[h]], axis=1),
                jnp.concatenate([backs[h], here], axis=1),
            )
        )

    experts = wide * 4
    gates = jnp.sum(
        jnp.where(route_ids[:, :, None] == jnp.arange(experts), route_weights[:, :, None], 0.0), axis=1
    )
    gates, _ = lax.optimization_barrier((gates, normed))
    other = to_x(gates)
    gates = jnp.where(x == 0, jnp.stack([gates, other]), jnp.stack([other, gates]))[:, None]
    step = 1
    while step < wide:
        gates, _ = lax.optimization_barrier((gates, sent[1] if step == 1 else rows[0]))
        other = send(gates, lambda z, x, c: (z ^ step, x, c))
        low = z & step == 0
        gates = jnp.where(
            low, jnp.concatenate([gates, other], axis=1), jnp.concatenate([other, gates], axis=1)
        )
        step *= 2
    mine = (z * 2 + x) * 2 + core
    pair = jnp.stack([mine, mine + 1 - 2 * core])
    gates = jnp.sum(
        jnp.where(pair[:, None] == jnp.arange(experts), gates[..., None, :], 0.0), axis=-1
    )
    gates = jnp.concatenate([gates[0], gates[1, ::-1]])
    gates = lax.dynamic_slice_in_dim(jnp.concatenate([gates, gates]), place, ring, 0)

    far = ring // 2
    fore, back = list(rows), list(rows)
    fore_at, back_at = {0: fore}, {0: back}
    for k in range(1, far):
        fore_at[k] = [along(fore_at[k - 1][h], 1) for h in halves]
        back_at[k] = [along(back_at[k - 1][h], -1) for h in halves]
    last = [along(fore_at[far - 1][0], 1), along(back_at[far - 1][1], -1)]

    hidden_width = expert_out.shape[0]
    early, in_other, down_other, expert_in, expert_out = lax.optimization_barrier(
        (rows[1], in_other, down_other, expert_in, expert_out)
    )
    joined_in = jnp.concatenate(
        [
            expert_in[:, :hidden_width],
            in_other[:, :hidden_width],
            expert_in[:, hidden_width:],
            in_other[:, hidden_width:],
        ],
        axis=1,
    )
    joined_down = jnp.concatenate([expert_out, down_other], axis=0)
    joined_in, joined_down = lax.optimization_barrier((joined_in, joined_down))
    is_first = jnp.arange(2 * hidden_width)[None, :] < hidden_width

    def run_experts(parts, gate):
        v = jnp.dot(jnp.concatenate(parts), joined_in, preferred_element_type=jnp.float32)
        hidden = jax.nn.silu(v[:, : 2 * hidden_width]) * v[:, 2 * hidden_width :]
        hidden = (hidden * jnp.where(is_first, gate[:, :1], gate[:, 1:])).astype(jnp.bfloat16)
        return jnp.dot(hidden, joined_down, preferred_element_type=jnp.float32)

    def cut(total, at):
        return [total[at + h * size : at + (h + 1) * size] for h in halves]

    ahead, behind = {}, {}
    ahead[0] = cut(run_experts([early if h == 1 else rows[h] for h in halves], gates[0]), 0)
    for k in range(1, far):
        total = run_experts(
            [*back_at[k], *fore_at[k]], jnp.concatenate([gates[k], gates[ring - k]])
        )
        ahead[k], behind[k] = cut(total, 0), cut(total, frames)
    state = state_next()
    last[0], last[1], state, *near = lax.optimization_barrier(
        (last[0], last[1], state, *ahead[far - 1], *behind[far - 1])
    )
    ahead[far - 1], behind[far - 1] = near[:2], near[2:]
    total = run_experts(last, gates[far]).astype(jnp.bfloat16)

    fore, back = [along(total[:size], 1), None], [None, along(total[size:], -1)]
    for k in range(far - 1, 0, -1):
        before = None
        for h in halves if k < far - 1 else (None,):
            todo = ((fore, 1, ahead, h), (back, -1, behind, h))
            if h is None:
                todo = (
                    (fore, 1, ahead, 1),
                    (back, -1, behind, 0),
                    (fore, 1, ahead, 0),
                    (back, -1, behind, 1),
                )
            loads = []
            for way, step, totals, at in todo:
                load = totals[k][at]
                if way[at] is not None:
                    got = way[at]
                    if before is not None:
                        got = lax.optimization_barrier((got, *before))[0]
                    load = load + got.astype(jnp.float32)
                loads.append(load.astype(jnp.bfloat16))
            before = loads
            for (way, step, totals, at), load in zip(todo, loads):
                way[at] = along(load, step)
    out = []
    for h in halves:
        total = ahead[0][h] + fore[h].astype(jnp.float32) + back[h].astype(jnp.float32)
        out.append((rows[h].astype(jnp.float32) + total).astype(jnp.bfloat16))
    return jnp.concatenate(out), state


def routed_experts(normed, out_proj, expert_in, expert_out, route_ids, route_weights):
    mixer_rows = jnp.dot(
        normed,
        lax.all_gather(out_proj, "narrow", axis=1, tiled=True),
        preferred_element_type=jnp.float32,
    ).astype(jnp.bfloat16)
    frames_here = mixer_rows.shape[0]
    model_width = mixer_rows.shape[1]
    topk_count = route_ids.shape[1]
    local_experts = expert_in.shape[0]
    devices = lax.axis_size(("wide", "narrow"))
    experts = local_experts * devices
    capacity = max(2, frames_here * topk_count * 5 // (4 * experts))
    flat_ids, positions = slot_positions(route_ids, experts)
    owners = jnp.arange(frames_here * topk_count, dtype=jnp.int32) // topk_count
    slot_table = (
        jnp.full((experts, capacity), frames_here, jnp.int32).at[flat_ids, positions].set(owners)
    )
    padded = jnp.concatenate([mixer_rows, jnp.zeros((1, model_width), jnp.bfloat16)], axis=0)
    outgoing = padded[slot_table]
    hidden_width = expert_out.shape[1]
    projected = jnp.einsum(
        "nlcd,ldf->nlcf",
        lax.all_to_all(
            outgoing.reshape(devices, local_experts, capacity, model_width),
            ("wide", "narrow"),
            split_axis=0,
            concat_axis=0,
            tiled=True,
        ),
        expert_in,
        preferred_element_type=jnp.float32,
    )
    hidden = (jax.nn.silu(projected[..., :hidden_width]) * projected[..., hidden_width:]).astype(
        jnp.bfloat16
    )
    returned = lax.all_to_all(
        jnp.einsum("nlcf,lfd->nlcd", hidden, expert_out, preferred_element_type=jnp.float32).astype(
            jnp.bfloat16
        ),
        ("wide", "narrow"),
        split_axis=0,
        concat_axis=0,
        tiled=True,
    )
    returned = returned.reshape(experts, capacity, model_width)
    picked = returned[flat_ids, positions].reshape(frames_here, topk_count, model_width)
    expert_sum = jnp.einsum("tk,tkd->td", route_weights, picked.astype(jnp.float32))
    layer_out = (mixer_rows.astype(jnp.float32) + expert_sum).astype(jnp.bfloat16)
    return layer_out


def solution(mesh):
    placed = (
        P(("groups", "wide", "narrow"), None),
        P(("groups", "wide", "narrow"), None),
        P(("groups", "wide", "narrow"), None),
        P(("groups", "wide", "narrow"), None),
        P(("groups", "wide", "narrow"), None),
        P(),
        P(),
        P(),
        P(),
        P(("groups", "wide", "narrow"), None, None, None),
        P(None, "narrow"),
        P(("wide", "narrow"), None, None),
        P(("wide", "narrow"), None, None),
        P(("groups", "wide", "narrow"), None),
        P(("groups", "wide", "narrow"), None),
    )
    return jax.shard_map(
        body,
        mesh=mesh,
        in_specs=placed,
        out_specs=(
            P(("groups", "wide", "narrow"), None),
            P(("groups", "wide", "narrow"), None, None, None),
        ),
        check_vma=False,
    )
```

```python
import functools

import jax
import jax.numpy as jnp
from jax import lax
from jax.experimental import pallas as pl
from jax.experimental.pallas import tpu as pltpu
from jax.sharding import PartitionSpec as P

epsilon = 1e-05


CHUNK = 8
NT = (((1,), (1,)), ((), ()))
TN = (((0,), (0,)), ((), ()))


def column_of(row_ref):
    count = row_ref.shape[1]
    i = lax.broadcasted_iota(jnp.int32, (count, count), 0)
    j = lax.broadcasted_iota(jnp.int32, (count, count), 1)
    return jnp.sum(jnp.where(i == j, row_ref[...], 0.0), axis=1, keepdims=True)


def decays(dt_ref, bias_ref, a_ref, step_ref, decay_ref):
    frames = dt_ref.shape[1]
    step_size = jax.nn.softplus(dt_ref[...] + column_of(bias_ref))
    rise = step_size * -jnp.exp(column_of(a_ref))
    s = lax.broadcasted_iota(jnp.int32, (frames, frames), 0)
    t = lax.broadcasted_iota(jnp.int32, (frames, frames), 1)
    upto = jnp.where(s <= t, 1.0, 0.0)
    step_ref[...] = step_size
    decay_ref[...] = jnp.dot(
        rise, upto, precision=lax.Precision.HIGHEST, preferred_element_type=jnp.float32
    )


def mixer_kernel(
    skip_ref,
    x_ref,
    z_ref,
    b_ref,
    c_ref,
    dt_ref,
    bias_ref,
    a_ref,
    gain_ref,
    state_ref,
    top_ref,
    bottom_ref,
    g_ref,
    ss_ref,
    step_ref,
    decay_ref,
):
    i = pl.program_id(0)
    frames, width = x_ref.shape
    head = width // CHUNK
    pl.when(i == 0)(lambda: decays(dt_ref, bias_ref, a_ref, step_ref, decay_ref))
    chunk = pl.ds(pl.multiple_of(i * CHUNK, CHUNK), CHUNK)
    step_size, decay = step_ref[chunk, :], decay_ref[chunk, :]
    decay_col = decay.T
    carry_col = jnp.exp(decay_col)
    t = lax.broadcasted_iota(jnp.int32, (frames, frames), 0)
    s = lax.broadcasted_iota(jnp.int32, (frames, frames), 1)
    c = c_ref[...]
    scores = lax.dot_general(c, b_ref[...], NT, preferred_element_type=jnp.float32)
    scores = jnp.where(s <= t, scores, 0.0)
    cc = jnp.concatenate([c, c], axis=1)
    left = lax.broadcasted_iota(jnp.int32, (frames, 2 * head), 1) < head
    squares = None
    for pair in range(CHUNK // 2):
        mixes = []
        for h in (2 * pair, 2 * pair + 1):
            spread = jnp.exp(jnp.minimum(decay_col[:, h : h + 1] - decay[h : h + 1, :], 0.0))
            mixes.append((spread * (scores * step_size[h : h + 1, :])).astype(jnp.bfloat16))
        at = slice(2 * head * pair, 2 * head * (pair + 1))
        x = x_ref[:, at]
        zero = jnp.zeros_like(x)
        y = jnp.dot(
            jnp.concatenate(mixes, axis=1),
            jnp.concatenate([jnp.where(left, x, zero), jnp.where(left, zero, x)], axis=0),
            preferred_element_type=jnp.float32,
        )
        state = state_ref[at, :]
        high = state.astype(jnp.bfloat16)
        low = (state - high.astype(jnp.float32)).astype(jnp.bfloat16)
        carried = lax.dot_general(
            cc, jnp.concatenate([high, low], axis=1), NT, preferred_element_type=jnp.float32
        )
        factor = jnp.where(
            left, carry_col[:, 2 * pair : 2 * pair + 1], carry_col[:, 2 * pair + 1 : 2 * pair + 2]
        )
        skip = jnp.where(left[:1], skip_ref[i * CHUNK + 2 * pair], skip_ref[i * CHUNK + 2 * pair + 1])
        mixed = y + factor * carried + skip * x.astype(jnp.float32)
        z = z_ref[:, at].astype(jnp.float32)
        g = mixed * jax.nn.silu(z)
        g_ref[i, :, at] = g
        squares = g * g if squares is None else squares + g * g

    @pl.when(i == 0)
    def _():
        ss_ref[...] = squares

    @pl.when(i > 0)
    def _():
        ss_ref[...] += squares

    steps = g_ref.shape[0]

    @pl.when(i == steps - 1)
    def _():
        mean = jnp.sum(ss_ref[...], axis=1, keepdims=True) / (steps * width)
        scale = lax.rsqrt(mean + epsilon)
        for j in range(steps):
            at = slice(j * width, (j + 1) * width)
            normed = (g_ref[j] * scale * gain_ref[:, at]).astype(jnp.bfloat16)
            top_ref[:, at] = normed[: frames // 2]
            bottom_ref[:, at] = normed[frames // 2 :]


def state_kernel(x_ref, b_ref, dt_ref, bias_ref, a_ref, state_ref, out_ref, step_ref, decay_ref):
    i = pl.program_id(0)
    frames, width = x_ref.shape
    head = width // CHUNK
    pl.when(i == 0)(lambda: decays(dt_ref, bias_ref, a_ref, step_ref, decay_ref))
    chunk = pl.ds(pl.multiple_of(i * CHUNK, CHUNK), CHUNK)
    step_size, decay = step_ref[chunk, :], decay_ref[chunk, :]
    end = decay[:, frames - 1 : frames]
    tail = (jnp.exp(end - decay) * step_size).T
    kept = jnp.exp(end)
    left = lax.broadcasted_iota(jnp.int32, (frames, 2 * head), 1) < head
    upper = lax.broadcasted_iota(jnp.int32, (2 * head, b_ref.shape[1]), 0) < head
    for pair in range(CHUNK // 2):
        at = slice(2 * head * pair, 2 * head * (pair + 1))
        factor = jnp.where(left, tail[:, 2 * pair : 2 * pair + 1], tail[:, 2 * pair + 1 : 2 * pair + 2])
        scaled = (x_ref[:, at].astype(jnp.float32) * factor).astype(jnp.bfloat16)
        added = lax.dot_general(scaled, b_ref[...], TN, preferred_element_type=jnp.float32)
        keep = jnp.where(upper, kept[2 * pair : 2 * pair + 1, :], kept[2 * pair + 1 : 2 * pair + 2, :])
        out_ref[at, :] = keep * state_ref[at, :] + added


def ssm_mixer(
    ssm_input, gate_input, b_proj, c_proj, dt_raw, a_log, dt_bias, d_skip, norm_gain, state_in
):
    frames, width = ssm_input.shape
    heads, head, inner = state_in.shape
    steps = heads // CHUNK
    part = width // steps
    state = state_in.reshape(width, inner)
    dt = dt_raw.T
    column = pl.BlockSpec((frames, part), lambda i: (0, i))
    whole = pl.BlockSpec((frames, inner), lambda i: (0, 0))
    per_head = pl.BlockSpec((heads, frames), lambda i: (0, 0))
    scalar = pl.BlockSpec((1, heads), lambda i: (0, 0))
    rows = pl.BlockSpec((part, inner), lambda i: (i, 0))
    full_row = pl.BlockSpec((1, width), lambda i: (0, 0))
    tables = [pltpu.VMEM((heads, frames), jnp.float32)] * 2
    normed = pl.pallas_call(
        mixer_kernel,
        grid=(steps,),
        in_specs=[
            pl.BlockSpec(memory_space=pltpu.SMEM),
            column,
            column,
            whole,
            whole,
            per_head,
            scalar,
            scalar,
            full_row,
            rows,
        ],
        out_specs=[pl.BlockSpec((frames // 2, width), lambda i: (0, 0))] * 2,
        out_shape=[jax.ShapeDtypeStruct((frames // 2, width), jnp.bfloat16)] * 2,
        scratch_shapes=[
            pltpu.VMEM((steps, frames, part), jnp.float32),
            pltpu.VMEM((frames, 2 * head), jnp.float32),
            *tables,
        ],
        compiler_params=pltpu.CompilerParams(vmem_limit_bytes=56 << 20),
        cost_estimate=pl.CostEstimate(flops=400_000_000, bytes_accessed=6_000_000, transcendentals=2_000_000),
        name="mixer",
    )(
        d_skip,
        ssm_input,
        gate_input,
        b_proj,
        c_proj,
        dt,
        dt_bias[None, :],
        a_log[None, :],
        norm_gain[None, :],
        state,
    )

    def state_next(ssm_input):
        out = pl.pallas_call(
            state_kernel,
            grid=(steps,),
            in_specs=[column, whole, per_head, scalar, scalar, rows],
            out_specs=rows,
            out_shape=jax.ShapeDtypeStruct((width, inner), jnp.float32),
            scratch_shapes=tables,
            compiler_params=pltpu.CompilerParams(vmem_limit_bytes=16 << 20),
            cost_estimate=pl.CostEstimate(flops=70_000_000, bytes_accessed=3_000_000, transcendentals=20_000),
            name="state",
        )(ssm_input, b_proj, dt, dt_bias[None, :], a_log[None, :], state)
        return out.reshape(heads, head, inner)

    return (normed, state_next)


def slot_positions(route_ids, experts):
    flat_ids = route_ids.reshape(-1)
    onehot = (flat_ids[:, None] == jnp.arange(experts, dtype=jnp.int32)[None, :]).astype(jnp.int32)
    earlier = jnp.cumsum(onehot, axis=0) - onehot
    return (flat_ids, jnp.sum(earlier * onehot, axis=1))


def body(
    ssm_input,
    gate_input,
    b_proj,
    c_proj,
    dt_raw,
    a_log,
    dt_bias,
    d_skip,
    norm_gain,
    state_in,
    out_proj,
    expert_in,
    expert_out,
    route_ids,
    route_weights,
):
    normed, state_next = ssm_mixer(
        ssm_input,
        gate_input,
        b_proj,
        c_proj,
        dt_raw,
        a_log,
        dt_bias,
        d_skip,
        norm_gain,
        state_in[0],
    )
    frames_here, topk_count = route_ids.shape
    local_experts = expert_in.shape[0]
    experts = local_experts * lax.axis_size(("wide", "narrow"))
    wide, narrow = lax.axis_size("wide"), lax.axis_size("narrow")
    if experts <= 4 * topk_count and narrow == 4 and wide & (wide - 1) == 0 and local_experts == 1:
        layer_out, state = dense_experts(
            normed,
            out_proj,
            expert_in[0],
            expert_out[0],
            route_ids,
            route_weights,
            lambda after: state_next(lax.optimization_barrier((ssm_input, after))[0]),
        )
    else:
        normed = jnp.concatenate(normed)
        layer_out = routed_experts(normed, out_proj, expert_in, expert_out, route_ids, route_weights)
        state = state_next(ssm_input)
    return (layer_out, state[None])


def routes(wide, move):
    pairs = []
    for z in range(wide):
        for x in range(2):
            for core in range(2):
                to = move(z, x, core)
                pairs.append(((z * 2 + x) * 2 + core, (to[0] * 2 + to[1]) * 2 + to[2]))
    return pairs


def dense_experts(normed, out_proj, expert_in, expert_out, route_ids, route_weights, state_next):
    frames = route_ids.shape[0]
    wide = lax.axis_size("wide")
    ring = 2 * wide
    z = lax.axis_index("wide")
    x, core = lax.axis_index("narrow") // 2, lax.axis_index("narrow") % 2
    place = jnp.where(x == 0, z, ring - 1 - z)
    axes = ("wide", "narrow")

    def send(value, move):
        return lax.ppermute(value, axes, routes(wide, move))

    def to_core(value):
        return send(value, lambda z, x, c: (z, x, 1 - c))

    def to_x(value):
        return send(value, lambda z, x, c: (z, 1 - x, c))

    def along(value, step):
        def move(z, x, c):
            p = ((z if x == 0 else ring - 1 - z) + step) % ring
            return (p, 0, c) if p < wide else (ring - 1 - p, 1, c)

        return send(value, move)

    out_other, in_other, down_other = to_core(out_proj), to_core(expert_in), to_core(expert_out)

    halves = range(2)
    size = frames // 2
    sent = [to_x(normed[h]) for h in halves]

    columns = lax.optimization_barrier(
        jnp.where(
            core == 0,
            jnp.concatenate([out_proj, out_other], axis=1),
            jnp.concatenate([out_other, out_proj], axis=1),
        )
    )

    def project(rows):
        return jnp.dot(rows, columns, preferred_element_type=jnp.float32).astype(jnp.bfloat16)

    own = [project(normed[h]) for h in halves]
    rows, backs = [], []
    for h in halves:
        backs.append(to_x(project(sent[h])))
        here = own[h]
        rows.append(
            jnp.where(
                x == 0,
                jnp.concatenate([here, backs[h]], axis=1),
                jnp.concatenate([backs[h], here], axis=1),
            )
        )

    far = ring // 2
    hidden_width = expert_out.shape[0]
    is_first = jnp.arange(2 * hidden_width)[None, :] < hidden_width

    def run_experts(parts, gate):
        v = jnp.dot(jnp.concatenate(parts), joined_in, preferred_element_type=jnp.float32)
        hidden = jax.nn.silu(v[:, : 2 * hidden_width]) * v[:, 2 * hidden_width :]
        hidden = (hidden * jnp.where(is_first, gate[:, :1], gate[:, 1:])).astype(jnp.bfloat16)
        return jnp.dot(hidden, joined_down, preferred_element_type=jnp.float32)

    experts = wide * 4
    gates = jnp.sum(
        jnp.where(route_ids[:, :, None] == jnp.arange(experts), route_weights[:, :, None], 0.0), axis=1
    )
    gates, _ = lax.optimization_barrier((gates, sent[1]))
    other = to_x(gates)
    step = 1
    fore_at, back_at = {0: rows}, {0: rows}
    for k in range(1, far):
        fore_at[k] = [along(fore_at[k - 1][h], 1) for h in halves]
        back_at[k] = [along(back_at[k - 1][h], -1) for h in halves]
        if k == 1:
            joined_in = jnp.concatenate(
                [
                    expert_in[:, :hidden_width],
                    in_other[:, :hidden_width],
                    expert_in[:, hidden_width:],
                    in_other[:, hidden_width:],
                ],
                axis=1,
            )
            joined_down = jnp.concatenate([expert_out, down_other], axis=0)
            back_at[1][1], joined_in, joined_down, other = lax.optimization_barrier(
                (back_at[1][1], joined_in, joined_down, other)
            )
            state = state_next(fore_at[1][0])
            gates = jnp.where(x == 0, jnp.stack([gates, other]), jnp.stack([other, gates]))[:, None]
        elif step < wide:
            other, back_at[k][1] = lax.optimization_barrier((other, back_at[k][1]))
            low = z & step == 0
            gates = jnp.where(
                low, jnp.concatenate([gates, other], axis=1), jnp.concatenate([other, gates], axis=1)
            )
            step *= 2
        if step < wide:
            other = send(gates, lambda z, x, c: (z ^ step, x, c))
    while step < wide:
        low = z & step == 0
        gates = jnp.where(
            low, jnp.concatenate([gates, other], axis=1), jnp.concatenate([other, gates], axis=1)
        )
        step *= 2
        if step < wide:
            other = send(gates, lambda z, x, c: (z ^ step, x, c))
    mine = (z * 2 + x) * 2 + core
    pair = jnp.stack([mine, mine + 1 - 2 * core])
    gates = jnp.sum(
        jnp.where(pair[:, None] == jnp.arange(experts), gates[..., None, :], 0.0), axis=-1
    )
    gates = jnp.concatenate([gates[0], gates[1, ::-1]])
    gates = lax.dynamic_slice_in_dim(jnp.concatenate([gates, gates]), place, ring, 0)
    last = [along(fore_at[far - 1][0], 1), along(back_at[far - 1][1], -1)]

    def cut(total, at):
        return [total[at + h * size : at + (h + 1) * size] for h in halves]

    ahead, behind = {}, {}
    ahead[0] = cut(run_experts(rows, gates[0]), 0)
    for k in range(1, far):
        total = run_experts(
            [*back_at[k], *fore_at[k]], jnp.concatenate([gates[k], gates[ring - k]])
        )
        ahead[k], behind[k] = cut(total, 0), cut(total, frames)
    last[0], last[1], state, *near = lax.optimization_barrier(
        (last[0], last[1], state, *ahead[far - 1], *behind[far - 1])
    )
    ahead[far - 1], behind[far - 1] = near[:2], near[2:]
    total = run_experts(last, gates[far]).astype(jnp.bfloat16)

    fore, back = [along(total[:size], 1), None], [None, along(total[size:], -1)]
    for k in range(far - 1, 0, -1):
        before = None
        for h in halves if k < far - 1 else (None,):
            todo = ((fore, 1, ahead, h), (back, -1, behind, h))
            if h is None:
                todo = (
                    (fore, 1, ahead, 1),
                    (back, -1, behind, 0),
                    (fore, 1, ahead, 0),
                    (back, -1, behind, 1),
                )
            loads = []
            for way, step, totals, at in todo:
                load = totals[k][at]
                if way[at] is not None:
                    got = way[at]
                    if before is not None:
                        got = lax.optimization_barrier((got, *before))[0]
                    load = load + got.astype(jnp.float32)
                loads.append(load.astype(jnp.bfloat16))
            before = loads
            for (way, step, totals, at), load in zip(todo, loads):
                way[at] = along(load, step)
    out = []
    for h in halves:
        total = ahead[0][h] + fore[h].astype(jnp.float32) + back[h].astype(jnp.float32)
        out.append((rows[h].astype(jnp.float32) + total).astype(jnp.bfloat16))
    return jnp.concatenate(out), state


def routed_experts(normed, out_proj, expert_in, expert_out, route_ids, route_weights):
    mixer_rows = jnp.dot(
        normed,
        lax.all_gather(out_proj, "narrow", axis=1, tiled=True),
        preferred_element_type=jnp.float32,
    ).astype(jnp.bfloat16)
    frames_here = mixer_rows.shape[0]
    model_width = mixer_rows.shape[1]
    topk_count = route_ids.shape[1]
    local_experts = expert_in.shape[0]
    devices = lax.axis_size(("wide", "narrow"))
    experts = local_experts * devices
    capacity = max(2, frames_here * topk_count * 5 // (4 * experts))
    flat_ids, positions = slot_positions(route_ids, experts)
    owners = jnp.arange(frames_here * topk_count, dtype=jnp.int32) // topk_count
    slot_table = (
        jnp.full((experts, capacity), frames_here, jnp.int32).at[flat_ids, positions].set(owners)
    )
    padded = jnp.concatenate([mixer_rows, jnp.zeros((1, model_width), jnp.bfloat16)], axis=0)
    outgoing = padded[slot_table]
    hidden_width = expert_out.shape[1]
    projected = jnp.einsum(
        "nlcd,ldf->nlcf",
        lax.all_to_all(
            outgoing.reshape(devices, local_experts, capacity, model_width),
            ("wide", "narrow"),
            split_axis=0,
            concat_axis=0,
            tiled=True,
        ),
        expert_in,
        preferred_element_type=jnp.float32,
    )
    hidden = (jax.nn.silu(projected[..., :hidden_width]) * projected[..., hidden_width:]).astype(
        jnp.bfloat16
    )
    returned = lax.all_to_all(
        jnp.einsum("nlcf,lfd->nlcd", hidden, expert_out, preferred_element_type=jnp.float32).astype(
            jnp.bfloat16
        ),
        ("wide", "narrow"),
        split_axis=0,
        concat_axis=0,
        tiled=True,
    )
    returned = returned.reshape(experts, capacity, model_width)
    picked = returned[flat_ids, positions].reshape(frames_here, topk_count, model_width)
    expert_sum = jnp.einsum("tk,tkd->td", route_weights, picked.astype(jnp.float32))
    layer_out = (mixer_rows.astype(jnp.float32) + expert_sum).astype(jnp.bfloat16)
    return layer_out


def solution(mesh):
    placed = (
        P(("groups", "wide", "narrow"), None),
        P(("groups", "wide", "narrow"), None),
        P(("groups", "wide", "narrow"), None),
        P(("groups", "wide", "narrow"), None),
        P(("groups", "wide", "narrow"), None),
        P(),
        P(),
        P(),
        P(),
        P(("groups", "wide", "narrow"), None, None, None),
        P(None, "narrow"),
        P(("wide", "narrow"), None, None),
        P(("wide", "narrow"), None, None),
        P(("groups", "wide", "narrow"), None),
        P(("groups", "wide", "narrow"), None),
    )
    return jax.shard_map(
        body,
        mesh=mesh,
        in_specs=placed,
        out_specs=(
            P(("groups", "wide", "narrow"), None),
            P(("groups", "wide", "narrow"), None, None, None),
        ),
        check_vma=False,
    )
```

```python
import functools

import jax
import jax.numpy as jnp
from jax import lax
from jax.experimental import pallas as pl
from jax.experimental.pallas import tpu as pltpu
from jax.sharding import PartitionSpec as P

epsilon = 1e-05


CHUNK = 8
NT = (((1,), (1,)), ((), ()))
TN = (((0,), (0,)), ((), ()))


def column_of(row_ref):
    count = row_ref.shape[1]
    i = lax.broadcasted_iota(jnp.int32, (count, count), 0)
    j = lax.broadcasted_iota(jnp.int32, (count, count), 1)
    return jnp.sum(jnp.where(i == j, row_ref[...], 0.0), axis=1, keepdims=True)


def decays(dt_ref, bias_ref, a_ref, step_ref, decay_ref):
    frames = dt_ref.shape[1]
    step_size = jax.nn.softplus(dt_ref[...] + column_of(bias_ref))
    rise = step_size * -jnp.exp(column_of(a_ref))
    s = lax.broadcasted_iota(jnp.int32, (frames, frames), 0)
    t = lax.broadcasted_iota(jnp.int32, (frames, frames), 1)
    upto = jnp.where(s <= t, 1.0, 0.0)
    step_ref[...] = step_size
    decay_ref[...] = jnp.dot(
        rise, upto, precision=lax.Precision.HIGHEST, preferred_element_type=jnp.float32
    )


def mixer_kernel(
    skip_ref,
    x_ref,
    z_ref,
    b_ref,
    c_ref,
    dt_ref,
    bias_ref,
    a_ref,
    gain_ref,
    state_ref,
    top_ref,
    bottom_ref,
    g_ref,
    ss_ref,
    step_ref,
    decay_ref,
):
    i = pl.program_id(0)
    frames, width = x_ref.shape
    head = width // CHUNK
    pl.when(i == 0)(lambda: decays(dt_ref, bias_ref, a_ref, step_ref, decay_ref))
    chunk = pl.ds(pl.multiple_of(i * CHUNK, CHUNK), CHUNK)
    step_size, decay = step_ref[chunk, :], decay_ref[chunk, :]
    decay_col = decay.T
    carry_col = jnp.exp(decay_col)
    t = lax.broadcasted_iota(jnp.int32, (frames, frames), 0)
    s = lax.broadcasted_iota(jnp.int32, (frames, frames), 1)
    c = c_ref[...]
    scores = lax.dot_general(c, b_ref[...], NT, preferred_element_type=jnp.float32)
    scores = jnp.where(s <= t, scores, 0.0)
    cc = jnp.concatenate([c, c], axis=1)
    left = lax.broadcasted_iota(jnp.int32, (frames, 2 * head), 1) < head
    squares = None
    for pair in range(CHUNK // 2):
        mixes = []
        for h in (2 * pair, 2 * pair + 1):
            spread = jnp.exp(jnp.minimum(decay_col[:, h : h + 1] - decay[h : h + 1, :], 0.0))
            mixes.append((spread * (scores * step_size[h : h + 1, :])).astype(jnp.bfloat16))
        at = slice(2 * head * pair, 2 * head * (pair + 1))
        x = x_ref[:, at]
        zero = jnp.zeros_like(x)
        y = jnp.dot(
            jnp.concatenate(mixes, axis=1),
            jnp.concatenate([jnp.where(left, x, zero), jnp.where(left, zero, x)], axis=0),
            preferred_element_type=jnp.float32,
        )
        state = state_ref[at, :]
        high = state.astype(jnp.bfloat16)
        low = (state - high.astype(jnp.float32)).astype(jnp.bfloat16)
        carried = lax.dot_general(
            cc, jnp.concatenate([high, low], axis=1), NT, preferred_element_type=jnp.float32
        )
        factor = jnp.where(
            left, carry_col[:, 2 * pair : 2 * pair + 1], carry_col[:, 2 * pair + 1 : 2 * pair + 2]
        )
        skip = jnp.where(left[:1], skip_ref[i * CHUNK + 2 * pair], skip_ref[i * CHUNK + 2 * pair + 1])
        mixed = y + factor * carried + skip * x.astype(jnp.float32)
        z = z_ref[:, at].astype(jnp.float32)
        g = mixed * jax.nn.silu(z)
        g_ref[i, :, at] = g
        squares = g * g if squares is None else squares + g * g

    @pl.when(i == 0)
    def _():
        ss_ref[...] = squares

    @pl.when(i > 0)
    def _():
        ss_ref[...] += squares

    steps = g_ref.shape[0]

    @pl.when(i == steps - 1)
    def _():
        mean = jnp.sum(ss_ref[...], axis=1, keepdims=True) / (steps * width)
        scale = lax.rsqrt(mean + epsilon)
        for j in range(steps):
            at = slice(j * width, (j + 1) * width)
            normed = (g_ref[j] * scale * gain_ref[:, at]).astype(jnp.bfloat16)
            top_ref[:, at] = normed[: frames // 2]
            bottom_ref[:, at] = normed[frames // 2 :]


def state_kernel(x_ref, b_ref, dt_ref, bias_ref, a_ref, state_ref, out_ref, step_ref, decay_ref):
    i = pl.program_id(0)
    frames, width = x_ref.shape
    head = width // CHUNK
    pl.when(i == 0)(lambda: decays(dt_ref, bias_ref, a_ref, step_ref, decay_ref))
    chunk = pl.ds(pl.multiple_of(i * CHUNK, CHUNK), CHUNK)
    step_size, decay = step_ref[chunk, :], decay_ref[chunk, :]
    end = decay[:, frames - 1 : frames]
    tail = (jnp.exp(end - decay) * step_size).T
    kept = jnp.exp(end)
    left = lax.broadcasted_iota(jnp.int32, (frames, 2 * head), 1) < head
    upper = lax.broadcasted_iota(jnp.int32, (2 * head, b_ref.shape[1]), 0) < head
    for pair in range(CHUNK // 2):
        at = slice(2 * head * pair, 2 * head * (pair + 1))
        factor = jnp.where(left, tail[:, 2 * pair : 2 * pair + 1], tail[:, 2 * pair + 1 : 2 * pair + 2])
        scaled = (x_ref[:, at].astype(jnp.float32) * factor).astype(jnp.bfloat16)
        added = lax.dot_general(scaled, b_ref[...], TN, preferred_element_type=jnp.float32)
        keep = jnp.where(upper, kept[2 * pair : 2 * pair + 1, :], kept[2 * pair + 1 : 2 * pair + 2, :])
        out_ref[at, :] = keep * state_ref[at, :] + added


def ssm_mixer(
    ssm_input, gate_input, b_proj, c_proj, dt_raw, a_log, dt_bias, d_skip, norm_gain, state_in
):
    frames, width = ssm_input.shape
    heads, head, inner = state_in.shape
    steps = heads // CHUNK
    part = width // steps
    state = state_in.reshape(width, inner)
    dt = dt_raw.T
    column = pl.BlockSpec((frames, part), lambda i: (0, i))
    whole = pl.BlockSpec((frames, inner), lambda i: (0, 0))
    per_head = pl.BlockSpec((heads, frames), lambda i: (0, 0))
    scalar = pl.BlockSpec((1, heads), lambda i: (0, 0))
    rows = pl.BlockSpec((part, inner), lambda i: (i, 0))
    full_row = pl.BlockSpec((1, width), lambda i: (0, 0))
    tables = [pltpu.VMEM((heads, frames), jnp.float32)] * 2
    normed = pl.pallas_call(
        mixer_kernel,
        grid=(steps,),
        in_specs=[
            pl.BlockSpec(memory_space=pltpu.SMEM),
            column,
            column,
            whole,
            whole,
            per_head,
            scalar,
            scalar,
            full_row,
            rows,
        ],
        out_specs=[pl.BlockSpec((frames // 2, width), lambda i: (0, 0))] * 2,
        out_shape=[jax.ShapeDtypeStruct((frames // 2, width), jnp.bfloat16)] * 2,
        scratch_shapes=[
            pltpu.VMEM((steps, frames, part), jnp.float32),
            pltpu.VMEM((frames, 2 * head), jnp.float32),
            *tables,
        ],
        compiler_params=pltpu.CompilerParams(vmem_limit_bytes=56 << 20),
        cost_estimate=pl.CostEstimate(flops=400_000_000, bytes_accessed=6_000_000, transcendentals=2_000_000),
        name="mixer",
    )(
        d_skip,
        ssm_input,
        gate_input,
        b_proj,
        c_proj,
        dt,
        dt_bias[None, :],
        a_log[None, :],
        norm_gain[None, :],
        state,
    )

    def state_next(ssm_input):
        out = pl.pallas_call(
            state_kernel,
            grid=(steps,),
            in_specs=[column, whole, per_head, scalar, scalar, rows],
            out_specs=rows,
            out_shape=jax.ShapeDtypeStruct((width, inner), jnp.float32),
            scratch_shapes=tables,
            compiler_params=pltpu.CompilerParams(vmem_limit_bytes=16 << 20),
            cost_estimate=pl.CostEstimate(flops=70_000_000, bytes_accessed=3_000_000, transcendentals=20_000),
            name="state",
        )(ssm_input, b_proj, dt, dt_bias[None, :], a_log[None, :], state)
        return out.reshape(heads, head, inner)

    return (normed, state_next)


def slot_positions(route_ids, experts):
    flat_ids = route_ids.reshape(-1)
    onehot = (flat_ids[:, None] == jnp.arange(experts, dtype=jnp.int32)[None, :]).astype(jnp.int32)
    earlier = jnp.cumsum(onehot, axis=0) - onehot
    return (flat_ids, jnp.sum(earlier * onehot, axis=1))


def body(
    ssm_input,
    gate_input,
    b_proj,
    c_proj,
    dt_raw,
    a_log,
    dt_bias,
    d_skip,
    norm_gain,
    state_in,
    out_proj,
    expert_in,
    expert_out,
    route_ids,
    route_weights,
):
    normed, state_next = ssm_mixer(
        ssm_input,
        gate_input,
        b_proj,
        c_proj,
        dt_raw,
        a_log,
        dt_bias,
        d_skip,
        norm_gain,
        state_in[0],
    )
    frames_here, topk_count = route_ids.shape
    local_experts = expert_in.shape[0]
    experts = local_experts * lax.axis_size(("wide", "narrow"))
    wide, narrow = lax.axis_size("wide"), lax.axis_size("narrow")
    if experts <= 4 * topk_count and narrow == 4 and wide & (wide - 1) == 0 and local_experts == 1:
        layer_out, state = dense_experts(
            normed,
            out_proj,
            expert_in[0],
            expert_out[0],
            route_ids,
            route_weights,
            lambda tie: state_next(after(ssm_input, tie)),
        )
    else:
        normed = jnp.concatenate(normed)
        layer_out = routed_experts(normed, out_proj, expert_in, expert_out, route_ids, route_weights)
        state = state_next(ssm_input)
    return (layer_out, state[None])


def routes(wide, move):
    pairs = []
    for z in range(wide):
        for x in range(2):
            for core in range(2):
                to = move(z, x, core)
                pairs.append(((z * 2 + x) * 2 + core, (to[0] * 2 + to[1]) * 2 + to[2]))
    return pairs


def after(value, *others):
    return lax.optimization_barrier((value, *others))[0]


def dense_experts(normed, out_proj, expert_in, expert_out, route_ids, route_weights, state_next):
    frames = route_ids.shape[0]
    wide = lax.axis_size("wide")
    ring = 2 * wide
    z = lax.axis_index("wide")
    x, core = lax.axis_index("narrow") // 2, lax.axis_index("narrow") % 2
    place = jnp.where(x == 0, z, ring - 1 - z)
    axes = ("wide", "narrow")

    def send(value, move):
        return lax.ppermute(value, axes, routes(wide, move))

    def to_core(value):
        return send(value, lambda z, x, c: (z, x, 1 - c))

    def to_x(value):
        return send(value, lambda z, x, c: (z, 1 - x, c))

    def along(value, step):
        def move(z, x, c):
            p = ((z if x == 0 else ring - 1 - z) + step) % ring
            return (p, 0, c) if p < wide else (ring - 1 - p, 1, c)

        return send(value, move)

    out_other, in_other, down_other = to_core(out_proj), to_core(expert_in), to_core(expert_out)

    halves = range(2)
    size = frames // 2
    sent = [to_x(normed[h]) for h in halves]

    columns = lax.optimization_barrier(
        jnp.where(
            core == 0,
            jnp.concatenate([out_proj, out_other], axis=1),
            jnp.concatenate([out_other, out_proj], axis=1),
        )
    )

    def project(rows):
        return jnp.dot(rows, columns, preferred_element_type=jnp.float32).astype(jnp.bfloat16)

    own = [project(normed[h]) for h in halves]
    rows, peer = [], None
    for h in halves:
        arrived = sent[h]
        if peer is not None:
            arrived = after(arrived, peer)
        peer = project(arrived)
        back = to_x(peer)
        rows.append(
            jnp.where(
                x == 0,
                jnp.concatenate([own[h], back], axis=1),
                jnp.concatenate([back, own[h]], axis=1),
            )
        )

    far = ring // 2
    hidden_width = expert_out.shape[0]
    is_first = jnp.arange(2 * hidden_width)[None, :] < hidden_width

    def join(in_other, down_other):
        joined_in = jnp.concatenate(
            [
                expert_in[:, :hidden_width],
                in_other[:, :hidden_width],
                expert_in[:, hidden_width:],
                in_other[:, hidden_width:],
            ],
            axis=1,
        )
        return joined_in, jnp.concatenate([expert_out, down_other], axis=0)

    def run_experts(parts, gate):
        v = jnp.dot(jnp.concatenate(parts), joined_in, preferred_element_type=jnp.float32)
        hidden = jax.nn.silu(v[:, : 2 * hidden_width]) * v[:, 2 * hidden_width :]
        hidden = (hidden * jnp.where(is_first, gate[:, :1], gate[:, 1:])).astype(jnp.bfloat16)
        return jnp.dot(hidden, joined_down, preferred_element_type=jnp.float32)

    def merge(gates, other, low):
        return jnp.where(
            low, jnp.concatenate([gates, other], axis=1), jnp.concatenate([other, gates], axis=1)
        )

    experts = wide * 4
    gates = jnp.sum(
        jnp.where(route_ids[:, :, None] == jnp.arange(experts), route_weights[:, :, None], 0.0), axis=1
    )
    other = to_x(after(gates, sent[1]))
    step = 0
    fore_at, back_at = {0: rows}, {0: rows}
    for k in range(1, far):
        fore_at[k] = [along(fore_at[k - 1][h], 1) for h in halves]
        back_at[k] = [along(back_at[k - 1][h], -1) for h in halves]
        if k == 1:
            fore_at[k][0], back_at[k][0], in_other, down_other = lax.optimization_barrier(
                (fore_at[k][0], back_at[k][0], in_other, down_other)
            )
            for way in (fore_at[k], back_at[k]):
                way[1] = after(way[1], way[0])
        if step < wide:
            other, back_at[k][1] = lax.optimization_barrier((other, back_at[k][1]))
            if step == 0:
                gates = jnp.where(x == 0, jnp.stack([gates, other]), jnp.stack([other, gates]))
                gates, step = gates[:, None], 1
            else:
                gates, step = merge(gates, other, z & step == 0), 2 * step
            if step < wide:
                other = send(gates, lambda z, x, c: (z ^ step, x, c))
        if k == far - 1:
            joined = join(in_other, down_other)
            back_at[k][1], joined_in, joined_down = lax.optimization_barrier((back_at[k][1], *joined))
    while step < wide:
        gates, step = merge(gates, other, z & step == 0), 2 * step
        if step < wide:
            other = send(gates, lambda z, x, c: (z ^ step, x, c))
    mine = (z * 2 + x) * 2 + core
    pair = jnp.stack([mine, mine + 1 - 2 * core])
    gates = jnp.sum(
        jnp.where(pair[:, None] == jnp.arange(experts), gates[..., None, :], 0.0), axis=-1
    )
    gates = jnp.concatenate([gates[0], gates[1, ::-1]])
    gates = lax.dynamic_slice_in_dim(jnp.concatenate([gates, gates]), place, ring, 0)
    last = [along(fore_at[far - 1][0], 1), along(back_at[far - 1][1], -1)]

    def hop_experts(k, tie):
        parts = rows if k == 0 else [*back_at[k], *fore_at[k]]
        gate = gates[0] if k == 0 else jnp.concatenate([gates[k], gates[ring - k]])
        if tie is not None:
            parts = [after(part, tie) for part in parts]
        total = run_experts(parts, gate)
        cut = [total[i * size : (i + 1) * size] for i in range(len(parts))]
        return cut[:2], cut[2:]

    ahead, behind = hop_experts(far - 1, None)
    last[0], last[1], *near = lax.optimization_barrier((*last, *ahead, *behind))
    ahead, behind = near[:2], near[2:]
    total = run_experts(last, gates[far]).astype(jnp.bfloat16)
    fore, back = [along(total[:size], 1), None], [None, along(total[size:], -1)]
    tie = total
    for k in range(far - 1, 0, -1):
        coming = hop_experts(k - 1, tie)
        if k == 1:
            state = state_next(tie)
        before = ()
        groups = [((fore, 1, ahead, h), (back, -1, behind, h)) for h in halves]
        if k == far - 1:
            groups = [((fore, 1, ahead, 1), (back, -1, behind, 0)), ((fore, 1, ahead, 0), (back, -1, behind, 1))]
        for group in groups:
            loads = []
            for way, step, totals, h in group:
                load = totals[h]
                if way[h] is not None:
                    load = load + after(way[h], *before).astype(jnp.float32)
                loads.append(load.astype(jnp.bfloat16))
            before = loads
            for (way, step, totals, h), load in zip(group, loads):
                way[h] = along(load, step)
        tie = loads[0]
        ahead, behind = coming
    out = []
    for h in halves:
        total = ahead[h] + fore[h].astype(jnp.float32) + back[h].astype(jnp.float32)
        out.append((rows[h].astype(jnp.float32) + total).astype(jnp.bfloat16))
    return jnp.concatenate(out), state


def routed_experts(normed, out_proj, expert_in, expert_out, route_ids, route_weights):
    mixer_rows = jnp.dot(
        normed,
        lax.all_gather(out_proj, "narrow", axis=1, tiled=True),
        preferred_element_type=jnp.float32,
    ).astype(jnp.bfloat16)
    frames_here = mixer_rows.shape[0]
    model_width = mixer_rows.shape[1]
    topk_count = route_ids.shape[1]
    local_experts = expert_in.shape[0]
    devices = lax.axis_size(("wide", "narrow"))
    experts = local_experts * devices
    capacity = max(2, frames_here * topk_count * 5 // (4 * experts))
    flat_ids, positions = slot_positions(route_ids, experts)
    owners = jnp.arange(frames_here * topk_count, dtype=jnp.int32) // topk_count
    slot_table = (
        jnp.full((experts, capacity), frames_here, jnp.int32).at[flat_ids, positions].set(owners)
    )
    padded = jnp.concatenate([mixer_rows, jnp.zeros((1, model_width), jnp.bfloat16)], axis=0)
    outgoing = padded[slot_table]
    hidden_width = expert_out.shape[1]
    projected = jnp.einsum(
        "nlcd,ldf->nlcf",
        lax.all_to_all(
            outgoing.reshape(devices, local_experts, capacity, model_width),
            ("wide", "narrow"),
            split_axis=0,
            concat_axis=0,
            tiled=True,
        ),
        expert_in,
        preferred_element_type=jnp.float32,
    )
    hidden = (jax.nn.silu(projected[..., :hidden_width]) * projected[..., hidden_width:]).astype(
        jnp.bfloat16
    )
    returned = lax.all_to_all(
        jnp.einsum("nlcf,lfd->nlcd", hidden, expert_out, preferred_element_type=jnp.float32).astype(
            jnp.bfloat16
        ),
        ("wide", "narrow"),
        split_axis=0,
        concat_axis=0,
        tiled=True,
    )
    returned = returned.reshape(experts, capacity, model_width)
    picked = returned[flat_ids, positions].reshape(frames_here, topk_count, model_width)
    expert_sum = jnp.einsum("tk,tkd->td", route_weights, picked.astype(jnp.float32))
    layer_out = (mixer_rows.astype(jnp.float32) + expert_sum).astype(jnp.bfloat16)
    return layer_out


def solution(mesh):
    placed = (
        P(("groups", "wide", "narrow"), None),
        P(("groups", "wide", "narrow"), None),
        P(("groups", "wide", "narrow"), None),
        P(("groups", "wide", "narrow"), None),
        P(("groups", "wide", "narrow"), None),
        P(),
        P(),
        P(),
        P(),
        P(("groups", "wide", "narrow"), None, None, None),
        P(None, "narrow"),
        P(("wide", "narrow"), None, None),
        P(("wide", "narrow"), None, None),
        P(("groups", "wide", "narrow"), None),
        P(("groups", "wide", "narrow"), None),
    )
    return jax.shard_map(
        body,
        mesh=mesh,
        in_specs=placed,
        out_specs=(
            P(("groups", "wide", "narrow"), None),
            P(("groups", "wide", "narrow"), None, None, None),
        ),
        check_vma=False,
    )
```

```python
import functools

import jax
import jax.numpy as jnp
from jax import lax
from jax.experimental import pallas as pl
from jax.experimental.pallas import tpu as pltpu
from jax.sharding import PartitionSpec as P

epsilon = 1e-05


CHUNK = 8
NT = (((1,), (1,)), ((), ()))
TN = (((0,), (0,)), ((), ()))


def column_of(row_ref):
    count = row_ref.shape[1]
    i = lax.broadcasted_iota(jnp.int32, (count, count), 0)
    j = lax.broadcasted_iota(jnp.int32, (count, count), 1)
    return jnp.sum(jnp.where(i == j, row_ref[...], 0.0), axis=1, keepdims=True)


def decays(dt_ref, bias_ref, a_ref, step_ref, decay_ref):
    frames = dt_ref.shape[1]
    step_size = jax.nn.softplus(dt_ref[...] + column_of(bias_ref))
    rise = step_size * -jnp.exp(column_of(a_ref))
    s = lax.broadcasted_iota(jnp.int32, (frames, frames), 0)
    t = lax.broadcasted_iota(jnp.int32, (frames, frames), 1)
    upto = jnp.where(s <= t, 1.0, 0.0)
    step_ref[...] = step_size
    decay_ref[...] = jnp.dot(
        rise, upto, precision=lax.Precision.HIGHEST, preferred_element_type=jnp.float32
    )


def mixer_kernel(
    skip_ref,
    x_ref,
    z_ref,
    b_ref,
    c_ref,
    dt_ref,
    bias_ref,
    a_ref,
    gain_ref,
    state_ref,
    top_ref,
    bottom_ref,
    g_ref,
    ss_ref,
    step_ref,
    decay_ref,
):
    i = pl.program_id(0)
    frames, width = x_ref.shape
    head = width // CHUNK
    pl.when(i == 0)(lambda: decays(dt_ref, bias_ref, a_ref, step_ref, decay_ref))
    chunk = pl.ds(pl.multiple_of(i * CHUNK, CHUNK), CHUNK)
    step_size, decay = step_ref[chunk, :], decay_ref[chunk, :]
    decay_col = decay.T
    carry_col = jnp.exp(decay_col)
    t = lax.broadcasted_iota(jnp.int32, (frames, frames), 0)
    s = lax.broadcasted_iota(jnp.int32, (frames, frames), 1)
    c = c_ref[...]
    scores = lax.dot_general(c, b_ref[...], NT, preferred_element_type=jnp.float32)
    scores = jnp.where(s <= t, scores, 0.0)
    cc = jnp.concatenate([c, c], axis=1)
    left = lax.broadcasted_iota(jnp.int32, (frames, 2 * head), 1) < head
    squares = None
    for pair in range(CHUNK // 2):
        mixes = []
        for h in (2 * pair, 2 * pair + 1):
            spread = jnp.exp(jnp.minimum(decay_col[:, h : h + 1] - decay[h : h + 1, :], 0.0))
            mixes.append((spread * (scores * step_size[h : h + 1, :])).astype(jnp.bfloat16))
        at = slice(2 * head * pair, 2 * head * (pair + 1))
        x = x_ref[:, at]
        zero = jnp.zeros_like(x)
        y = jnp.dot(
            jnp.concatenate(mixes, axis=1),
            jnp.concatenate([jnp.where(left, x, zero), jnp.where(left, zero, x)], axis=0),
            preferred_element_type=jnp.float32,
        )
        state = state_ref[at, :]
        high = state.astype(jnp.bfloat16)
        low = (state - high.astype(jnp.float32)).astype(jnp.bfloat16)
        carried = lax.dot_general(
            cc, jnp.concatenate([high, low], axis=1), NT, preferred_element_type=jnp.float32
        )
        factor = jnp.where(
            left, carry_col[:, 2 * pair : 2 * pair + 1], carry_col[:, 2 * pair + 1 : 2 * pair + 2]
        )
        skip = jnp.where(left[:1], skip_ref[i * CHUNK + 2 * pair], skip_ref[i * CHUNK + 2 * pair + 1])
        mixed = y + factor * carried + skip * x.astype(jnp.float32)
        z = z_ref[:, at].astype(jnp.float32)
        g = mixed * jax.nn.silu(z)
        g_ref[i, :, at] = g
        squares = g * g if squares is None else squares + g * g

    @pl.when(i == 0)
    def _():
        ss_ref[...] = squares

    @pl.when(i > 0)
    def _():
        ss_ref[...] += squares

    steps = g_ref.shape[0]

    @pl.when(i == steps - 1)
    def _():
        mean = jnp.sum(ss_ref[...], axis=1, keepdims=True) / (steps * width)
        scale = lax.rsqrt(mean + epsilon)
        for j in range(steps):
            at = slice(j * width, (j + 1) * width)
            normed = (g_ref[j] * scale * gain_ref[:, at]).astype(jnp.bfloat16)
            top_ref[:, at] = normed[: frames // 2]
            bottom_ref[:, at] = normed[frames // 2 :]


def state_kernel(x_ref, b_ref, dt_ref, bias_ref, a_ref, state_ref, out_ref, step_ref, decay_ref):
    i = pl.program_id(0)
    frames, width = x_ref.shape
    head = width // CHUNK
    pl.when(i == 0)(lambda: decays(dt_ref, bias_ref, a_ref, step_ref, decay_ref))
    chunk = pl.ds(pl.multiple_of(i * CHUNK, CHUNK), CHUNK)
    step_size, decay = step_ref[chunk, :], decay_ref[chunk, :]
    end = decay[:, frames - 1 : frames]
    tail = (jnp.exp(end - decay) * step_size).T
    kept = jnp.exp(end)
    left = lax.broadcasted_iota(jnp.int32, (frames, 2 * head), 1) < head
    upper = lax.broadcasted_iota(jnp.int32, (2 * head, b_ref.shape[1]), 0) < head
    for pair in range(CHUNK // 2):
        at = slice(2 * head * pair, 2 * head * (pair + 1))
        factor = jnp.where(left, tail[:, 2 * pair : 2 * pair + 1], tail[:, 2 * pair + 1 : 2 * pair + 2])
        scaled = (x_ref[:, at].astype(jnp.float32) * factor).astype(jnp.bfloat16)
        added = lax.dot_general(scaled, b_ref[...], TN, preferred_element_type=jnp.float32)
        keep = jnp.where(upper, kept[2 * pair : 2 * pair + 1, :], kept[2 * pair + 1 : 2 * pair + 2, :])
        out_ref[at, :] = keep * state_ref[at, :] + added


def ssm_mixer(
    ssm_input, gate_input, b_proj, c_proj, dt_raw, a_log, dt_bias, d_skip, norm_gain, state_in
):
    frames, width = ssm_input.shape
    heads, head, inner = state_in.shape
    steps = heads // CHUNK
    part = width // steps
    state = state_in.reshape(width, inner)
    dt = dt_raw.T
    column = pl.BlockSpec((frames, part), lambda i: (0, i))
    whole = pl.BlockSpec((frames, inner), lambda i: (0, 0))
    per_head = pl.BlockSpec((heads, frames), lambda i: (0, 0))
    scalar = pl.BlockSpec((1, heads), lambda i: (0, 0))
    rows = pl.BlockSpec((part, inner), lambda i: (i, 0))
    full_row = pl.BlockSpec((1, width), lambda i: (0, 0))
    tables = [pltpu.VMEM((heads, frames), jnp.float32)] * 2
    normed = pl.pallas_call(
        mixer_kernel,
        grid=(steps,),
        in_specs=[
            pl.BlockSpec(memory_space=pltpu.SMEM),
            column,
            column,
            whole,
            whole,
            per_head,
            scalar,
            scalar,
            full_row,
            rows,
        ],
        out_specs=[pl.BlockSpec((frames // 2, width), lambda i: (0, 0))] * 2,
        out_shape=[jax.ShapeDtypeStruct((frames // 2, width), jnp.bfloat16)] * 2,
        scratch_shapes=[
            pltpu.VMEM((steps, frames, part), jnp.float32),
            pltpu.VMEM((frames, 2 * head), jnp.float32),
            *tables,
        ],
        compiler_params=pltpu.CompilerParams(vmem_limit_bytes=56 << 20),
        cost_estimate=pl.CostEstimate(flops=400_000_000, bytes_accessed=6_000_000, transcendentals=2_000_000),
        name="mixer",
    )(
        d_skip,
        ssm_input,
        gate_input,
        b_proj,
        c_proj,
        dt,
        dt_bias[None, :],
        a_log[None, :],
        norm_gain[None, :],
        state,
    )

    def state_next(ssm_input):
        out = pl.pallas_call(
            state_kernel,
            grid=(steps,),
            in_specs=[column, whole, per_head, scalar, scalar, rows],
            out_specs=rows,
            out_shape=jax.ShapeDtypeStruct((width, inner), jnp.float32),
            scratch_shapes=tables,
            compiler_params=pltpu.CompilerParams(vmem_limit_bytes=16 << 20),
            cost_estimate=pl.CostEstimate(flops=70_000_000, bytes_accessed=3_000_000, transcendentals=20_000),
            name="state",
        )(ssm_input, b_proj, dt, dt_bias[None, :], a_log[None, :], state)
        return out.reshape(heads, head, inner)

    return (normed, state_next)


def slot_positions(route_ids, experts):
    flat_ids = route_ids.reshape(-1)
    onehot = (flat_ids[:, None] == jnp.arange(experts, dtype=jnp.int32)[None, :]).astype(jnp.int32)
    earlier = jnp.cumsum(onehot, axis=0) - onehot
    return (flat_ids, jnp.sum(earlier * onehot, axis=1))


def body(
    ssm_input,
    gate_input,
    b_proj,
    c_proj,
    dt_raw,
    a_log,
    dt_bias,
    d_skip,
    norm_gain,
    state_in,
    out_proj,
    expert_in,
    expert_out,
    route_ids,
    route_weights,
):
    normed, state_next = ssm_mixer(
        ssm_input,
        gate_input,
        b_proj,
        c_proj,
        dt_raw,
        a_log,
        dt_bias,
        d_skip,
        norm_gain,
        state_in[0],
    )
    frames_here, topk_count = route_ids.shape
    local_experts = expert_in.shape[0]
    experts = local_experts * lax.axis_size(("wide", "narrow"))
    wide, narrow = lax.axis_size("wide"), lax.axis_size("narrow")
    if experts <= 4 * topk_count and narrow == 4 and wide & (wide - 1) == 0 and local_experts == 1:
        layer_out, state = dense_experts(
            normed,
            out_proj,
            expert_in[0],
            expert_out[0],
            route_ids,
            route_weights,
            lambda tie: state_next(after(ssm_input, tie)),
        )
    else:
        normed = jnp.concatenate(normed)
        layer_out = routed_experts(normed, out_proj, expert_in, expert_out, route_ids, route_weights)
        state = state_next(ssm_input)
    return (layer_out, state[None])


def routes(wide, move):
    pairs = []
    for z in range(wide):
        for x in range(2):
            for core in range(2):
                to = move(z, x, core)
                pairs.append(((z * 2 + x) * 2 + core, (to[0] * 2 + to[1]) * 2 + to[2]))
    return pairs


def after(value, *others):
    return lax.optimization_barrier((value, *others))[0]


def dense_experts(normed, out_proj, expert_in, expert_out, route_ids, route_weights, state_next):
    frames = route_ids.shape[0]
    wide = lax.axis_size("wide")
    ring = 2 * wide
    z = lax.axis_index("wide")
    x, core = lax.axis_index("narrow") // 2, lax.axis_index("narrow") % 2
    place = jnp.where(x == 0, z, ring - 1 - z)
    axes = ("wide", "narrow")

    def send(value, move):
        return lax.ppermute(value, axes, routes(wide, move))

    def to_core(value):
        return send(value, lambda z, x, c: (z, x, 1 - c))

    def to_x(value):
        return send(value, lambda z, x, c: (z, 1 - x, c))

    def along(value, step):
        def move(z, x, c):
            p = ((z if x == 0 else ring - 1 - z) + step) % ring
            return (p, 0, c) if p < wide else (ring - 1 - p, 1, c)

        return send(value, move)

    out_other, in_other, down_other = to_core(out_proj), to_core(expert_in), to_core(expert_out)

    experts = wide * 4
    gates = jnp.sum(
        jnp.where(route_ids[:, :, None] == jnp.arange(experts), route_weights[:, :, None], 0.0), axis=1
    )
    normed_top, normed_bottom, other = lax.optimization_barrier((*normed, to_x(gates)))
    gates = jnp.where(x == 0, jnp.stack([gates, other]), jnp.stack([other, gates]))[:, None]

    halves = range(2)
    size = frames // 2
    hidden_width = expert_out.shape[0]
    expert_in = after(expert_in, normed_top)
    gate_in, up_in = lax.optimization_barrier((expert_in[:, :hidden_width], expert_in[:, hidden_width:]))
    sent = [to_x(normed_top), to_x(after(normed_bottom, gate_in))]

    step = 1
    while step < wide:
        other = send(gates, lambda z, x, c: (z ^ step, x, c))
        gates = jnp.where(
            z & step == 0,
            jnp.concatenate([gates, other], axis=1),
            jnp.concatenate([other, gates], axis=1),
        )
        step *= 2
    sent[1], gates = lax.optimization_barrier((sent[1], gates))
    mine = (z * 2 + x) * 2 + core
    pair = jnp.stack([mine, mine + 1 - 2 * core])
    gates = jnp.sum(
        jnp.where(pair[:, None] == jnp.arange(experts), gates[..., None, :], 0.0), axis=-1
    )
    gates = jnp.concatenate([gates[0], gates[1, ::-1]])
    gates = lax.dynamic_slice_in_dim(jnp.concatenate([gates, gates]), place, ring, 0)

    columns = lax.optimization_barrier(
        jnp.where(
            core == 0,
            jnp.concatenate([out_proj, out_other], axis=1),
            jnp.concatenate([out_other, out_proj], axis=1),
        )
    )

    def project(rows):
        return jnp.dot(rows, columns, preferred_element_type=jnp.float32).astype(jnp.bfloat16)

    own = [project(normed_top), project(normed_bottom)]
    rows, peer = [], None
    for h in halves:
        arrived = sent[h]
        if peer is not None:
            arrived = after(arrived, peer)
        peer = project(arrived)
        back = to_x(peer)
        rows.append(
            jnp.where(
                x == 0,
                jnp.concatenate([own[h], back], axis=1),
                jnp.concatenate([back, own[h]], axis=1),
            )
        )

    far = ring // 2
    fore_at, back_at = {0: rows}, {0: rows}
    for k in range(1, far):
        fore_at[k] = [along(fore_at[k - 1][h], 1) for h in halves]
        back_at[k] = [along(back_at[k - 1][h], -1) for h in halves]
    last = [along(fore_at[far - 1][0], 1), along(back_at[far - 1][1], -1)]

    joined_in = jnp.concatenate(
        [gate_in, in_other[:, :hidden_width], up_in, in_other[:, hidden_width:]], axis=1
    )
    joined_down = jnp.concatenate([expert_out, down_other], axis=0)
    joined_in, joined_down = lax.optimization_barrier((joined_in, joined_down))
    is_first = jnp.arange(2 * hidden_width)[None, :] < hidden_width

    def run_experts(parts, gate):
        v = jnp.dot(jnp.concatenate(parts), joined_in, preferred_element_type=jnp.float32)
        hidden = jax.nn.silu(v[:, : 2 * hidden_width]) * v[:, 2 * hidden_width :]
        hidden = (hidden * jnp.where(is_first, gate[:, :1], gate[:, 1:])).astype(jnp.bfloat16)
        return jnp.dot(hidden, joined_down, preferred_element_type=jnp.float32)

    def hop_experts(k, tie):
        parts = rows if k == 0 else [*back_at[k], *fore_at[k]]
        gate = gates[0] if k == 0 else jnp.concatenate([gates[k], gates[ring - k]])
        parts = [after(part, tie) for part in parts]
        total = run_experts(parts, gate)
        cut = [total[i * size : (i + 1) * size] for i in range(len(parts))]
        return cut[:2], cut[2:]

    total = run_experts(last, gates[far]).astype(jnp.bfloat16)
    fore, back = [along(total[:size], 1), None], [None, along(total[size:], -1)]
    ahead, behind = hop_experts(far - 1, total)
    tie = total
    for k in range(far - 1, 0, -1):
        if k > 1:
            coming = hop_experts(k - 1, tie)
        before = ()
        groups = [((fore, 1, ahead, h), (back, -1, behind, h)) for h in halves]
        if k == far - 1:
            groups = [((fore, 1, ahead, 1), (back, -1, behind, 0)), ((fore, 1, ahead, 0), (back, -1, behind, 1))]
        for group in groups:
            loads = []
            for way, step, totals, h in group:
                load = totals[h]
                if way[h] is not None:
                    load = load + after(way[h], *before).astype(jnp.float32)
                loads.append(load.astype(jnp.bfloat16))
            before = loads
            for (way, step, totals, h), load in zip(group, loads):
                way[h] = along(load, step)
        tie = loads[0]
        if k == 1:
            coming = hop_experts(0, tie)
            state = state_next(tie)
        ahead, behind = coming
    out = []
    for h in halves:
        total = ahead[h] + fore[h].astype(jnp.float32) + back[h].astype(jnp.float32)
        out.append((rows[h].astype(jnp.float32) + total).astype(jnp.bfloat16))
    return jnp.concatenate(out), state


def routed_experts(normed, out_proj, expert_in, expert_out, route_ids, route_weights):
    mixer_rows = jnp.dot(
        normed,
        lax.all_gather(out_proj, "narrow", axis=1, tiled=True),
        preferred_element_type=jnp.float32,
    ).astype(jnp.bfloat16)
    frames_here = mixer_rows.shape[0]
    model_width = mixer_rows.shape[1]
    topk_count = route_ids.shape[1]
    local_experts = expert_in.shape[0]
    devices = lax.axis_size(("wide", "narrow"))
    experts = local_experts * devices
    capacity = max(2, frames_here * topk_count * 5 // (4 * experts))
    flat_ids, positions = slot_positions(route_ids, experts)
    owners = jnp.arange(frames_here * topk_count, dtype=jnp.int32) // topk_count
    slot_table = (
        jnp.full((experts, capacity), frames_here, jnp.int32).at[flat_ids, positions].set(owners)
    )
    padded = jnp.concatenate([mixer_rows, jnp.zeros((1, model_width), jnp.bfloat16)], axis=0)
    outgoing = padded[slot_table]
    hidden_width = expert_out.shape[1]
    projected = jnp.einsum(
        "nlcd,ldf->nlcf",
        lax.all_to_all(
            outgoing.reshape(devices, local_experts, capacity, model_width),
            ("wide", "narrow"),
            split_axis=0,
            concat_axis=0,
            tiled=True,
        ),
        expert_in,
        preferred_element_type=jnp.float32,
    )
    hidden = (jax.nn.silu(projected[..., :hidden_width]) * projected[..., hidden_width:]).astype(
        jnp.bfloat16
    )
    returned = lax.all_to_all(
        jnp.einsum("nlcf,lfd->nlcd", hidden, expert_out, preferred_element_type=jnp.float32).astype(
            jnp.bfloat16
        ),
        ("wide", "narrow"),
        split_axis=0,
        concat_axis=0,
        tiled=True,
    )
    returned = returned.reshape(experts, capacity, model_width)
    picked = returned[flat_ids, positions].reshape(frames_here, topk_count, model_width)
    expert_sum = jnp.einsum("tk,tkd->td", route_weights, picked.astype(jnp.float32))
    layer_out = (mixer_rows.astype(jnp.float32) + expert_sum).astype(jnp.bfloat16)
    return layer_out


def solution(mesh):
    placed = (
        P(("groups", "wide", "narrow"), None),
        P(("groups", "wide", "narrow"), None),
        P(("groups", "wide", "narrow"), None),
        P(("groups", "wide", "narrow"), None),
        P(("groups", "wide", "narrow"), None),
        P(),
        P(),
        P(),
        P(),
        P(("groups", "wide", "narrow"), None, None, None),
        P(None, "narrow"),
        P(("wide", "narrow"), None, None),
        P(("wide", "narrow"), None, None),
        P(("groups", "wide", "narrow"), None),
        P(("groups", "wide", "narrow"), None),
    )
    return jax.shard_map(
        body,
        mesh=mesh,
        in_specs=placed,
        out_specs=(
            P(("groups", "wide", "narrow"), None),
            P(("groups", "wide", "narrow"), None, None, None),
        ),
        check_vma=False,
    )
```

```python
import functools

import jax
import jax.numpy as jnp
from jax import lax
from jax.experimental import pallas as pl
from jax.experimental.pallas import tpu as pltpu
from jax.sharding import PartitionSpec as P

epsilon = 1e-05


CHUNK = 8
NT = (((1,), (1,)), ((), ()))
TN = (((0,), (0,)), ((), ()))


def column_of(row_ref):
    count = row_ref.shape[1]
    i = lax.broadcasted_iota(jnp.int32, (count, count), 0)
    j = lax.broadcasted_iota(jnp.int32, (count, count), 1)
    return jnp.sum(jnp.where(i == j, row_ref[...], 0.0), axis=1, keepdims=True)


def decays(dt_ref, bias_ref, a_ref, step_ref, decay_ref):
    frames = dt_ref.shape[1]
    step_size = jax.nn.softplus(dt_ref[...] + column_of(bias_ref))
    rise = step_size * -jnp.exp(column_of(a_ref))
    s = lax.broadcasted_iota(jnp.int32, (frames, frames), 0)
    t = lax.broadcasted_iota(jnp.int32, (frames, frames), 1)
    upto = jnp.where(s <= t, 1.0, 0.0)
    step_ref[...] = step_size
    decay_ref[...] = jnp.dot(
        rise, upto, precision=lax.Precision.HIGHEST, preferred_element_type=jnp.float32
    )


def mixer_kernel(
    skip_ref,
    x_ref,
    z_ref,
    b_ref,
    c_ref,
    dt_ref,
    bias_ref,
    a_ref,
    gain_ref,
    state_ref,
    top_ref,
    bottom_ref,
    g_ref,
    ss_ref,
    step_ref,
    decay_ref,
):
    i = pl.program_id(0)
    frames, width = x_ref.shape
    head = width // CHUNK
    pl.when(i == 0)(lambda: decays(dt_ref, bias_ref, a_ref, step_ref, decay_ref))
    chunk = pl.ds(pl.multiple_of(i * CHUNK, CHUNK), CHUNK)
    step_size, decay = step_ref[chunk, :], decay_ref[chunk, :]
    decay_col = decay.T
    carry_col = jnp.exp(decay_col)
    t = lax.broadcasted_iota(jnp.int32, (frames, frames), 0)
    s = lax.broadcasted_iota(jnp.int32, (frames, frames), 1)
    c = c_ref[...]
    scores = lax.dot_general(c, b_ref[...], NT, preferred_element_type=jnp.float32)
    scores = jnp.where(s <= t, scores, 0.0)
    cc = jnp.concatenate([c, c], axis=1)
    left = lax.broadcasted_iota(jnp.int32, (frames, 2 * head), 1) < head
    squares = None
    for pair in range(CHUNK // 2):
        mixes = []
        for h in (2 * pair, 2 * pair + 1):
            spread = jnp.exp(jnp.minimum(decay_col[:, h : h + 1] - decay[h : h + 1, :], 0.0))
            mixes.append((spread * (scores * step_size[h : h + 1, :])).astype(jnp.bfloat16))
        at = slice(2 * head * pair, 2 * head * (pair + 1))
        x = x_ref[:, at]
        zero = jnp.zeros_like(x)
        y = jnp.dot(
            jnp.concatenate(mixes, axis=1),
            jnp.concatenate([jnp.where(left, x, zero), jnp.where(left, zero, x)], axis=0),
            preferred_element_type=jnp.float32,
        )
        state = state_ref[at, :]
        high = state.astype(jnp.bfloat16)
        low = (state - high.astype(jnp.float32)).astype(jnp.bfloat16)
        carried = lax.dot_general(
            cc, jnp.concatenate([high, low], axis=1), NT, preferred_element_type=jnp.float32
        )
        factor = jnp.where(
            left, carry_col[:, 2 * pair : 2 * pair + 1], carry_col[:, 2 * pair + 1 : 2 * pair + 2]
        )
        skip = jnp.where(left[:1], skip_ref[i * CHUNK + 2 * pair], skip_ref[i * CHUNK + 2 * pair + 1])
        mixed = y + factor * carried + skip * x.astype(jnp.float32)
        z = z_ref[:, at].astype(jnp.float32)
        g = mixed * jax.nn.silu(z)
        g_ref[i, :, at] = g
        squares = g * g if squares is None else squares + g * g

    @pl.when(i == 0)
    def _():
        ss_ref[...] = squares

    @pl.when(i > 0)
    def _():
        ss_ref[...] += squares

    steps = g_ref.shape[0]

    @pl.when(i == steps - 1)
    def _():
        mean = jnp.sum(ss_ref[...], axis=1, keepdims=True) / (steps * width)
        scale = lax.rsqrt(mean + epsilon)
        for j in range(steps):
            at = slice(j * width, (j + 1) * width)
            normed = (g_ref[j] * scale * gain_ref[:, at]).astype(jnp.bfloat16)
            top_ref[:, at] = normed[: frames // 2]
            bottom_ref[:, at] = normed[frames // 2 :]


def state_kernel(x_ref, b_ref, dt_ref, bias_ref, a_ref, state_ref, out_ref, step_ref, decay_ref):
    i = pl.program_id(0)
    frames, width = x_ref.shape
    head = width // CHUNK
    pl.when(i == 0)(lambda: decays(dt_ref, bias_ref, a_ref, step_ref, decay_ref))
    chunk = pl.ds(pl.multiple_of(i * CHUNK, CHUNK), CHUNK)
    step_size, decay = step_ref[chunk, :], decay_ref[chunk, :]
    end = decay[:, frames - 1 : frames]
    tail = (jnp.exp(end - decay) * step_size).T
    kept = jnp.exp(end)
    left = lax.broadcasted_iota(jnp.int32, (frames, 2 * head), 1) < head
    upper = lax.broadcasted_iota(jnp.int32, (2 * head, b_ref.shape[1]), 0) < head
    for pair in range(CHUNK // 2):
        at = slice(2 * head * pair, 2 * head * (pair + 1))
        factor = jnp.where(left, tail[:, 2 * pair : 2 * pair + 1], tail[:, 2 * pair + 1 : 2 * pair + 2])
        scaled = (x_ref[:, at].astype(jnp.float32) * factor).astype(jnp.bfloat16)
        added = lax.dot_general(scaled, b_ref[...], TN, preferred_element_type=jnp.float32)
        keep = jnp.where(upper, kept[2 * pair : 2 * pair + 1, :], kept[2 * pair + 1 : 2 * pair + 2, :])
        out_ref[at, :] = keep * state_ref[at, :] + added


def ssm_mixer(
    ssm_input, gate_input, b_proj, c_proj, dt_raw, a_log, dt_bias, d_skip, norm_gain, state_in
):
    frames, width = ssm_input.shape
    heads, head, inner = state_in.shape
    steps = heads // CHUNK
    part = width // steps
    state = state_in.reshape(width, inner)
    dt = dt_raw.T
    column = pl.BlockSpec((frames, part), lambda i: (0, i))
    whole = pl.BlockSpec((frames, inner), lambda i: (0, 0))
    per_head = pl.BlockSpec((heads, frames), lambda i: (0, 0))
    scalar = pl.BlockSpec((1, heads), lambda i: (0, 0))
    rows = pl.BlockSpec((part, inner), lambda i: (i, 0))
    full_row = pl.BlockSpec((1, width), lambda i: (0, 0))
    tables = [pltpu.VMEM((heads, frames), jnp.float32)] * 2
    normed = pl.pallas_call(
        mixer_kernel,
        grid=(steps,),
        in_specs=[
            pl.BlockSpec(memory_space=pltpu.SMEM),
            column,
            column,
            whole,
            whole,
            per_head,
            scalar,
            scalar,
            full_row,
            rows,
        ],
        out_specs=[pl.BlockSpec((frames // 2, width), lambda i: (0, 0))] * 2,
        out_shape=[jax.ShapeDtypeStruct((frames // 2, width), jnp.bfloat16)] * 2,
        scratch_shapes=[
            pltpu.VMEM((steps, frames, part), jnp.float32),
            pltpu.VMEM((frames, 2 * head), jnp.float32),
            *tables,
        ],
        compiler_params=pltpu.CompilerParams(vmem_limit_bytes=56 << 20),
        cost_estimate=pl.CostEstimate(flops=400_000_000, bytes_accessed=6_000_000, transcendentals=2_000_000),
        name="mixer",
    )(
        d_skip,
        ssm_input,
        gate_input,
        b_proj,
        c_proj,
        dt,
        dt_bias[None, :],
        a_log[None, :],
        norm_gain[None, :],
        state,
    )

    def state_next(ssm_input):
        out = pl.pallas_call(
            state_kernel,
            grid=(steps,),
            in_specs=[column, whole, per_head, scalar, scalar, rows],
            out_specs=rows,
            out_shape=jax.ShapeDtypeStruct((width, inner), jnp.float32),
            scratch_shapes=tables,
            compiler_params=pltpu.CompilerParams(vmem_limit_bytes=16 << 20),
            cost_estimate=pl.CostEstimate(flops=70_000_000, bytes_accessed=3_000_000, transcendentals=20_000),
            name="state",
        )(ssm_input, b_proj, dt, dt_bias[None, :], a_log[None, :], state)
        return out.reshape(heads, head, inner)

    return (normed, state_next)


def slot_positions(route_ids, experts):
    flat_ids = route_ids.reshape(-1)
    onehot = (flat_ids[:, None] == jnp.arange(experts, dtype=jnp.int32)[None, :]).astype(jnp.int32)
    earlier = jnp.cumsum(onehot, axis=0) - onehot
    return (flat_ids, jnp.sum(earlier * onehot, axis=1))


def body(
    ssm_input,
    gate_input,
    b_proj,
    c_proj,
    dt_raw,
    a_log,
    dt_bias,
    d_skip,
    norm_gain,
    state_in,
    out_proj,
    expert_in,
    expert_out,
    route_ids,
    route_weights,
):
    normed, state_next = ssm_mixer(
        ssm_input,
        gate_input,
        b_proj,
        c_proj,
        dt_raw,
        a_log,
        dt_bias,
        d_skip,
        norm_gain,
        state_in[0],
    )
    frames_here, topk_count = route_ids.shape
    local_experts = expert_in.shape[0]
    experts = local_experts * lax.axis_size(("wide", "narrow"))
    wide, narrow = lax.axis_size("wide"), lax.axis_size("narrow")
    if experts <= 4 * topk_count and narrow == 4 and wide & (wide - 1) == 0 and local_experts == 1:
        layer_out, state = dense_experts(
            normed,
            out_proj,
            expert_in[0],
            expert_out[0],
            route_ids,
            route_weights,
            lambda tie: state_next(after(ssm_input, tie)),
        )
    else:
        normed = jnp.concatenate(normed)
        layer_out = routed_experts(normed, out_proj, expert_in, expert_out, route_ids, route_weights)
        state = state_next(ssm_input)
    return (layer_out, state[None])


def routes(wide, move):
    pairs = []
    for z in range(wide):
        for x in range(2):
            for core in range(2):
                to = move(z, x, core)
                pairs.append(((z * 2 + x) * 2 + core, (to[0] * 2 + to[1]) * 2 + to[2]))
    return pairs


def after(value, *others):
    return lax.optimization_barrier((value, *others))[0]


def dense_experts(normed, out_proj, expert_in, expert_out, route_ids, route_weights, state_next):
    frames = route_ids.shape[0]
    wide = lax.axis_size("wide")
    ring = 2 * wide
    z = lax.axis_index("wide")
    x, core = lax.axis_index("narrow") // 2, lax.axis_index("narrow") % 2
    place = jnp.where(x == 0, z, ring - 1 - z)
    axes = ("wide", "narrow")

    def send(value, move):
        return lax.ppermute(value, axes, routes(wide, move))

    def to_core(value):
        return send(value, lambda z, x, c: (z, x, 1 - c))

    def to_x(value):
        return send(value, lambda z, x, c: (z, 1 - x, c))

    def along(value, step):
        def move(z, x, c):
            p = ((z if x == 0 else ring - 1 - z) + step) % ring
            return (p, 0, c) if p < wide else (ring - 1 - p, 1, c)

        return send(value, move)

    out_other, in_other, down_other = to_core(out_proj), to_core(expert_in), to_core(expert_out)

    experts = wide * 4
    gates = jnp.sum(
        jnp.where(route_ids[:, :, None] == jnp.arange(experts), route_weights[:, :, None], 0.0), axis=1
    )
    normed_top, normed_bottom, other = lax.optimization_barrier((*normed, to_x(gates)))
    gates = jnp.where(x == 0, jnp.stack([gates, other]), jnp.stack([other, gates]))[:, None]

    halves = range(2)
    size = frames // 2
    hidden_width = expert_out.shape[0]
    columns = lax.optimization_barrier(
        jnp.where(
            core == 0,
            jnp.concatenate([out_proj, out_other], axis=1),
            jnp.concatenate([out_other, out_proj], axis=1),
        )
    )
    sent = [to_x(normed_top), to_x(after(normed_bottom, columns))]

    def project(rows):
        return jnp.dot(rows, columns, preferred_element_type=jnp.float32).astype(jnp.bfloat16)

    own = [project(normed_top), project(normed_bottom)]

    def merge(gates, other, low):
        return jnp.where(
            low, jnp.concatenate([gates, other], axis=1), jnp.concatenate([other, gates], axis=1)
        )

    rows, peer = [], None
    for h in halves:
        arrived = sent[h]
        if peer is not None:
            arrived = after(arrived, peer)
        peer = project(arrived)
        back = to_x(peer)
        rows.append(
            jnp.where(
                x == 0,
                jnp.concatenate([own[h], back], axis=1),
                jnp.concatenate([back, own[h]], axis=1),
            )
        )

    far = ring // 2
    fore_at, back_at = {0: rows}, {0: rows}
    gates, step = after(gates, sent[1]), 1
    for k in range(1, far):
        if step < wide:
            other = send(gates, lambda z, x, c: (z ^ step, x, c))
        fore_at[k] = [along(fore_at[k - 1][h], 1) for h in halves]
        back_at[k] = [along(back_at[k - 1][h], -1) for h in halves]
        if step < wide:
            other, back_at[k][1] = lax.optimization_barrier((other, back_at[k][1]))
            gates, step = merge(gates, other, z & step == 0), 2 * step
    while step < wide:
        other = send(gates, lambda z, x, c: (z ^ step, x, c))
        gates, step = merge(gates, other, z & step == 0), 2 * step
    mine = (z * 2 + x) * 2 + core
    pair = jnp.stack([mine, mine + 1 - 2 * core])
    gates = jnp.sum(
        jnp.where(pair[:, None] == jnp.arange(experts), gates[..., None, :], 0.0), axis=-1
    )
    gates = jnp.concatenate([gates[0], gates[1, ::-1]])
    gates = lax.dynamic_slice_in_dim(jnp.concatenate([gates, gates]), place, ring, 0)
    last = [along(fore_at[far - 1][0], 1), along(back_at[far - 1][1], -1)]

    joined_in = jnp.concatenate(
        [
            expert_in[:, :hidden_width],
            in_other[:, :hidden_width],
            expert_in[:, hidden_width:],
            in_other[:, hidden_width:],
        ],
        axis=1,
    )
    joined_down = jnp.concatenate([expert_out, down_other], axis=0)
    joined_in, joined_down = lax.optimization_barrier((joined_in, joined_down))
    is_first = jnp.arange(2 * hidden_width)[None, :] < hidden_width

    def run_experts(parts, gate):
        v = jnp.dot(jnp.concatenate(parts), joined_in, preferred_element_type=jnp.float32)
        hidden = jax.nn.silu(v[:, : 2 * hidden_width]) * v[:, 2 * hidden_width :]
        hidden = (hidden * jnp.where(is_first, gate[:, :1], gate[:, 1:])).astype(jnp.bfloat16)
        return jnp.dot(hidden, joined_down, preferred_element_type=jnp.float32)

    def hop_experts(k, tie):
        parts = rows if k == 0 else [*back_at[k], *fore_at[k]]
        gate = gates[0] if k == 0 else jnp.concatenate([gates[k], gates[ring - k]])
        parts = [after(part, tie) for part in parts]
        total = run_experts(parts, gate)
        cut = [total[i * size : (i + 1) * size] for i in range(len(parts))]
        return cut[:2], cut[2:]

    total = run_experts(last, gates[far]).astype(jnp.bfloat16)
    fore, back = [along(total[:size], 1), None], [None, along(total[size:], -1)]
    ahead, behind = hop_experts(far - 1, total)
    groups = [((fore, 1, 1), (back, -1, 0)), ((fore, 1, 0), (back, -1, 1))]
    for k in range(far - 1, 0, -1):
        before = ()
        for group in groups:
            loads = []
            for way, step, h in group:
                load = (ahead if step > 0 else behind)[h]
                if way[h] is not None:
                    load = load + after(way[h], *before).astype(jnp.float32)
                loads.append(load.astype(jnp.bfloat16))
            for (way, step, h), load in zip(group, loads):
                way[h] = along(load, step)
            if not before:
                coming = hop_experts(k - 1, loads[0])
                before = (*loads, *coming[0], *coming[1])
                if k == 1:
                    state = state_next(loads[0])
                    before += (state,)
        ahead, behind = coming
    out = []
    for h in halves:
        total = ahead[h] + fore[h].astype(jnp.float32) + back[h].astype(jnp.float32)
        out.append((rows[h].astype(jnp.float32) + total).astype(jnp.bfloat16))
    return jnp.concatenate(out), state


def routed_experts(normed, out_proj, expert_in, expert_out, route_ids, route_weights):
    mixer_rows = jnp.dot(
        normed,
        lax.all_gather(out_proj, "narrow", axis=1, tiled=True),
        preferred_element_type=jnp.float32,
    ).astype(jnp.bfloat16)
    frames_here = mixer_rows.shape[0]
    model_width = mixer_rows.shape[1]
    topk_count = route_ids.shape[1]
    local_experts = expert_in.shape[0]
    devices = lax.axis_size(("wide", "narrow"))
    experts = local_experts * devices
    capacity = max(2, frames_here * topk_count * 5 // (4 * experts))
    flat_ids, positions = slot_positions(route_ids, experts)
    owners = jnp.arange(frames_here * topk_count, dtype=jnp.int32) // topk_count
    slot_table = (
        jnp.full((experts, capacity), frames_here, jnp.int32).at[flat_ids, positions].set(owners)
    )
    padded = jnp.concatenate([mixer_rows, jnp.zeros((1, model_width), jnp.bfloat16)], axis=0)
    outgoing = padded[slot_table]
    hidden_width = expert_out.shape[1]
    projected = jnp.einsum(
        "nlcd,ldf->nlcf",
        lax.all_to_all(
            outgoing.reshape(devices, local_experts, capacity, model_width),
            ("wide", "narrow"),
            split_axis=0,
            concat_axis=0,
            tiled=True,
        ),
        expert_in,
        preferred_element_type=jnp.float32,
    )
    hidden = (jax.nn.silu(projected[..., :hidden_width]) * projected[..., hidden_width:]).astype(
        jnp.bfloat16
    )
    returned = lax.all_to_all(
        jnp.einsum("nlcf,lfd->nlcd", hidden, expert_out, preferred_element_type=jnp.float32).astype(
            jnp.bfloat16
        ),
        ("wide", "narrow"),
        split_axis=0,
        concat_axis=0,
        tiled=True,
    )
    returned = returned.reshape(experts, capacity, model_width)
    picked = returned[flat_ids, positions].reshape(frames_here, topk_count, model_width)
    expert_sum = jnp.einsum("tk,tkd->td", route_weights, picked.astype(jnp.float32))
    layer_out = (mixer_rows.astype(jnp.float32) + expert_sum).astype(jnp.bfloat16)
    return layer_out


def solution(mesh):
    placed = (
        P(("groups", "wide", "narrow"), None),
        P(("groups", "wide", "narrow"), None),
        P(("groups", "wide", "narrow"), None),
        P(("groups", "wide", "narrow"), None),
        P(("groups", "wide", "narrow"), None),
        P(),
        P(),
        P(),
        P(),
        P(("groups", "wide", "narrow"), None, None, None),
        P(None, "narrow"),
        P(("wide", "narrow"), None, None),
        P(("wide", "narrow"), None, None),
        P(("groups", "wide", "narrow"), None),
        P(("groups", "wide", "narrow"), None),
    )
    return jax.shard_map(
        body,
        mesh=mesh,
        in_specs=placed,
        out_specs=(
            P(("groups", "wide", "narrow"), None),
            P(("groups", "wide", "narrow"), None, None, None),
        ),
        check_vma=False,
    )
```

```python
import functools

import jax
import jax.numpy as jnp
from jax import lax
from jax.experimental import pallas as pl
from jax.experimental.pallas import tpu as pltpu
from jax.sharding import PartitionSpec as P

epsilon = 1e-05


CHUNK = 8
NT = (((1,), (1,)), ((), ()))
TN = (((0,), (0,)), ((), ()))


def column_of(row_ref):
    count = row_ref.shape[1]
    i = lax.broadcasted_iota(jnp.int32, (count, count), 0)
    j = lax.broadcasted_iota(jnp.int32, (count, count), 1)
    return jnp.sum(jnp.where(i == j, row_ref[...], 0.0), axis=1, keepdims=True)


def decays(dt_ref, bias_ref, a_ref, step_ref, decay_ref):
    frames = dt_ref.shape[1]
    step_size = jax.nn.softplus(dt_ref[...] + column_of(bias_ref))
    rise = step_size * -jnp.exp(column_of(a_ref))
    s = lax.broadcasted_iota(jnp.int32, (frames, frames), 0)
    t = lax.broadcasted_iota(jnp.int32, (frames, frames), 1)
    upto = jnp.where(s <= t, 1.0, 0.0)
    step_ref[...] = step_size
    decay_ref[...] = jnp.dot(
        rise, upto, precision=lax.Precision.HIGHEST, preferred_element_type=jnp.float32
    )


def mixer_kernel(
    skip_ref,
    x_ref,
    z_ref,
    b_ref,
    c_ref,
    dt_ref,
    bias_ref,
    a_ref,
    gain_ref,
    state_ref,
    top_ref,
    bottom_ref,
    g_ref,
    ss_ref,
    step_ref,
    decay_ref,
):
    i = pl.program_id(0)
    frames, width = x_ref.shape
    head = width // CHUNK
    pl.when(i == 0)(lambda: decays(dt_ref, bias_ref, a_ref, step_ref, decay_ref))
    chunk = pl.ds(pl.multiple_of(i * CHUNK, CHUNK), CHUNK)
    step_size, decay = step_ref[chunk, :], decay_ref[chunk, :]
    decay_col = decay.T
    carry_col = jnp.exp(decay_col)
    t = lax.broadcasted_iota(jnp.int32, (frames, frames), 0)
    s = lax.broadcasted_iota(jnp.int32, (frames, frames), 1)
    c = c_ref[...]
    scores = lax.dot_general(c, b_ref[...], NT, preferred_element_type=jnp.float32)
    scores = jnp.where(s <= t, scores, 0.0)
    cc = jnp.concatenate([c, c], axis=1)
    left = lax.broadcasted_iota(jnp.int32, (frames, 2 * head), 1) < head
    squares = None
    for pair in range(CHUNK // 2):
        mixes = []
        for h in (2 * pair, 2 * pair + 1):
            spread = jnp.exp(jnp.minimum(decay_col[:, h : h + 1] - decay[h : h + 1, :], 0.0))
            mixes.append((spread * (scores * step_size[h : h + 1, :])).astype(jnp.bfloat16))
        at = slice(2 * head * pair, 2 * head * (pair + 1))
        x = x_ref[:, at]
        zero = jnp.zeros_like(x)
        y = jnp.dot(
            jnp.concatenate(mixes, axis=1),
            jnp.concatenate([jnp.where(left, x, zero), jnp.where(left, zero, x)], axis=0),
            preferred_element_type=jnp.float32,
        )
        state = state_ref[at, :]
        high = state.astype(jnp.bfloat16)
        low = (state - high.astype(jnp.float32)).astype(jnp.bfloat16)
        carried = lax.dot_general(
            cc, jnp.concatenate([high, low], axis=1), NT, preferred_element_type=jnp.float32
        )
        factor = jnp.where(
            left, carry_col[:, 2 * pair : 2 * pair + 1], carry_col[:, 2 * pair + 1 : 2 * pair + 2]
        )
        skip = jnp.where(left[:1], skip_ref[i * CHUNK + 2 * pair], skip_ref[i * CHUNK + 2 * pair + 1])
        mixed = y + factor * carried + skip * x.astype(jnp.float32)
        z = z_ref[:, at].astype(jnp.float32)
        g = mixed * jax.nn.silu(z)
        g_ref[i, :, at] = g
        squares = g * g if squares is None else squares + g * g

    @pl.when(i == 0)
    def _():
        ss_ref[...] = squares

    @pl.when(i > 0)
    def _():
        ss_ref[...] += squares

    steps = g_ref.shape[0]

    @pl.when(i == steps - 1)
    def _():
        mean = jnp.sum(ss_ref[...], axis=1, keepdims=True) / (steps * width)
        scale = lax.rsqrt(mean + epsilon)
        for j in range(steps):
            at = slice(j * width, (j + 1) * width)
            normed = (g_ref[j] * scale * gain_ref[:, at]).astype(jnp.bfloat16)
            top_ref[:, at] = normed[: frames // 2]
            bottom_ref[:, at] = normed[frames // 2 :]


def state_kernel(x_ref, b_ref, dt_ref, bias_ref, a_ref, state_ref, out_ref, step_ref, decay_ref):
    i = pl.program_id(0)
    frames, width = x_ref.shape
    head = width // CHUNK
    pl.when(i == 0)(lambda: decays(dt_ref, bias_ref, a_ref, step_ref, decay_ref))
    chunk = pl.ds(pl.multiple_of(i * CHUNK, CHUNK), CHUNK)
    step_size, decay = step_ref[chunk, :], decay_ref[chunk, :]
    end = decay[:, frames - 1 : frames]
    tail = (jnp.exp(end - decay) * step_size).T
    kept = jnp.exp(end)
    left = lax.broadcasted_iota(jnp.int32, (frames, 2 * head), 1) < head
    upper = lax.broadcasted_iota(jnp.int32, (2 * head, b_ref.shape[1]), 0) < head
    for pair in range(CHUNK // 2):
        at = slice(2 * head * pair, 2 * head * (pair + 1))
        factor = jnp.where(left, tail[:, 2 * pair : 2 * pair + 1], tail[:, 2 * pair + 1 : 2 * pair + 2])
        scaled = (x_ref[:, at].astype(jnp.float32) * factor).astype(jnp.bfloat16)
        added = lax.dot_general(scaled, b_ref[...], TN, preferred_element_type=jnp.float32)
        keep = jnp.where(upper, kept[2 * pair : 2 * pair + 1, :], kept[2 * pair + 1 : 2 * pair + 2, :])
        out_ref[at, :] = keep * state_ref[at, :] + added


def ssm_mixer(
    ssm_input, gate_input, b_proj, c_proj, dt_raw, a_log, dt_bias, d_skip, norm_gain, state_in
):
    frames, width = ssm_input.shape
    heads, head, inner = state_in.shape
    steps = heads // CHUNK
    part = width // steps
    state = state_in.reshape(width, inner)
    dt = dt_raw.T
    column = pl.BlockSpec((frames, part), lambda i: (0, i))
    whole = pl.BlockSpec((frames, inner), lambda i: (0, 0))
    per_head = pl.BlockSpec((heads, frames), lambda i: (0, 0))
    scalar = pl.BlockSpec((1, heads), lambda i: (0, 0))
    rows = pl.BlockSpec((part, inner), lambda i: (i, 0))
    full_row = pl.BlockSpec((1, width), lambda i: (0, 0))
    tables = [pltpu.VMEM((heads, frames), jnp.float32)] * 2
    normed = pl.pallas_call(
        mixer_kernel,
        grid=(steps,),
        in_specs=[
            pl.BlockSpec(memory_space=pltpu.SMEM),
            column,
            column,
            whole,
            whole,
            per_head,
            scalar,
            scalar,
            full_row,
            rows,
        ],
        out_specs=[pl.BlockSpec((frames // 2, width), lambda i: (0, 0))] * 2,
        out_shape=[jax.ShapeDtypeStruct((frames // 2, width), jnp.bfloat16)] * 2,
        scratch_shapes=[
            pltpu.VMEM((steps, frames, part), jnp.float32),
            pltpu.VMEM((frames, 2 * head), jnp.float32),
            *tables,
        ],
        compiler_params=pltpu.CompilerParams(vmem_limit_bytes=56 << 20),
        cost_estimate=pl.CostEstimate(flops=400_000_000, bytes_accessed=6_000_000, transcendentals=2_000_000),
        name="mixer",
    )(
        d_skip,
        ssm_input,
        gate_input,
        b_proj,
        c_proj,
        dt,
        dt_bias[None, :],
        a_log[None, :],
        norm_gain[None, :],
        state,
    )

    def state_next(ssm_input):
        out = pl.pallas_call(
            state_kernel,
            grid=(steps,),
            in_specs=[column, whole, per_head, scalar, scalar, rows],
            out_specs=rows,
            out_shape=jax.ShapeDtypeStruct((width, inner), jnp.float32),
            scratch_shapes=tables,
            compiler_params=pltpu.CompilerParams(vmem_limit_bytes=16 << 20),
            cost_estimate=pl.CostEstimate(flops=70_000_000, bytes_accessed=3_000_000, transcendentals=20_000),
            name="state",
        )(ssm_input, b_proj, dt, dt_bias[None, :], a_log[None, :], state)
        return out.reshape(heads, head, inner)

    return (normed, state_next)


def slot_positions(route_ids, experts):
    flat_ids = route_ids.reshape(-1)
    onehot = (flat_ids[:, None] == jnp.arange(experts, dtype=jnp.int32)[None, :]).astype(jnp.int32)
    earlier = jnp.cumsum(onehot, axis=0) - onehot
    return (flat_ids, jnp.sum(earlier * onehot, axis=1))


def body(
    ssm_input,
    gate_input,
    b_proj,
    c_proj,
    dt_raw,
    a_log,
    dt_bias,
    d_skip,
    norm_gain,
    state_in,
    out_proj,
    expert_in,
    expert_out,
    route_ids,
    route_weights,
):
    normed, state_next = ssm_mixer(
        ssm_input,
        gate_input,
        b_proj,
        c_proj,
        dt_raw,
        a_log,
        dt_bias,
        d_skip,
        norm_gain,
        state_in[0],
    )
    frames_here, topk_count = route_ids.shape
    local_experts = expert_in.shape[0]
    experts = local_experts * lax.axis_size(("wide", "narrow"))
    wide, narrow = lax.axis_size("wide"), lax.axis_size("narrow")
    if experts <= 4 * topk_count and narrow == 4 and wide & (wide - 1) == 0 and local_experts == 1:
        layer_out, state = dense_experts(
            normed,
            out_proj,
            expert_in[0],
            expert_out[0],
            route_ids,
            route_weights,
            functools.partial(state_next, ssm_input),
        )
    else:
        normed = jnp.concatenate(normed)
        layer_out = routed_experts(normed, out_proj, expert_in, expert_out, route_ids, route_weights)
        state = state_next(ssm_input)
    return (layer_out, state[None])


def routes(wide, move):
    pairs = []
    for z in range(wide):
        for x in range(2):
            for core in range(2):
                to = move(z, x, core)
                pairs.append(((z * 2 + x) * 2 + core, (to[0] * 2 + to[1]) * 2 + to[2]))
    return pairs


def after(value, *others):
    return lax.optimization_barrier((value, *others))[0]


def dense_experts(normed, out_proj, expert_in, expert_out, route_ids, route_weights, state_next):
    frames = route_ids.shape[0]
    wide = lax.axis_size("wide")
    ring = 2 * wide
    z = lax.axis_index("wide")
    x, core = lax.axis_index("narrow") // 2, lax.axis_index("narrow") % 2
    place = jnp.where(x == 0, z, ring - 1 - z)
    axes = ("wide", "narrow")

    def send(value, move):
        return lax.ppermute(value, axes, routes(wide, move))

    def to_core(value):
        return send(value, lambda z, x, c: (z, x, 1 - c))

    def to_x(value):
        return send(value, lambda z, x, c: (z, 1 - x, c))

    def along(value, step):
        def move(z, x, c):
            p = ((z if x == 0 else ring - 1 - z) + step) % ring
            return (p, 0, c) if p < wide else (ring - 1 - p, 1, c)

        return send(value, move)

    out_other, in_other, down_other = to_core(out_proj), to_core(expert_in), to_core(expert_out)

    experts = wide * 4
    gates = jnp.sum(
        jnp.where(route_ids[:, :, None] == jnp.arange(experts), route_weights[:, :, None], 0.0), axis=1
    )
    high = gates.astype(jnp.bfloat16)
    low = (gates - high.astype(jnp.float32)).astype(jnp.bfloat16)
    lanes = -(-2 * experts // 128) * 128
    spare = jnp.zeros((frames, lanes - 2 * experts), jnp.bfloat16)
    gates = jnp.concatenate([high, low, spare], axis=1)
    normed_top, normed_bottom = normed

    halves = range(2)
    size = frames // 2
    hidden_width = expert_out.shape[0]
    columns = lax.optimization_barrier(
        jnp.where(
            core == 0,
            jnp.concatenate([out_proj, out_other], axis=1),
            jnp.concatenate([out_other, out_proj], axis=1),
        )
    )
    sent = [to_x(normed_top), to_x(after(normed_bottom, columns))]

    def project(rows):
        return jnp.dot(rows, columns, preferred_element_type=jnp.float32).astype(jnp.bfloat16)

    own = [project(normed_top), project(normed_bottom)]
    rows, peer = [], None
    for h in halves:
        arrived = sent[h]
        if peer is not None:
            arrived, state = lax.optimization_barrier((arrived, state_next()))
        peer = project(arrived)
        back = to_x(peer)
        gate = gates[h * size : (h + 1) * size]
        rows.append(
            jnp.where(
                x == 0,
                jnp.concatenate([own[h], back, gate], axis=1),
                jnp.concatenate([back, own[h], gate], axis=1),
            )
        )

    far = ring // 2
    fore_at, back_at = {0: rows}, {0: rows}
    for k in range(1, far):
        fore_at[k] = [along(fore_at[k - 1][h], 1) for h in halves]
        back_at[k] = [along(back_at[k - 1][h], -1) for h in halves]
    last = [along(fore_at[far - 1][0], 1), along(back_at[far - 1][1], -1)]

    joined_in = jnp.concatenate(
        [
            expert_in[:, :hidden_width],
            in_other[:, :hidden_width],
            expert_in[:, hidden_width:],
            in_other[:, hidden_width:],
        ],
        axis=1,
    )
    depth = expert_in.shape[0]
    joined_in = jnp.pad(joined_in, ((0, lanes), (0, 0)))
    joined_down = jnp.concatenate([expert_out, down_other], axis=0)
    joined_in, joined_down = lax.optimization_barrier((joined_in, joined_down))
    is_first = jnp.arange(2 * hidden_width)[None, :] < hidden_width

    mine = (z * 2 + x) * 2 + core
    lane = jnp.arange(2 * experts)[None, :] % experts
    choose = [lane == mine, lane == mine + 1 - 2 * core]

    def run_experts(parts):
        parts = jnp.concatenate(parts)
        v = jnp.dot(parts, joined_in, preferred_element_type=jnp.float32)
        gate = parts[:, depth : depth + 2 * experts].astype(jnp.float32)
        gate = [jnp.sum(jnp.where(test, gate, 0.0), axis=1, keepdims=True) for test in choose]
        hidden = jax.nn.silu(v[:, : 2 * hidden_width]) * v[:, 2 * hidden_width :]
        hidden = (hidden * jnp.where(is_first, gate[0], gate[1])).astype(jnp.bfloat16)
        return jnp.dot(hidden, joined_down, preferred_element_type=jnp.float32)

    def hop_experts(k, tie):
        parts = rows if k == 0 else [*back_at[k], *fore_at[k]]
        total = run_experts([after(part, tie) for part in parts])
        if k == 0:
            return total, ()
        cut = [total[i * size : (i + 1) * size] for i in range(len(parts))]
        return cut[:2], cut[2:]

    total = run_experts(last).astype(jnp.bfloat16)
    fore, back = [along(total[:size], 1), None], [None, along(total[size:], -1)]
    ahead, behind = hop_experts(far - 1, total)
    groups = [((fore, 1, 1), (back, -1, 0)), ((fore, 1, 0), (back, -1, 1))]
    for k in range(far - 1, 0, -1):
        before = ()
        for group in groups:
            loads = []
            for way, step, h in group:
                load = (ahead if step > 0 else behind)[h]
                if way[h] is not None:
                    load = load + after(way[h], *before).astype(jnp.float32)
                loads.append(load.astype(jnp.bfloat16))
            for (way, step, h), load in zip(group, loads):
                way[h] = along(load, step)
            if not before:
                before = tuple(loads)
                if k < far - 1:
                    coming = hop_experts(k - 1, loads[0])
                    before += (*coming[0], *coming[1]) if k > 1 else (coming[0],)
            elif k == far - 1:
                coming = hop_experts(k - 1, loads[0])
        ahead, behind = coming
    total = ahead + jnp.concatenate(fore).astype(jnp.float32) + jnp.concatenate(back).astype(jnp.float32)
    mixer_rows = jnp.concatenate([row[:, :depth] for row in rows]).astype(jnp.float32)
    return (mixer_rows + total).astype(jnp.bfloat16), state


def routed_experts(normed, out_proj, expert_in, expert_out, route_ids, route_weights):
    mixer_rows = jnp.dot(
        normed,
        lax.all_gather(out_proj, "narrow", axis=1, tiled=True),
        preferred_element_type=jnp.float32,
    ).astype(jnp.bfloat16)
    frames_here = mixer_rows.shape[0]
    model_width = mixer_rows.shape[1]
    topk_count = route_ids.shape[1]
    local_experts = expert_in.shape[0]
    devices = lax.axis_size(("wide", "narrow"))
    experts = local_experts * devices
    capacity = max(2, frames_here * topk_count * 5 // (4 * experts))
    flat_ids, positions = slot_positions(route_ids, experts)
    owners = jnp.arange(frames_here * topk_count, dtype=jnp.int32) // topk_count
    slot_table = (
        jnp.full((experts, capacity), frames_here, jnp.int32).at[flat_ids, positions].set(owners)
    )
    padded = jnp.concatenate([mixer_rows, jnp.zeros((1, model_width), jnp.bfloat16)], axis=0)
    outgoing = padded[slot_table]
    hidden_width = expert_out.shape[1]
    projected = jnp.einsum(
        "nlcd,ldf->nlcf",
        lax.all_to_all(
            outgoing.reshape(devices, local_experts, capacity, model_width),
            ("wide", "narrow"),
            split_axis=0,
            concat_axis=0,
            tiled=True,
        ),
        expert_in,
        preferred_element_type=jnp.float32,
    )
    hidden = (jax.nn.silu(projected[..., :hidden_width]) * projected[..., hidden_width:]).astype(
        jnp.bfloat16
    )
    returned = lax.all_to_all(
        jnp.einsum("nlcf,lfd->nlcd", hidden, expert_out, preferred_element_type=jnp.float32).astype(
            jnp.bfloat16
        ),
        ("wide", "narrow"),
        split_axis=0,
        concat_axis=0,
        tiled=True,
    )
    returned = returned.reshape(experts, capacity, model_width)
    picked = returned[flat_ids, positions].reshape(frames_here, topk_count, model_width)
    expert_sum = jnp.einsum("tk,tkd->td", route_weights, picked.astype(jnp.float32))
    layer_out = (mixer_rows.astype(jnp.float32) + expert_sum).astype(jnp.bfloat16)
    return layer_out


def solution(mesh):
    placed = (
        P(("groups", "wide", "narrow"), None),
        P(("groups", "wide", "narrow"), None),
        P(("groups", "wide", "narrow"), None),
        P(("groups", "wide", "narrow"), None),
        P(("groups", "wide", "narrow"), None),
        P(),
        P(),
        P(),
        P(),
        P(("groups", "wide", "narrow"), None, None, None),
        P(None, "narrow"),
        P(("wide", "narrow"), None, None),
        P(("wide", "narrow"), None, None),
        P(("groups", "wide", "narrow"), None),
        P(("groups", "wide", "narrow"), None),
    )
    return jax.shard_map(
        body,
        mesh=mesh,
        in_specs=placed,
        out_specs=(
            P(("groups", "wide", "narrow"), None),
            P(("groups", "wide", "narrow"), None, None, None),
        ),
        check_vma=False,
    )
```

```python
import functools

import jax
import jax.numpy as jnp
from jax import lax
from jax.experimental import pallas as pl
from jax.experimental.pallas import tpu as pltpu
from jax.sharding import PartitionSpec as P

epsilon = 1e-05


CHUNK = 8
NT = (((1,), (1,)), ((), ()))
TN = (((0,), (0,)), ((), ()))


def column_of(row_ref):
    count = row_ref.shape[1]
    i = lax.broadcasted_iota(jnp.int32, (count, count), 0)
    j = lax.broadcasted_iota(jnp.int32, (count, count), 1)
    return jnp.sum(jnp.where(i == j, row_ref[...], 0.0), axis=1, keepdims=True)


def decays(dt_ref, bias_ref, a_ref, step_ref, decay_ref):
    frames = dt_ref.shape[1]
    step_size = jax.nn.softplus(dt_ref[...] + column_of(bias_ref))
    rise = step_size * -jnp.exp(column_of(a_ref))
    s = lax.broadcasted_iota(jnp.int32, (frames, frames), 0)
    t = lax.broadcasted_iota(jnp.int32, (frames, frames), 1)
    upto = jnp.where(s <= t, 1.0, 0.0)
    step_ref[...] = step_size
    decay_ref[...] = jnp.dot(
        rise, upto, precision=lax.Precision.HIGHEST, preferred_element_type=jnp.float32
    )


def mixer_kernel(
    skip_ref,
    x_ref,
    z_ref,
    b_ref,
    c_ref,
    dt_ref,
    bias_ref,
    a_ref,
    gain_ref,
    state_ref,
    top_ref,
    bottom_ref,
    next_ref,
    g_ref,
    ss_ref,
    step_ref,
    decay_ref,
):
    i = pl.program_id(0)
    frames, width = x_ref.shape
    head = width // CHUNK
    pl.when(i == 0)(lambda: decays(dt_ref, bias_ref, a_ref, step_ref, decay_ref))
    chunk = pl.ds(pl.multiple_of(i * CHUNK, CHUNK), CHUNK)
    step_size, decay = step_ref[chunk, :], decay_ref[chunk, :]
    decay_col = decay.T
    carry_col = jnp.exp(decay_col)
    end = decay[:, frames - 1 : frames]
    tail = (jnp.exp(end - decay) * step_size).T
    kept = jnp.exp(end)
    b = b_ref[...]
    upper = lax.broadcasted_iota(jnp.int32, (2 * head, b.shape[1]), 0) < head
    t = lax.broadcasted_iota(jnp.int32, (frames, frames), 0)
    s = lax.broadcasted_iota(jnp.int32, (frames, frames), 1)
    c = c_ref[...]
    scores = lax.dot_general(c, b, NT, preferred_element_type=jnp.float32)
    scores = jnp.where(s <= t, scores, 0.0)
    cc = jnp.concatenate([c, c], axis=1)
    left = lax.broadcasted_iota(jnp.int32, (frames, 2 * head), 1) < head
    squares = None
    for pair in range(CHUNK // 2):
        mixes = []
        for h in (2 * pair, 2 * pair + 1):
            spread = jnp.exp(jnp.minimum(decay_col[:, h : h + 1] - decay[h : h + 1, :], 0.0))
            mixes.append((spread * (scores * step_size[h : h + 1, :])).astype(jnp.bfloat16))
        at = slice(2 * head * pair, 2 * head * (pair + 1))
        x = x_ref[:, at]
        zero = jnp.zeros_like(x)
        y = jnp.dot(
            jnp.concatenate(mixes, axis=1),
            jnp.concatenate([jnp.where(left, x, zero), jnp.where(left, zero, x)], axis=0),
            preferred_element_type=jnp.float32,
        )
        state = state_ref[at, :]
        high = state.astype(jnp.bfloat16)
        low = (state - high.astype(jnp.float32)).astype(jnp.bfloat16)
        carried = lax.dot_general(
            cc, jnp.concatenate([high, low], axis=1), NT, preferred_element_type=jnp.float32
        )
        factor = jnp.where(
            left, carry_col[:, 2 * pair : 2 * pair + 1], carry_col[:, 2 * pair + 1 : 2 * pair + 2]
        )
        skip = jnp.where(left[:1], skip_ref[i * CHUNK + 2 * pair], skip_ref[i * CHUNK + 2 * pair + 1])
        mixed = y + factor * carried + skip * x.astype(jnp.float32)
        z = z_ref[:, at].astype(jnp.float32)
        g = mixed * jax.nn.silu(z)
        g_ref[i, :, at] = g
        factor = jnp.where(left, tail[:, 2 * pair : 2 * pair + 1], tail[:, 2 * pair + 1 : 2 * pair + 2])
        scaled = (x.astype(jnp.float32) * factor).astype(jnp.bfloat16)
        added = lax.dot_general(scaled, b, TN, preferred_element_type=jnp.float32)
        keep = jnp.where(upper, kept[2 * pair : 2 * pair + 1, :], kept[2 * pair + 1 : 2 * pair + 2, :])
        next_ref[at, :] = keep * state + added
        squares = g * g if squares is None else squares + g * g

    @pl.when(i == 0)
    def _():
        ss_ref[...] = squares

    @pl.when(i > 0)
    def _():
        ss_ref[...] += squares

    steps = g_ref.shape[0]

    @pl.when(i == steps - 1)
    def _():
        mean = jnp.sum(ss_ref[...], axis=1, keepdims=True) / (steps * width)
        scale = lax.rsqrt(mean + epsilon)
        for j in range(steps):
            at = slice(j * width, (j + 1) * width)
            normed = (g_ref[j] * scale * gain_ref[:, at]).astype(jnp.bfloat16)
            top_ref[:, at] = normed[: frames // 2]
            bottom_ref[:, at] = normed[frames // 2 :]


def ssm_mixer(
    ssm_input, gate_input, b_proj, c_proj, dt_raw, a_log, dt_bias, d_skip, norm_gain, state_in
):
    frames, width = ssm_input.shape
    heads, head, inner = state_in.shape
    steps = heads // CHUNK
    part = width // steps
    state = state_in.reshape(width, inner)
    dt = dt_raw.T
    column = pl.BlockSpec((frames, part), lambda i: (0, i))
    whole = pl.BlockSpec((frames, inner), lambda i: (0, 0))
    per_head = pl.BlockSpec((heads, frames), lambda i: (0, 0))
    scalar = pl.BlockSpec((1, heads), lambda i: (0, 0))
    rows = pl.BlockSpec((part, inner), lambda i: (i, 0))
    full_row = pl.BlockSpec((1, width), lambda i: (0, 0))
    tables = [pltpu.VMEM((heads, frames), jnp.float32)] * 2
    top, bottom, state = pl.pallas_call(
        mixer_kernel,
        grid=(steps,),
        in_specs=[
            pl.BlockSpec(memory_space=pltpu.SMEM),
            column,
            column,
            whole,
            whole,
            per_head,
            scalar,
            scalar,
            full_row,
            rows,
        ],
        out_specs=[pl.BlockSpec((frames // 2, width), lambda i: (0, 0))] * 2 + [rows],
        out_shape=[jax.ShapeDtypeStruct((frames // 2, width), jnp.bfloat16)] * 2
        + [jax.ShapeDtypeStruct((width, inner), jnp.float32)],
        scratch_shapes=[
            pltpu.VMEM((steps, frames, part), jnp.float32),
            pltpu.VMEM((frames, 2 * head), jnp.float32),
            *tables,
        ],
        compiler_params=pltpu.CompilerParams(vmem_limit_bytes=56 << 20),
        cost_estimate=pl.CostEstimate(flops=400_000_000, bytes_accessed=6_000_000, transcendentals=2_000_000),
        name="mixer",
    )(
        d_skip,
        ssm_input,
        gate_input,
        b_proj,
        c_proj,
        dt,
        dt_bias[None, :],
        a_log[None, :],
        norm_gain[None, :],
        state,
    )

    return ((top, bottom), state.reshape(heads, head, inner))


def slot_positions(route_ids, experts):
    flat_ids = route_ids.reshape(-1)
    onehot = (flat_ids[:, None] == jnp.arange(experts, dtype=jnp.int32)[None, :]).astype(jnp.int32)
    earlier = jnp.cumsum(onehot, axis=0) - onehot
    return (flat_ids, jnp.sum(earlier * onehot, axis=1))


def body(
    ssm_input,
    gate_input,
    b_proj,
    c_proj,
    dt_raw,
    a_log,
    dt_bias,
    d_skip,
    norm_gain,
    state_in,
    out_proj,
    expert_in,
    expert_out,
    route_ids,
    route_weights,
):
    normed, state = ssm_mixer(
        ssm_input,
        gate_input,
        b_proj,
        c_proj,
        dt_raw,
        a_log,
        dt_bias,
        d_skip,
        norm_gain,
        state_in[0],
    )
    frames_here, topk_count = route_ids.shape
    local_experts = expert_in.shape[0]
    experts = local_experts * lax.axis_size(("wide", "narrow"))
    wide, narrow = lax.axis_size("wide"), lax.axis_size("narrow")
    if experts <= 4 * topk_count and narrow == 4 and wide & (wide - 1) == 0 and local_experts == 1:
        layer_out = dense_experts(
            normed, out_proj, expert_in[0], expert_out[0], route_ids, route_weights
        )
    else:
        layer_out = routed_experts(
            jnp.concatenate(normed), out_proj, expert_in, expert_out, route_ids, route_weights
        )
    return (layer_out, state[None])


def routes(wide, move):
    pairs = []
    for z in range(wide):
        for x in range(2):
            for core in range(2):
                to = move(z, x, core)
                pairs.append(((z * 2 + x) * 2 + core, (to[0] * 2 + to[1]) * 2 + to[2]))
    return pairs


def after(value, *others):
    return lax.optimization_barrier((value, *others))[0]


def dense_experts(normed, out_proj, expert_in, expert_out, route_ids, route_weights):
    frames = route_ids.shape[0]
    wide = lax.axis_size("wide")
    ring = 2 * wide
    z = lax.axis_index("wide")
    x, core = lax.axis_index("narrow") // 2, lax.axis_index("narrow") % 2
    place = jnp.where(x == 0, z, ring - 1 - z)
    axes = ("wide", "narrow")

    def send(value, move):
        return lax.ppermute(value, axes, routes(wide, move))

    def to_core(value):
        return send(value, lambda z, x, c: (z, x, 1 - c))

    def to_x(value):
        return send(value, lambda z, x, c: (z, 1 - x, c))

    def along(value, step):
        def move(z, x, c):
            p = ((z if x == 0 else ring - 1 - z) + step) % ring
            return (p, 0, c) if p < wide else (ring - 1 - p, 1, c)

        return send(value, move)

    out_other, in_other, down_other = to_core(out_proj), to_core(expert_in), to_core(expert_out)

    experts = wide * 4
    gates = jnp.sum(
        jnp.where(route_ids[:, :, None] == jnp.arange(experts), route_weights[:, :, None], 0.0), axis=1
    )
    normed_top, normed_bottom, other = lax.optimization_barrier((*normed, to_x(gates)))
    gates = jnp.where(x == 0, jnp.stack([gates, other]), jnp.stack([other, gates]))[:, None]

    halves = range(2)
    size = frames // 2
    hidden_width = expert_out.shape[0]
    columns = lax.optimization_barrier(
        jnp.where(
            core == 0,
            jnp.concatenate([out_proj, out_other], axis=1),
            jnp.concatenate([out_other, out_proj], axis=1),
        )
    )
    columns, normed_bottom = lax.optimization_barrier((columns, normed_bottom))
    sent = [to_x(normed_top), to_x(normed_bottom)]

    def project(rows):
        return jnp.dot(rows, columns, preferred_element_type=jnp.float32).astype(jnp.bfloat16)

    def merge(gates, other, low):
        return jnp.where(
            low, jnp.concatenate([gates, other], axis=1), jnp.concatenate([other, gates], axis=1)
        )

    own = [project(normed_top), project(normed_bottom)]
    gates, own[0] = lax.optimization_barrier((gates, own[0]))
    step = 1
    while step < wide:
        other = send(gates, lambda z, x, c: (z ^ step, x, c))
        gates, step = merge(gates, other, z & step == 0), 2 * step
    sent[1], gates = lax.optimization_barrier((sent[1], gates))
    mine = (z * 2 + x) * 2 + core
    pair = jnp.stack([mine, mine + 1 - 2 * core])
    gates = jnp.sum(
        jnp.where(pair[:, None] == jnp.arange(experts), gates[..., None, :], 0.0), axis=-1
    )
    gates = jnp.concatenate([gates[0], gates[1, ::-1]])
    gates = lax.dynamic_slice_in_dim(jnp.concatenate([gates, gates]), place, ring, 0)

    rows = []
    for h in halves:
        back = to_x(project(sent[h]))
        rows.append(
            jnp.where(
                x == 0,
                jnp.concatenate([own[h], back], axis=1),
                jnp.concatenate([back, own[h]], axis=1),
            )
        )

    rows[1], expert_in, expert_out = lax.optimization_barrier((rows[1], expert_in, expert_out))

    far = ring // 2
    fore_at, back_at = {0: rows}, {0: rows}
    for k in range(1, far):
        fore_at[k] = [along(fore_at[k - 1][h], 1) for h in halves]
        back_at[k] = [along(back_at[k - 1][h], -1) for h in halves]
    last = [along(fore_at[far - 1][0], 1), along(back_at[far - 1][1], -1)]

    joined_in = jnp.concatenate(
        [
            expert_in[:, :hidden_width],
            in_other[:, :hidden_width],
            expert_in[:, hidden_width:],
            in_other[:, hidden_width:],
        ],
        axis=1,
    )
    joined_down = jnp.concatenate([expert_out, down_other], axis=0)
    joined_in, joined_down = lax.optimization_barrier((joined_in, joined_down))
    is_first = jnp.arange(2 * hidden_width)[None, :] < hidden_width

    def run_experts(parts, gate):
        v = jnp.dot(jnp.concatenate(parts), joined_in, preferred_element_type=jnp.float32)
        hidden = jax.nn.silu(v[:, : 2 * hidden_width]) * v[:, 2 * hidden_width :]
        hidden = (hidden * jnp.where(is_first, gate[:, :1], gate[:, 1:])).astype(jnp.bfloat16)
        return jnp.dot(hidden, joined_down, preferred_element_type=jnp.float32)

    def hop_experts(k, tie):
        parts = [after(part, tie) for part in (rows if k == 0 else [*back_at[k], *fore_at[k]])]
        if k == 0:
            return run_experts(parts, gates[0]), None
        total = run_experts(parts, jnp.concatenate([gates[k], gates[ring - k]]))
        cut = [total[i * size : (i + 1) * size] for i in range(len(parts))]
        return cut[:2], cut[2:]

    total = run_experts(last, gates[far]).astype(jnp.bfloat16)
    fore, back = [along(total[:size], 1), None], [None, along(total[size:], -1)]
    ahead, behind = hop_experts(far - 1, total)
    groups = [((fore, 1, 1), (back, -1, 0)), ((fore, 1, 0), (back, -1, 1))]
    for k in range(far - 1, 0, -1):
        before = ()
        for group in groups:
            loads = []
            for way, step, h in group:
                load = (ahead if step > 0 else behind)[h]
                if way[h] is not None:
                    load = load + after(way[h], *before).astype(jnp.float32)
                loads.append(load.astype(jnp.bfloat16))
            for (way, step, h), load in zip(group, loads):
                way[h] = along(load, step)
            if not before:
                coming = hop_experts(k - 1, loads[0])
                before = tuple(loads)
        ahead, behind = coming
    total = ahead + jnp.concatenate(fore).astype(jnp.float32) + jnp.concatenate(back).astype(jnp.float32)
    return (jnp.concatenate(rows).astype(jnp.float32) + total).astype(jnp.bfloat16)


def routed_experts(normed, out_proj, expert_in, expert_out, route_ids, route_weights):
    mixer_rows = jnp.dot(
        normed,
        lax.all_gather(out_proj, "narrow", axis=1, tiled=True),
        preferred_element_type=jnp.float32,
    ).astype(jnp.bfloat16)
    frames_here = mixer_rows.shape[0]
    model_width = mixer_rows.shape[1]
    topk_count = route_ids.shape[1]
    local_experts = expert_in.shape[0]
    devices = lax.axis_size(("wide", "narrow"))
    experts = local_experts * devices
    capacity = max(2, frames_here * topk_count * 5 // (4 * experts))
    flat_ids, positions = slot_positions(route_ids, experts)
    owners = jnp.arange(frames_here * topk_count, dtype=jnp.int32) // topk_count
    slot_table = (
        jnp.full((experts, capacity), frames_here, jnp.int32).at[flat_ids, positions].set(owners)
    )
    padded = jnp.concatenate([mixer_rows, jnp.zeros((1, model_width), jnp.bfloat16)], axis=0)
    outgoing = padded[slot_table]
    hidden_width = expert_out.shape[1]
    projected = jnp.einsum(
        "nlcd,ldf->nlcf",
        lax.all_to_all(
            outgoing.reshape(devices, local_experts, capacity, model_width),
            ("wide", "narrow"),
            split_axis=0,
            concat_axis=0,
            tiled=True,
        ),
        expert_in,
        preferred_element_type=jnp.float32,
    )
    hidden = (jax.nn.silu(projected[..., :hidden_width]) * projected[..., hidden_width:]).astype(
        jnp.bfloat16
    )
    returned = lax.all_to_all(
        jnp.einsum("nlcf,lfd->nlcd", hidden, expert_out, preferred_element_type=jnp.float32).astype(
            jnp.bfloat16
        ),
        ("wide", "narrow"),
        split_axis=0,
        concat_axis=0,
        tiled=True,
    )
    returned = returned.reshape(experts, capacity, model_width)
    picked = returned[flat_ids, positions].reshape(frames_here, topk_count, model_width)
    expert_sum = jnp.einsum("tk,tkd->td", route_weights, picked.astype(jnp.float32))
    layer_out = (mixer_rows.astype(jnp.float32) + expert_sum).astype(jnp.bfloat16)
    return layer_out


def solution(mesh):
    placed = (
        P(("groups", "wide", "narrow"), None),
        P(("groups", "wide", "narrow"), None),
        P(("groups", "wide", "narrow"), None),
        P(("groups", "wide", "narrow"), None),
        P(("groups", "wide", "narrow"), None),
        P(),
        P(),
        P(),
        P(),
        P(("groups", "wide", "narrow"), None, None, None),
        P(None, "narrow"),
        P(("wide", "narrow"), None, None),
        P(("wide", "narrow"), None, None),
        P(("groups", "wide", "narrow"), None),
        P(("groups", "wide", "narrow"), None),
    )
    return jax.shard_map(
        body,
        mesh=mesh,
        in_specs=placed,
        out_specs=(
            P(("groups", "wide", "narrow"), None),
            P(("groups", "wide", "narrow"), None, None, None),
        ),
        check_vma=False,
    )
```

```python
import functools

import jax
import jax.numpy as jnp
from jax import lax
from jax.experimental import pallas as pl
from jax.experimental.pallas import tpu as pltpu
from jax.sharding import PartitionSpec as P

epsilon = 1e-05


CHUNK = 8
NT = (((1,), (1,)), ((), ()))
TN = (((0,), (0,)), ((), ()))


def column_of(row_ref):
    count = row_ref.shape[1]
    i = lax.broadcasted_iota(jnp.int32, (count, count), 0)
    j = lax.broadcasted_iota(jnp.int32, (count, count), 1)
    return jnp.sum(jnp.where(i == j, row_ref[...], 0.0), axis=1, keepdims=True)


def decays(dt_ref, bias_ref, a_ref, step_ref, decay_ref):
    frames = dt_ref.shape[1]
    step_size = jax.nn.softplus(dt_ref[...] + column_of(bias_ref))
    rise = step_size * -jnp.exp(column_of(a_ref))
    s = lax.broadcasted_iota(jnp.int32, (frames, frames), 0)
    t = lax.broadcasted_iota(jnp.int32, (frames, frames), 1)
    upto = jnp.where(s <= t, 1.0, 0.0)
    step_ref[...] = step_size
    decay_ref[...] = jnp.dot(
        rise, upto, precision=lax.Precision.HIGHEST, preferred_element_type=jnp.float32
    )


def mixer_kernel(
    skip_ref,
    x_ref,
    z_ref,
    b_ref,
    c_ref,
    dt_ref,
    bias_ref,
    a_ref,
    gain_ref,
    state_ref,
    top_ref,
    bottom_ref,
    next_ref,
    g_ref,
    ss_ref,
    step_ref,
    decay_ref,
):
    i = pl.program_id(0)
    frames, width = x_ref.shape
    head = width // CHUNK
    pl.when(i == 0)(lambda: decays(dt_ref, bias_ref, a_ref, step_ref, decay_ref))
    chunk = pl.ds(pl.multiple_of(i * CHUNK, CHUNK), CHUNK)
    step_size, decay = step_ref[chunk, :], decay_ref[chunk, :]
    decay_col = decay.T
    carry_col = jnp.exp(decay_col)
    end = decay[:, frames - 1 : frames]
    tail = (jnp.exp(end - decay) * step_size).T
    kept = jnp.exp(end)
    b = b_ref[...]
    upper = lax.broadcasted_iota(jnp.int32, (2 * head, b.shape[1]), 0) < head
    t = lax.broadcasted_iota(jnp.int32, (frames, frames), 0)
    s = lax.broadcasted_iota(jnp.int32, (frames, frames), 1)
    c = c_ref[...]
    scores = lax.dot_general(c, b, NT, preferred_element_type=jnp.float32)
    scores = jnp.where(s <= t, scores, 0.0)
    cc = jnp.concatenate([c, c], axis=1)
    left = lax.broadcasted_iota(jnp.int32, (frames, 2 * head), 1) < head
    squares = None
    for pair in range(CHUNK // 2):
        mixes = []
        for h in (2 * pair, 2 * pair + 1):
            spread = jnp.exp(jnp.minimum(decay_col[:, h : h + 1] - decay[h : h + 1, :], 0.0))
            mixes.append((spread * (scores * step_size[h : h + 1, :])).astype(jnp.bfloat16))
        at = slice(2 * head * pair, 2 * head * (pair + 1))
        x = x_ref[:, at]
        zero = jnp.zeros_like(x)
        y = jnp.dot(
            jnp.concatenate(mixes, axis=1),
            jnp.concatenate([jnp.where(left, x, zero), jnp.where(left, zero, x)], axis=0),
            preferred_element_type=jnp.float32,
        )
        state = state_ref[at, :]
        high = state.astype(jnp.bfloat16)
        low = (state - high.astype(jnp.float32)).astype(jnp.bfloat16)
        carried = lax.dot_general(
            cc, jnp.concatenate([high, low], axis=1), NT, preferred_element_type=jnp.float32
        )
        factor = jnp.where(
            left, carry_col[:, 2 * pair : 2 * pair + 1], carry_col[:, 2 * pair + 1 : 2 * pair + 2]
        )
        skip = jnp.where(left[:1], skip_ref[i * CHUNK + 2 * pair], skip_ref[i * CHUNK + 2 * pair + 1])
        mixed = y + factor * carried + skip * x.astype(jnp.float32)
        z = z_ref[:, at].astype(jnp.float32)
        g = mixed * jax.nn.silu(z)
        g_ref[i, :, at] = g
        factor = jnp.where(left, tail[:, 2 * pair : 2 * pair + 1], tail[:, 2 * pair + 1 : 2 * pair + 2])
        scaled = (x.astype(jnp.float32) * factor).astype(jnp.bfloat16)
        added = lax.dot_general(scaled, b, TN, preferred_element_type=jnp.float32)
        keep = jnp.where(upper, kept[2 * pair : 2 * pair + 1, :], kept[2 * pair + 1 : 2 * pair + 2, :])
        next_ref[at, :] = keep * state + added
        squares = g * g if squares is None else squares + g * g

    @pl.when(i == 0)
    def _():
        ss_ref[...] = squares

    @pl.when(i > 0)
    def _():
        ss_ref[...] += squares

    steps = g_ref.shape[0]

    @pl.when(i == steps - 1)
    def _():
        mean = jnp.sum(ss_ref[...], axis=1, keepdims=True) / (steps * width)
        scale = lax.rsqrt(mean + epsilon)
        for j in range(steps):
            at = slice(j * width, (j + 1) * width)
            normed = (g_ref[j] * scale * gain_ref[:, at]).astype(jnp.bfloat16)
            top_ref[:, at] = normed[: frames // 2]
            bottom_ref[:, at] = normed[frames // 2 :]


def ssm_mixer(
    ssm_input, gate_input, b_proj, c_proj, dt_raw, a_log, dt_bias, d_skip, norm_gain, state_in
):
    frames, width = ssm_input.shape
    heads, head, inner = state_in.shape
    steps = heads // CHUNK
    part = width // steps
    state = state_in.reshape(width, inner)
    dt = dt_raw.T
    column = pl.BlockSpec((frames, part), lambda i: (0, i))
    whole = pl.BlockSpec((frames, inner), lambda i: (0, 0))
    per_head = pl.BlockSpec((heads, frames), lambda i: (0, 0))
    scalar = pl.BlockSpec((1, heads), lambda i: (0, 0))
    rows = pl.BlockSpec((part, inner), lambda i: (i, 0))
    full_row = pl.BlockSpec((1, width), lambda i: (0, 0))
    tables = [pltpu.VMEM((heads, frames), jnp.float32)] * 2
    top, bottom, state = pl.pallas_call(
        mixer_kernel,
        grid=(steps,),
        in_specs=[
            pl.BlockSpec(memory_space=pltpu.SMEM),
            column,
            column,
            whole,
            whole,
            per_head,
            scalar,
            scalar,
            full_row,
            rows,
        ],
        out_specs=[pl.BlockSpec((frames // 2, width), lambda i: (0, 0))] * 2 + [rows],
        out_shape=[jax.ShapeDtypeStruct((frames // 2, width), jnp.bfloat16)] * 2
        + [jax.ShapeDtypeStruct((width, inner), jnp.float32)],
        scratch_shapes=[
            pltpu.VMEM((steps, frames, part), jnp.float32),
            pltpu.VMEM((frames, 2 * head), jnp.float32),
            *tables,
        ],
        compiler_params=pltpu.CompilerParams(vmem_limit_bytes=56 << 20),
        cost_estimate=pl.CostEstimate(flops=400_000_000, bytes_accessed=6_000_000, transcendentals=2_000_000),
        name="mixer",
    )(
        d_skip,
        ssm_input,
        gate_input,
        b_proj,
        c_proj,
        dt,
        dt_bias[None, :],
        a_log[None, :],
        norm_gain[None, :],
        state,
    )

    return ((top, bottom), state.reshape(heads, head, inner))


def slot_positions(route_ids, experts):
    flat_ids = route_ids.reshape(-1)
    onehot = (flat_ids[:, None] == jnp.arange(experts, dtype=jnp.int32)[None, :]).astype(jnp.int32)
    earlier = jnp.cumsum(onehot, axis=0) - onehot
    return (flat_ids, jnp.sum(earlier * onehot, axis=1))


def body(
    ssm_input,
    gate_input,
    b_proj,
    c_proj,
    dt_raw,
    a_log,
    dt_bias,
    d_skip,
    norm_gain,
    state_in,
    out_proj,
    expert_in,
    expert_out,
    route_ids,
    route_weights,
):
    normed, state = ssm_mixer(
        ssm_input,
        gate_input,
        b_proj,
        c_proj,
        dt_raw,
        a_log,
        dt_bias,
        d_skip,
        norm_gain,
        state_in[0],
    )
    frames_here, topk_count = route_ids.shape
    local_experts = expert_in.shape[0]
    experts = local_experts * lax.axis_size(("wide", "narrow"))
    wide, narrow = lax.axis_size("wide"), lax.axis_size("narrow")
    if experts <= 4 * topk_count and narrow == 4 and wide & (wide - 1) == 0 and local_experts == 1:
        layer_out = dense_experts(
            normed, out_proj, expert_in[0], expert_out[0], route_ids, route_weights
        )
    else:
        layer_out = routed_experts(
            jnp.concatenate(normed), out_proj, expert_in, expert_out, route_ids, route_weights
        )
    return (layer_out, state[None])


def routes(wide, move):
    pairs = []
    for z in range(wide):
        for x in range(2):
            for core in range(2):
                to = move(z, x, core)
                pairs.append(((z * 2 + x) * 2 + core, (to[0] * 2 + to[1]) * 2 + to[2]))
    return pairs


def after(value, *others):
    return lax.optimization_barrier((value, *others))[0]


def dense_experts(normed, out_proj, expert_in, expert_out, route_ids, route_weights):
    frames = route_ids.shape[0]
    wide = lax.axis_size("wide")
    ring = 2 * wide
    z = lax.axis_index("wide")
    x, core = lax.axis_index("narrow") // 2, lax.axis_index("narrow") % 2
    place = jnp.where(x == 0, z, ring - 1 - z)
    axes = ("wide", "narrow")

    def send(value, move):
        return lax.ppermute(value, axes, routes(wide, move))

    def to_core(value):
        return send(value, lambda z, x, c: (z, x, 1 - c))

    def to_x(value):
        return send(value, lambda z, x, c: (z, 1 - x, c))

    def along(value, step):
        def move(z, x, c):
            p = ((z if x == 0 else ring - 1 - z) + step) % ring
            return (p, 0, c) if p < wide else (ring - 1 - p, 1, c)

        return send(value, move)

    out_other, in_other, down_other = to_core(out_proj), to_core(expert_in), to_core(expert_out)

    experts = wide * 4
    gates = jnp.sum(
        jnp.where(route_ids[:, :, None] == jnp.arange(experts), route_weights[:, :, None], 0.0), axis=1
    )
    gates = jnp.pad(gates, ((0, 0), (0, -experts % 128)))
    gates = lax.all_gather(gates, axes, axis=0, tiled=False)
    normed_top, normed_bottom = normed

    halves = range(2)
    size = frames // 2
    hidden_width = expert_out.shape[0]
    columns = lax.optimization_barrier(
        jnp.where(
            core == 0,
            jnp.concatenate([out_proj, out_other], axis=1),
            jnp.concatenate([out_other, out_proj], axis=1),
        )
    )
    columns, normed_bottom = lax.optimization_barrier((columns, normed_bottom))
    sent = [to_x(normed_top), to_x(normed_bottom)]

    def project(rows):
        return jnp.dot(rows, columns, preferred_element_type=jnp.float32).astype(jnp.bfloat16)

    own = [project(normed_top), project(normed_bottom)]
    rows = []
    for h in halves:
        back = to_x(project(sent[h]))
        rows.append(
            jnp.where(
                x == 0,
                jnp.concatenate([own[h], back], axis=1),
                jnp.concatenate([back, own[h]], axis=1),
            )
        )

    rows[1], expert_in, expert_out = lax.optimization_barrier((rows[1], expert_in, expert_out))

    far = ring // 2
    fore_at, back_at = {0: rows}, {0: rows}
    for k in range(1, far):
        fore_at[k] = [along(fore_at[k - 1][h], 1) for h in halves]
        back_at[k] = [along(back_at[k - 1][h], -1) for h in halves]
    last = [along(fore_at[far - 1][0], 1), along(back_at[far - 1][1], -1)]

    back_at[far - 1][0], gates = lax.optimization_barrier((back_at[far - 1][0], gates))

    mine = (z * 2 + x) * 2 + core
    lanes = jnp.arange(gates.shape[-1])
    gates = lax.dynamic_slice_in_dim(gates.reshape(wide, 2, 2, frames, -1), core, 1, 2)[:, :, 0]
    gates = jnp.stack(
        [jnp.sum(jnp.where(lanes == e, gates, 0.0), axis=-1) for e in (mine, mine + 1 - 2 * core)], axis=-1
    )
    gates = jnp.concatenate([gates[:, 0], gates[::-1, 1]])
    gates = lax.dynamic_slice_in_dim(jnp.concatenate([gates, gates]), place, ring, 0)

    joined_in = jnp.concatenate(
        [
            expert_in[:, :hidden_width],
            in_other[:, :hidden_width],
            expert_in[:, hidden_width:],
            in_other[:, hidden_width:],
        ],
        axis=1,
    )
    joined_down = jnp.concatenate([expert_out, down_other], axis=0)
    joined_in, joined_down = lax.optimization_barrier((joined_in, joined_down))
    is_first = jnp.arange(2 * hidden_width)[None, :] < hidden_width

    def run_experts(parts, gate):
        v = jnp.dot(jnp.concatenate(parts), joined_in, preferred_element_type=jnp.float32)
        hidden = jax.nn.silu(v[:, : 2 * hidden_width]) * v[:, 2 * hidden_width :]
        hidden = (hidden * jnp.where(is_first, gate[:, :1], gate[:, 1:])).astype(jnp.bfloat16)
        return jnp.dot(hidden, joined_down, preferred_element_type=jnp.float32)

    def hop_experts(k, tie):
        parts = [after(part, tie) for part in (rows if k == 0 else [*back_at[k], *fore_at[k]])]
        if k == 0:
            return run_experts(parts, gates[0]), None
        total = run_experts(parts, jnp.concatenate([gates[k], gates[ring - k]]))
        cut = [total[i * size : (i + 1) * size] for i in range(len(parts))]
        return cut[:2], cut[2:]

    total = run_experts(last, gates[far]).astype(jnp.bfloat16)
    fore, back = [along(total[:size], 1), None], [None, along(total[size:], -1)]
    ahead, behind = hop_experts(far - 1, total)
    groups = [((fore, 1, 1), (back, -1, 0)), ((fore, 1, 0), (back, -1, 1))]
    for k in range(far - 1, 0, -1):
        before = ()
        for group in groups:
            loads = []
            for way, step, h in group:
                load = (ahead if step > 0 else behind)[h]
                if way[h] is not None:
                    load = load + after(way[h], *before).astype(jnp.float32)
                loads.append(load.astype(jnp.bfloat16))
            for (way, step, h), load in zip(group, loads):
                way[h] = along(load, step)
            if not before:
                coming = hop_experts(k - 1, loads[0])
                before = tuple(loads)
        ahead, behind = coming
    total = ahead + jnp.concatenate(fore).astype(jnp.float32) + jnp.concatenate(back).astype(jnp.float32)
    return (jnp.concatenate(rows).astype(jnp.float32) + total).astype(jnp.bfloat16)


def routed_experts(normed, out_proj, expert_in, expert_out, route_ids, route_weights):
    mixer_rows = jnp.dot(
        normed,
        lax.all_gather(out_proj, "narrow", axis=1, tiled=True),
        preferred_element_type=jnp.float32,
    ).astype(jnp.bfloat16)
    frames_here = mixer_rows.shape[0]
    model_width = mixer_rows.shape[1]
    topk_count = route_ids.shape[1]
    local_experts = expert_in.shape[0]
    devices = lax.axis_size(("wide", "narrow"))
    experts = local_experts * devices
    capacity = max(2, frames_here * topk_count * 5 // (4 * experts))
    flat_ids, positions = slot_positions(route_ids, experts)
    owners = jnp.arange(frames_here * topk_count, dtype=jnp.int32) // topk_count
    slot_table = (
        jnp.full((experts, capacity), frames_here, jnp.int32).at[flat_ids, positions].set(owners)
    )
    padded = jnp.concatenate([mixer_rows, jnp.zeros((1, model_width), jnp.bfloat16)], axis=0)
    outgoing = padded[slot_table]
    hidden_width = expert_out.shape[1]
    projected = jnp.einsum(
        "nlcd,ldf->nlcf",
        lax.all_to_all(
            outgoing.reshape(devices, local_experts, capacity, model_width),
            ("wide", "narrow"),
            split_axis=0,
            concat_axis=0,
            tiled=True,
        ),
        expert_in,
        preferred_element_type=jnp.float32,
    )
    hidden = (jax.nn.silu(projected[..., :hidden_width]) * projected[..., hidden_width:]).astype(
        jnp.bfloat16
    )
    returned = lax.all_to_all(
        jnp.einsum("nlcf,lfd->nlcd", hidden, expert_out, preferred_element_type=jnp.float32).astype(
            jnp.bfloat16
        ),
        ("wide", "narrow"),
        split_axis=0,
        concat_axis=0,
        tiled=True,
    )
    returned = returned.reshape(experts, capacity, model_width)
    picked = returned[flat_ids, positions].reshape(frames_here, topk_count, model_width)
    expert_sum = jnp.einsum("tk,tkd->td", route_weights, picked.astype(jnp.float32))
    layer_out = (mixer_rows.astype(jnp.float32) + expert_sum).astype(jnp.bfloat16)
    return layer_out


def solution(mesh):
    placed = (
        P(("groups", "wide", "narrow"), None),
        P(("groups", "wide", "narrow"), None),
        P(("groups", "wide", "narrow"), None),
        P(("groups", "wide", "narrow"), None),
        P(("groups", "wide", "narrow"), None),
        P(),
        P(),
        P(),
        P(),
        P(("groups", "wide", "narrow"), None, None, None),
        P(None, "narrow"),
        P(("wide", "narrow"), None, None),
        P(("wide", "narrow"), None, None),
        P(("groups", "wide", "narrow"), None),
        P(("groups", "wide", "narrow"), None),
    )
    return jax.shard_map(
        body,
        mesh=mesh,
        in_specs=placed,
        out_specs=(
            P(("groups", "wide", "narrow"), None),
            P(("groups", "wide", "narrow"), None, None, None),
        ),
        check_vma=False,
    )
```

```python
import functools

import jax
import jax.numpy as jnp
from jax import lax
from jax.experimental import pallas as pl
from jax.experimental.pallas import tpu as pltpu
from jax.sharding import PartitionSpec as P

epsilon = 1e-05


CHUNK = 8
NT = (((1,), (1,)), ((), ()))
TN = (((0,), (0,)), ((), ()))


def column_of(row_ref):
    count = row_ref.shape[1]
    i = lax.broadcasted_iota(jnp.int32, (count, count), 0)
    j = lax.broadcasted_iota(jnp.int32, (count, count), 1)
    return jnp.sum(jnp.where(i == j, row_ref[...], 0.0), axis=1, keepdims=True)


def decays(dt_ref, bias_ref, a_ref, step_ref, decay_ref):
    frames = dt_ref.shape[1]
    step_size = jax.nn.softplus(dt_ref[...] + column_of(bias_ref))
    rise = step_size * -jnp.exp(column_of(a_ref))
    s = lax.broadcasted_iota(jnp.int32, (frames, frames), 0)
    t = lax.broadcasted_iota(jnp.int32, (frames, frames), 1)
    upto = jnp.where(s <= t, 1.0, 0.0)
    step_ref[...] = step_size
    decay_ref[...] = jnp.dot(
        rise, upto, precision=lax.Precision.HIGHEST, preferred_element_type=jnp.float32
    )


def mixer_kernel(
    skip_ref,
    x_ref,
    z_ref,
    b_ref,
    c_ref,
    dt_ref,
    bias_ref,
    a_ref,
    gain_ref,
    state_ref,
    top_ref,
    bottom_ref,
    next_ref,
    g_ref,
    ss_ref,
    step_ref,
    decay_ref,
):
    i = pl.program_id(0)
    frames, width = x_ref.shape
    head = width // CHUNK
    pl.when(i == 0)(lambda: decays(dt_ref, bias_ref, a_ref, step_ref, decay_ref))
    chunk = pl.ds(pl.multiple_of(i * CHUNK, CHUNK), CHUNK)
    step_size, decay = step_ref[chunk, :], decay_ref[chunk, :]
    decay_col = decay.T
    carry_col = jnp.exp(decay_col)
    end = decay[:, frames - 1 : frames]
    tail = (jnp.exp(end - decay) * step_size).T
    kept = jnp.exp(end)
    b = b_ref[...]
    upper = lax.broadcasted_iota(jnp.int32, (2 * head, b.shape[1]), 0) < head
    t = lax.broadcasted_iota(jnp.int32, (frames, frames), 0)
    s = lax.broadcasted_iota(jnp.int32, (frames, frames), 1)
    c = c_ref[...]
    scores = lax.dot_general(c, b, NT, preferred_element_type=jnp.float32)
    scores = jnp.where(s <= t, scores, 0.0)
    cc = jnp.concatenate([c, c], axis=1)
    left = lax.broadcasted_iota(jnp.int32, (frames, 2 * head), 1) < head
    squares = None
    for pair in range(CHUNK // 2):
        mixes = []
        for h in (2 * pair, 2 * pair + 1):
            spread = jnp.exp(jnp.minimum(decay_col[:, h : h + 1] - decay[h : h + 1, :], 0.0))
            mixes.append((spread * (scores * step_size[h : h + 1, :])).astype(jnp.bfloat16))
        at = slice(2 * head * pair, 2 * head * (pair + 1))
        x = x_ref[:, at]
        zero = jnp.zeros_like(x)
        y = jnp.dot(
            jnp.concatenate(mixes, axis=1),
            jnp.concatenate([jnp.where(left, x, zero), jnp.where(left, zero, x)], axis=0),
            preferred_element_type=jnp.float32,
        )
        state = state_ref[at, :]
        high = state.astype(jnp.bfloat16)
        low = (state - high.astype(jnp.float32)).astype(jnp.bfloat16)
        carried = lax.dot_general(
            cc, jnp.concatenate([high, low], axis=1), NT, preferred_element_type=jnp.float32
        )
        factor = jnp.where(
            left, carry_col[:, 2 * pair : 2 * pair + 1], carry_col[:, 2 * pair + 1 : 2 * pair + 2]
        )
        skip = jnp.where(left[:1], skip_ref[i * CHUNK + 2 * pair], skip_ref[i * CHUNK + 2 * pair + 1])
        mixed = y + factor * carried + skip * x.astype(jnp.float32)
        z = z_ref[:, at].astype(jnp.float32)
        g = mixed * jax.nn.silu(z)
        g_ref[i, :, at] = g
        factor = jnp.where(left, tail[:, 2 * pair : 2 * pair + 1], tail[:, 2 * pair + 1 : 2 * pair + 2])
        scaled = (x.astype(jnp.float32) * factor).astype(jnp.bfloat16)
        added = lax.dot_general(scaled, b, TN, preferred_element_type=jnp.float32)
        keep = jnp.where(upper, kept[2 * pair : 2 * pair + 1, :], kept[2 * pair + 1 : 2 * pair + 2, :])
        next_ref[at, :] = keep * state + added
        squares = g * g if squares is None else squares + g * g

    @pl.when(i == 0)
    def _():
        ss_ref[...] = squares

    @pl.when(i > 0)
    def _():
        ss_ref[...] += squares

    steps = g_ref.shape[0]

    @pl.when(i == steps - 1)
    def _():
        mean = jnp.sum(ss_ref[...], axis=1, keepdims=True) / (steps * width)
        scale = lax.rsqrt(mean + epsilon)
        for j in range(steps):
            at = slice(j * width, (j + 1) * width)
            normed = (g_ref[j] * scale * gain_ref[:, at]).astype(jnp.bfloat16)
            top_ref[:, at] = normed[: frames // 2]
            bottom_ref[:, at] = normed[frames // 2 :]


def ssm_mixer(
    ssm_input, gate_input, b_proj, c_proj, dt_raw, a_log, dt_bias, d_skip, norm_gain, state_in
):
    frames, width = ssm_input.shape
    heads, head, inner = state_in.shape
    steps = heads // CHUNK
    part = width // steps
    state = state_in.reshape(width, inner)
    dt = dt_raw.T
    column = pl.BlockSpec((frames, part), lambda i: (0, i))
    whole = pl.BlockSpec((frames, inner), lambda i: (0, 0))
    per_head = pl.BlockSpec((heads, frames), lambda i: (0, 0))
    scalar = pl.BlockSpec((1, heads), lambda i: (0, 0))
    rows = pl.BlockSpec((part, inner), lambda i: (i, 0))
    full_row = pl.BlockSpec((1, width), lambda i: (0, 0))
    tables = [pltpu.VMEM((heads, frames), jnp.float32)] * 2
    top, bottom, state = pl.pallas_call(
        mixer_kernel,
        grid=(steps,),
        in_specs=[
            pl.BlockSpec(memory_space=pltpu.SMEM),
            column,
            column,
            whole,
            whole,
            per_head,
            scalar,
            scalar,
            full_row,
            rows,
        ],
        out_specs=[pl.BlockSpec((frames // 2, width), lambda i: (0, 0))] * 2 + [rows],
        out_shape=[jax.ShapeDtypeStruct((frames // 2, width), jnp.bfloat16)] * 2
        + [jax.ShapeDtypeStruct((width, inner), jnp.float32)],
        scratch_shapes=[
            pltpu.VMEM((steps, frames, part), jnp.float32),
            pltpu.VMEM((frames, 2 * head), jnp.float32),
            *tables,
        ],
        compiler_params=pltpu.CompilerParams(vmem_limit_bytes=56 << 20),
        cost_estimate=pl.CostEstimate(flops=400_000_000, bytes_accessed=6_000_000, transcendentals=2_000_000),
        name="mixer",
    )(
        d_skip,
        ssm_input,
        gate_input,
        b_proj,
        c_proj,
        dt,
        dt_bias[None, :],
        a_log[None, :],
        norm_gain[None, :],
        state,
    )

    return ((top, bottom), state.reshape(heads, head, inner))


def slot_positions(route_ids, experts):
    flat_ids = route_ids.reshape(-1)
    onehot = (flat_ids[:, None] == jnp.arange(experts, dtype=jnp.int32)[None, :]).astype(jnp.int32)
    earlier = jnp.cumsum(onehot, axis=0) - onehot
    return (flat_ids, jnp.sum(earlier * onehot, axis=1))


def body(
    ssm_input,
    gate_input,
    b_proj,
    c_proj,
    dt_raw,
    a_log,
    dt_bias,
    d_skip,
    norm_gain,
    state_in,
    out_proj,
    expert_in,
    expert_out,
    route_ids,
    route_weights,
):
    normed, state = ssm_mixer(
        ssm_input,
        gate_input,
        b_proj,
        c_proj,
        dt_raw,
        a_log,
        dt_bias,
        d_skip,
        norm_gain,
        state_in[0],
    )
    frames_here, topk_count = route_ids.shape
    local_experts = expert_in.shape[0]
    experts = local_experts * lax.axis_size(("wide", "narrow"))
    wide, narrow = lax.axis_size("wide"), lax.axis_size("narrow")
    if experts <= 4 * topk_count and narrow == 4 and wide & (wide - 1) == 0 and local_experts == 1:
        layer_out = dense_experts(
            normed, out_proj, expert_in[0], expert_out[0], route_ids, route_weights
        )
    else:
        layer_out = routed_experts(
            jnp.concatenate(normed), out_proj, expert_in, expert_out, route_ids, route_weights
        )
    return (layer_out, state[None])


def routes(wide, move):
    pairs = []
    for z in range(wide):
        for x in range(2):
            for core in range(2):
                to = move(z, x, core)
                pairs.append(((z * 2 + x) * 2 + core, (to[0] * 2 + to[1]) * 2 + to[2]))
    return pairs


def after(value, *others):
    return lax.optimization_barrier((value, *others))[0]


def dense_experts(normed, out_proj, expert_in, expert_out, route_ids, route_weights):
    frames = route_ids.shape[0]
    wide = lax.axis_size("wide")
    ring = 2 * wide
    z = lax.axis_index("wide")
    x, core = lax.axis_index("narrow") // 2, lax.axis_index("narrow") % 2
    place = jnp.where(x == 0, z, ring - 1 - z)
    axes = ("wide", "narrow")

    def send(value, move):
        return lax.ppermute(value, axes, routes(wide, move))

    def to_core(value):
        return send(value, lambda z, x, c: (z, x, 1 - c))

    def to_x(value):
        return send(value, lambda z, x, c: (z, 1 - x, c))

    def along(value, step):
        def move(z, x, c):
            p = ((z if x == 0 else ring - 1 - z) + step) % ring
            return (p, 0, c) if p < wide else (ring - 1 - p, 1, c)

        return send(value, move)

    out_other, in_other, down_other = to_core(out_proj), to_core(expert_in), to_core(expert_out)

    normed_top, normed_bottom = normed

    halves = range(2)
    size = frames // 2
    hidden_width = expert_out.shape[0]
    columns = lax.optimization_barrier(
        jnp.where(
            core == 0,
            jnp.concatenate([out_proj, out_other], axis=1),
            jnp.concatenate([out_other, out_proj], axis=1),
        )
    )
    columns, normed_bottom, route_weights = lax.optimization_barrier(
        (columns, normed_bottom, route_weights)
    )
    sent = [to_x(normed_top), to_x(normed_bottom)]

    def project(rows):
        return jnp.dot(rows, columns, preferred_element_type=jnp.float32).astype(jnp.bfloat16)

    experts = wide * 4
    chosen = route_ids.T[None] == jnp.arange(experts)[:, None, None]
    gates = jnp.sum(jnp.where(chosen, route_weights.T[None], 0.0), axis=1)
    gates = jnp.pad(gates, ((0, -experts % 128), (0, 0)))
    sent[0], gates = lax.optimization_barrier((sent[0], gates))
    gates = lax.all_gather(gates, axes, axis=0, tiled=False)

    own = [project(normed_top), project(normed_bottom)]
    rows = []
    for h in halves:
        back = to_x(project(sent[h]))
        rows.append(
            jnp.where(
                x == 0,
                jnp.concatenate([own[h], back], axis=1),
                jnp.concatenate([back, own[h]], axis=1),
            )
        )

    rows[1], expert_in, expert_out = lax.optimization_barrier((rows[1], expert_in, expert_out))

    far = ring // 2
    fore_at, back_at = {0: rows}, {0: rows}
    for k in range(1, far):
        fore_at[k] = [along(fore_at[k - 1][h], 1) for h in halves]
        back_at[k] = [along(back_at[k - 1][h], -1) for h in halves]
    last = [along(fore_at[far - 1][0], 1), along(back_at[far - 1][1], -1)]

    value = back_at[far - 1][0][0, 0]
    late = (value != value).astype(jnp.int32)
    mine = (z * 2 + x) * 2 + core
    expert = jnp.arange(experts)[None, :, None]
    at = (place + jnp.arange(ring)) % ring
    clip = jnp.where(at < wide, at * 4, (ring - 1 - at) * 4 + 2) + core
    clip = clip[:, None] == jnp.arange(4 * wide)
    picked = []
    for e in (mine + late, mine + 1 - 2 * core + late):
        of_expert = jnp.sum(jnp.where(expert == e, gates[:, :experts], 0.0), axis=1)
        picked.append(jnp.sum(jnp.where(clip[:, :, None], of_expert[None], 0.0), axis=1))
    gates = jnp.stack(picked, axis=-1)

    joined_in = jnp.concatenate(
        [
            expert_in[:, :hidden_width],
            in_other[:, :hidden_width],
            expert_in[:, hidden_width:],
            in_other[:, hidden_width:],
        ],
        axis=1,
    )
    joined_down = jnp.concatenate([expert_out, down_other], axis=0)
    joined_in, joined_down = lax.optimization_barrier((joined_in, joined_down))
    is_first = jnp.arange(2 * hidden_width)[None, :] < hidden_width

    def run_experts(parts, gate):
        v = jnp.dot(jnp.concatenate(parts), joined_in, preferred_element_type=jnp.float32)
        hidden = jax.nn.silu(v[:, : 2 * hidden_width]) * v[:, 2 * hidden_width :]
        hidden = (hidden * jnp.where(is_first, gate[:, :1], gate[:, 1:])).astype(jnp.bfloat16)
        return jnp.dot(hidden, joined_down, preferred_element_type=jnp.float32)

    def hop_experts(k, tie):
        parts = [after(part, tie) for part in (rows if k == 0 else [*back_at[k], *fore_at[k]])]
        if k == 0:
            return run_experts(parts, gates[0]), None
        total = run_experts(parts, jnp.concatenate([gates[k], gates[ring - k]]))
        cut = [total[i * size : (i + 1) * size] for i in range(len(parts))]
        return cut[:2], cut[2:]

    total = run_experts(last, gates[far]).astype(jnp.bfloat16)
    fore, back = [along(total[:size], 1), None], [None, along(total[size:], -1)]
    ahead, behind = hop_experts(far - 1, total)
    groups = [((fore, 1, 1), (back, -1, 0)), ((fore, 1, 0), (back, -1, 1))]
    for k in range(far - 1, 0, -1):
        before = ()
        for group in groups:
            loads = []
            for way, step, h in group:
                load = (ahead if step > 0 else behind)[h]
                if way[h] is not None:
                    load = load + after(way[h], *before).astype(jnp.float32)
                loads.append(load.astype(jnp.bfloat16))
            for (way, step, h), load in zip(group, loads):
                way[h] = along(load, step)
            if not before:
                coming = hop_experts(k - 1, loads[0])
                before = tuple(loads)
        ahead, behind = coming
    total = ahead + jnp.concatenate(fore).astype(jnp.float32) + jnp.concatenate(back).astype(jnp.float32)
    return (jnp.concatenate(rows).astype(jnp.float32) + total).astype(jnp.bfloat16)


def routed_experts(normed, out_proj, expert_in, expert_out, route_ids, route_weights):
    mixer_rows = jnp.dot(
        normed,
        lax.all_gather(out_proj, "narrow", axis=1, tiled=True),
        preferred_element_type=jnp.float32,
    ).astype(jnp.bfloat16)
    frames_here = mixer_rows.shape[0]
    model_width = mixer_rows.shape[1]
    topk_count = route_ids.shape[1]
    local_experts = expert_in.shape[0]
    devices = lax.axis_size(("wide", "narrow"))
    experts = local_experts * devices
    capacity = max(2, frames_here * topk_count * 5 // (4 * experts))
    flat_ids, positions = slot_positions(route_ids, experts)
    owners = jnp.arange(frames_here * topk_count, dtype=jnp.int32) // topk_count
    slot_table = (
        jnp.full((experts, capacity), frames_here, jnp.int32).at[flat_ids, positions].set(owners)
    )
    padded = jnp.concatenate([mixer_rows, jnp.zeros((1, model_width), jnp.bfloat16)], axis=0)
    outgoing = padded[slot_table]
    hidden_width = expert_out.shape[1]
    projected = jnp.einsum(
        "nlcd,ldf->nlcf",
        lax.all_to_all(
            outgoing.reshape(devices, local_experts, capacity, model_width),
            ("wide", "narrow"),
            split_axis=0,
            concat_axis=0,
            tiled=True,
        ),
        expert_in,
        preferred_element_type=jnp.float32,
    )
    hidden = (jax.nn.silu(projected[..., :hidden_width]) * projected[..., hidden_width:]).astype(
        jnp.bfloat16
    )
    returned = lax.all_to_all(
        jnp.einsum("nlcf,lfd->nlcd", hidden, expert_out, preferred_element_type=jnp.float32).astype(
            jnp.bfloat16
        ),
        ("wide", "narrow"),
        split_axis=0,
        concat_axis=0,
        tiled=True,
    )
    returned = returned.reshape(experts, capacity, model_width)
    picked = returned[flat_ids, positions].reshape(frames_here, topk_count, model_width)
    expert_sum = jnp.einsum("tk,tkd->td", route_weights, picked.astype(jnp.float32))
    layer_out = (mixer_rows.astype(jnp.float32) + expert_sum).astype(jnp.bfloat16)
    return layer_out


def solution(mesh):
    placed = (
        P(("groups", "wide", "narrow"), None),
        P(("groups", "wide", "narrow"), None),
        P(("groups", "wide", "narrow"), None),
        P(("groups", "wide", "narrow"), None),
        P(("groups", "wide", "narrow"), None),
        P(),
        P(),
        P(),
        P(),
        P(("groups", "wide", "narrow"), None, None, None),
        P(None, "narrow"),
        P(("wide", "narrow"), None, None),
        P(("wide", "narrow"), None, None),
        P(("groups", "wide", "narrow"), None),
        P(("groups", "wide", "narrow"), None),
    )
    return jax.shard_map(
        body,
        mesh=mesh,
        in_specs=placed,
        out_specs=(
            P(("groups", "wide", "narrow"), None),
            P(("groups", "wide", "narrow"), None, None, None),
        ),
        check_vma=False,
    )
```

```python
import functools

import jax
import jax.numpy as jnp
from jax import lax
from jax.experimental import pallas as pl
from jax.experimental.pallas import tpu as pltpu
from jax.sharding import PartitionSpec as P

epsilon = 1e-05


CHUNK = 8
NT = (((1,), (1,)), ((), ()))
TN = (((0,), (0,)), ((), ()))


def column_of(row_ref):
    count = row_ref.shape[1]
    i = lax.broadcasted_iota(jnp.int32, (count, count), 0)
    j = lax.broadcasted_iota(jnp.int32, (count, count), 1)
    return jnp.sum(jnp.where(i == j, row_ref[...], 0.0), axis=1, keepdims=True)


def decays(dt_ref, bias_ref, a_ref, step_ref, decay_ref):
    frames = dt_ref.shape[1]
    step_size = jax.nn.softplus(dt_ref[...] + column_of(bias_ref))
    rise = step_size * -jnp.exp(column_of(a_ref))
    s = lax.broadcasted_iota(jnp.int32, (frames, frames), 0)
    t = lax.broadcasted_iota(jnp.int32, (frames, frames), 1)
    upto = jnp.where(s <= t, 1.0, 0.0)
    step_ref[...] = step_size
    decay_ref[...] = jnp.dot(
        rise, upto, precision=lax.Precision.HIGHEST, preferred_element_type=jnp.float32
    )


def mixer_kernel(
    skip_ref,
    x_ref,
    z_ref,
    b_ref,
    c_ref,
    dt_ref,
    bias_ref,
    a_ref,
    gain_ref,
    state_ref,
    top_ref,
    bottom_ref,
    next_ref,
    g_ref,
    ss_ref,
    step_ref,
    decay_ref,
):
    i = pl.program_id(0)
    frames, width = x_ref.shape
    head = width // CHUNK
    pl.when(i == 0)(lambda: decays(dt_ref, bias_ref, a_ref, step_ref, decay_ref))
    chunk = pl.ds(pl.multiple_of(i * CHUNK, CHUNK), CHUNK)
    step_size, decay = step_ref[chunk, :], decay_ref[chunk, :]
    decay_col = decay.T
    carry_col = jnp.exp(decay_col)
    end = decay[:, frames - 1 : frames]
    tail = (jnp.exp(end - decay) * step_size).T
    kept = jnp.exp(end)
    b = b_ref[...]
    upper = lax.broadcasted_iota(jnp.int32, (2 * head, b.shape[1]), 0) < head
    t = lax.broadcasted_iota(jnp.int32, (frames, frames), 0)
    s = lax.broadcasted_iota(jnp.int32, (frames, frames), 1)
    c = c_ref[...]
    scores = lax.dot_general(c, b, NT, preferred_element_type=jnp.float32)
    scores = jnp.where(s <= t, scores, 0.0)
    cc = jnp.concatenate([c, c], axis=1)
    left = lax.broadcasted_iota(jnp.int32, (frames, 2 * head), 1) < head
    squares = None
    for pair in range(CHUNK // 2):
        mixes = []
        for h in (2 * pair, 2 * pair + 1):
            spread = jnp.exp(jnp.minimum(decay_col[:, h : h + 1] - decay[h : h + 1, :], 0.0))
            mixes.append((spread * (scores * step_size[h : h + 1, :])).astype(jnp.bfloat16))
        at = slice(2 * head * pair, 2 * head * (pair + 1))
        x = x_ref[:, at]
        zero = jnp.zeros_like(x)
        y = jnp.dot(
            jnp.concatenate(mixes, axis=1),
            jnp.concatenate([jnp.where(left, x, zero), jnp.where(left, zero, x)], axis=0),
            preferred_element_type=jnp.float32,
        )
        state = state_ref[at, :]
        high = state.astype(jnp.bfloat16)
        low = (state - high.astype(jnp.float32)).astype(jnp.bfloat16)
        carried = lax.dot_general(
            cc, jnp.concatenate([high, low], axis=1), NT, preferred_element_type=jnp.float32
        )
        factor = jnp.where(
            left, carry_col[:, 2 * pair : 2 * pair + 1], carry_col[:, 2 * pair + 1 : 2 * pair + 2]
        )
        skip = jnp.where(left[:1], skip_ref[i * CHUNK + 2 * pair], skip_ref[i * CHUNK + 2 * pair + 1])
        mixed = y + factor * carried + skip * x.astype(jnp.float32)
        z = z_ref[:, at].astype(jnp.float32)
        g = mixed * jax.nn.silu(z)
        g_ref[i, :, at] = g
        factor = jnp.where(left, tail[:, 2 * pair : 2 * pair + 1], tail[:, 2 * pair + 1 : 2 * pair + 2])
        scaled = (x.astype(jnp.float32) * factor).astype(jnp.bfloat16)
        added = lax.dot_general(scaled, b, TN, preferred_element_type=jnp.float32)
        keep = jnp.where(upper, kept[2 * pair : 2 * pair + 1, :], kept[2 * pair + 1 : 2 * pair + 2, :])
        next_ref[at, :] = keep * state + added
        squares = g * g if squares is None else squares + g * g

    @pl.when(i == 0)
    def _():
        ss_ref[...] = squares

    @pl.when(i > 0)
    def _():
        ss_ref[...] += squares

    steps = g_ref.shape[0]

    @pl.when(i == steps - 1)
    def _():
        mean = jnp.sum(ss_ref[...], axis=1, keepdims=True) / (steps * width)
        scale = lax.rsqrt(mean + epsilon)
        for j in range(steps):
            at = slice(j * width, (j + 1) * width)
            normed = (g_ref[j] * scale * gain_ref[:, at]).astype(jnp.bfloat16)
            top_ref[:, at] = normed[: frames // 2]
            bottom_ref[:, at] = normed[frames // 2 :]


def ssm_mixer(
    ssm_input, gate_input, b_proj, c_proj, dt_raw, a_log, dt_bias, d_skip, norm_gain, state_in
):
    frames, width = ssm_input.shape
    heads, head, inner = state_in.shape
    steps = heads // CHUNK
    part = width // steps
    state = state_in.reshape(width, inner)
    dt = dt_raw.T
    column = pl.BlockSpec((frames, part), lambda i: (0, i))
    whole = pl.BlockSpec((frames, inner), lambda i: (0, 0))
    per_head = pl.BlockSpec((heads, frames), lambda i: (0, 0))
    scalar = pl.BlockSpec((1, heads), lambda i: (0, 0))
    rows = pl.BlockSpec((part, inner), lambda i: (i, 0))
    full_row = pl.BlockSpec((1, width), lambda i: (0, 0))
    tables = [pltpu.VMEM((heads, frames), jnp.float32)] * 2
    top, bottom, state = pl.pallas_call(
        mixer_kernel,
        grid=(steps,),
        in_specs=[
            pl.BlockSpec(memory_space=pltpu.SMEM),
            column,
            column,
            whole,
            whole,
            per_head,
            scalar,
            scalar,
            full_row,
            rows,
        ],
        out_specs=[pl.BlockSpec((frames // 2, width), lambda i: (0, 0))] * 2 + [rows],
        out_shape=[jax.ShapeDtypeStruct((frames // 2, width), jnp.bfloat16)] * 2
        + [jax.ShapeDtypeStruct((width, inner), jnp.float32)],
        scratch_shapes=[
            pltpu.VMEM((steps, frames, part), jnp.float32),
            pltpu.VMEM((frames, 2 * head), jnp.float32),
            *tables,
        ],
        compiler_params=pltpu.CompilerParams(vmem_limit_bytes=56 << 20),
        cost_estimate=pl.CostEstimate(flops=400_000_000, bytes_accessed=6_000_000, transcendentals=2_000_000),
        name="mixer",
    )(
        d_skip,
        ssm_input,
        gate_input,
        b_proj,
        c_proj,
        dt,
        dt_bias[None, :],
        a_log[None, :],
        norm_gain[None, :],
        state,
    )

    return ((top, bottom), state.reshape(heads, head, inner))


def slot_positions(route_ids, experts):
    flat_ids = route_ids.reshape(-1)
    onehot = (flat_ids[:, None] == jnp.arange(experts, dtype=jnp.int32)[None, :]).astype(jnp.int32)
    earlier = jnp.cumsum(onehot, axis=0) - onehot
    return (flat_ids, jnp.sum(earlier * onehot, axis=1))


def body(
    ssm_input,
    gate_input,
    b_proj,
    c_proj,
    dt_raw,
    a_log,
    dt_bias,
    d_skip,
    norm_gain,
    state_in,
    out_proj,
    expert_in,
    expert_out,
    route_ids,
    route_weights,
):
    normed, state = ssm_mixer(
        ssm_input,
        gate_input,
        b_proj,
        c_proj,
        dt_raw,
        a_log,
        dt_bias,
        d_skip,
        norm_gain,
        state_in[0],
    )
    frames_here, topk_count = route_ids.shape
    local_experts = expert_in.shape[0]
    experts = local_experts * lax.axis_size(("wide", "narrow"))
    wide, narrow = lax.axis_size("wide"), lax.axis_size("narrow")
    if experts <= 4 * topk_count and narrow == 4 and wide & (wide - 1) == 0 and local_experts == 1:
        layer_out = dense_experts(
            normed, out_proj, expert_in[0], expert_out[0], route_ids, route_weights
        )
    else:
        layer_out = routed_experts(
            jnp.concatenate(normed), out_proj, expert_in, expert_out, route_ids, route_weights
        )
    return (layer_out, state[None])


def routes(wide, move):
    pairs = []
    for z in range(wide):
        for x in range(2):
            for core in range(2):
                to = move(z, x, core)
                pairs.append(((z * 2 + x) * 2 + core, (to[0] * 2 + to[1]) * 2 + to[2]))
    return pairs


def after(value, *others):
    return lax.optimization_barrier((value, *others))[0]


def dense_experts(normed, out_proj, expert_in, expert_out, route_ids, route_weights):
    frames = route_ids.shape[0]
    wide = lax.axis_size("wide")
    ring = 2 * wide
    z = lax.axis_index("wide")
    x, core = lax.axis_index("narrow") // 2, lax.axis_index("narrow") % 2
    place = jnp.where(x == 0, z, ring - 1 - z)
    axes = ("wide", "narrow")

    def send(value, move):
        return lax.ppermute(value, axes, routes(wide, move))

    def to_core(value):
        return send(value, lambda z, x, c: (z, x, 1 - c))

    def to_x(value):
        return send(value, lambda z, x, c: (z, 1 - x, c))

    def along(value, step):
        def move(z, x, c):
            p = ((z if x == 0 else ring - 1 - z) + step) % ring
            return (p, 0, c) if p < wide else (ring - 1 - p, 1, c)

        return send(value, move)

    out_other, in_other, down_other = to_core(out_proj), to_core(expert_in), to_core(expert_out)

    experts = wide * 4
    gates = jnp.sum(
        jnp.where(route_ids[:, :, None] == jnp.arange(experts), route_weights[:, :, None], 0.0), axis=1
    )
    normed_top, normed_bottom, other = lax.optimization_barrier((*normed, to_x(gates)))
    gates = jnp.where(x == 0, jnp.stack([gates, other]), jnp.stack([other, gates]))[:, None]

    halves = range(2)
    size = frames // 2
    hidden_width = expert_out.shape[0]
    columns = lax.optimization_barrier(
        jnp.where(
            core == 0,
            jnp.concatenate([out_proj, out_other], axis=1),
            jnp.concatenate([out_other, out_proj], axis=1),
        )
    )
    columns, normed_bottom = lax.optimization_barrier((columns, normed_bottom))
    sent = [to_x(normed_top), to_x(normed_bottom)]

    def project(rows):
        return jnp.dot(rows, columns, preferred_element_type=jnp.float32).astype(jnp.bfloat16)

    own = [project(normed_top), project(normed_bottom)]
    rows = []
    for h in halves:
        back = to_x(project(sent[h]))
        rows.append(
            jnp.where(
                x == 0,
                jnp.concatenate([own[h], back], axis=1),
                jnp.concatenate([back, own[h]], axis=1),
            )
        )

    rows[1], expert_in, expert_out = lax.optimization_barrier((rows[1], expert_in, expert_out))

    far = ring // 2
    fore_at, back_at = {0: rows}, {0: rows}
    for k in range(1, far):
        fore_at[k] = [along(fore_at[k - 1][h], 1) for h in halves]
        back_at[k] = [along(back_at[k - 1][h], -1) for h in halves]
        if k == far // 2:
            fore_at[k][0], gates = lax.optimization_barrier((fore_at[k][0], gates))
    last = [along(fore_at[far - 1][0], 1), along(back_at[far - 1][1], -1)]

    spread = [gates]
    for away in range(1, wide):
        spread.append(send(gates, lambda z, x, c: (z ^ away, x, c)))
    gates, bit = jnp.concatenate(spread, axis=1), 1
    while bit < wide:
        turned = jnp.concatenate([gates[:, (i ^ bit) : (i ^ bit) + 1] for i in range(wide)], axis=1)
        gates, bit = jnp.where(z & bit == 0, gates, turned), 2 * bit

    mine = (z * 2 + x) * 2 + core
    pair = jnp.stack([mine, mine + 1 - 2 * core])
    gates = jnp.sum(
        jnp.where(pair[:, None] == jnp.arange(experts), gates[..., None, :], 0.0), axis=-1
    )
    gates = jnp.concatenate([gates[0], gates[1, ::-1]])
    gates = lax.dynamic_slice_in_dim(jnp.concatenate([gates, gates]), place, ring, 0)

    joined_in = jnp.concatenate(
        [
            expert_in[:, :hidden_width],
            in_other[:, :hidden_width],
            expert_in[:, hidden_width:],
            in_other[:, hidden_width:],
        ],
        axis=1,
    )
    joined_down = jnp.concatenate([expert_out, down_other], axis=0)
    joined_in, joined_down = lax.optimization_barrier((joined_in, joined_down))
    is_first = jnp.arange(2 * hidden_width)[None, :] < hidden_width

    def run_experts(parts, gate):
        v = jnp.dot(jnp.concatenate(parts), joined_in, preferred_element_type=jnp.float32)
        hidden = jax.nn.silu(v[:, : 2 * hidden_width]) * v[:, 2 * hidden_width :]
        hidden = (hidden * jnp.where(is_first, gate[:, :1], gate[:, 1:])).astype(jnp.bfloat16)
        return jnp.dot(hidden, joined_down, preferred_element_type=jnp.float32)

    def hop_experts(k, tie):
        parts = [after(part, tie) for part in (rows if k == 0 else [*back_at[k], *fore_at[k]])]
        if k == 0:
            return run_experts(parts, gates[0]), None
        total = run_experts(parts, jnp.concatenate([gates[k], gates[ring - k]]))
        cut = [total[i * size : (i + 1) * size] for i in range(len(parts))]
        return cut[:2], cut[2:]

    total = run_experts(last, gates[far]).astype(jnp.bfloat16)
    fore, back = [along(total[:size], 1), None], [None, along(total[size:], -1)]
    ahead, behind = hop_experts(far - 1, total)
    groups = [((fore, 1, 1), (back, -1, 0)), ((fore, 1, 0), (back, -1, 1))]
    for k in range(far - 1, 0, -1):
        before = ()
        for group in groups:
            loads = []
            for way, step, h in group:
                load = (ahead if step > 0 else behind)[h]
                if way[h] is not None:
                    load = load + after(way[h], *before).astype(jnp.float32)
                loads.append(load.astype(jnp.bfloat16))
            for (way, step, h), load in zip(group, loads):
                way[h] = along(load, step)
            if not before:
                coming = hop_experts(k - 1, loads[0])
                before = tuple(loads)
        ahead, behind = coming
    total = ahead + jnp.concatenate(fore).astype(jnp.float32) + jnp.concatenate(back).astype(jnp.float32)
    return (jnp.concatenate(rows).astype(jnp.float32) + total).astype(jnp.bfloat16)


def routed_experts(normed, out_proj, expert_in, expert_out, route_ids, route_weights):
    mixer_rows = jnp.dot(
        normed,
        lax.all_gather(out_proj, "narrow", axis=1, tiled=True),
        preferred_element_type=jnp.float32,
    ).astype(jnp.bfloat16)
    frames_here = mixer_rows.shape[0]
    model_width = mixer_rows.shape[1]
    topk_count = route_ids.shape[1]
    local_experts = expert_in.shape[0]
    devices = lax.axis_size(("wide", "narrow"))
    experts = local_experts * devices
    capacity = max(2, frames_here * topk_count * 5 // (4 * experts))
    flat_ids, positions = slot_positions(route_ids, experts)
    owners = jnp.arange(frames_here * topk_count, dtype=jnp.int32) // topk_count
    slot_table = (
        jnp.full((experts, capacity), frames_here, jnp.int32).at[flat_ids, positions].set(owners)
    )
    padded = jnp.concatenate([mixer_rows, jnp.zeros((1, model_width), jnp.bfloat16)], axis=0)
    outgoing = padded[slot_table]
    hidden_width = expert_out.shape[1]
    projected = jnp.einsum(
        "nlcd,ldf->nlcf",
        lax.all_to_all(
            outgoing.reshape(devices, local_experts, capacity, model_width),
            ("wide", "narrow"),
            split_axis=0,
            concat_axis=0,
            tiled=True,
        ),
        expert_in,
        preferred_element_type=jnp.float32,
    )
    hidden = (jax.nn.silu(projected[..., :hidden_width]) * projected[..., hidden_width:]).astype(
        jnp.bfloat16
    )
    returned = lax.all_to_all(
        jnp.einsum("nlcf,lfd->nlcd", hidden, expert_out, preferred_element_type=jnp.float32).astype(
            jnp.bfloat16
        ),
        ("wide", "narrow"),
        split_axis=0,
        concat_axis=0,
        tiled=True,
    )
    returned = returned.reshape(experts, capacity, model_width)
    picked = returned[flat_ids, positions].reshape(frames_here, topk_count, model_width)
    expert_sum = jnp.einsum("tk,tkd->td", route_weights, picked.astype(jnp.float32))
    layer_out = (mixer_rows.astype(jnp.float32) + expert_sum).astype(jnp.bfloat16)
    return layer_out


def solution(mesh):
    placed = (
        P(("groups", "wide", "narrow"), None),
        P(("groups", "wide", "narrow"), None),
        P(("groups", "wide", "narrow"), None),
        P(("groups", "wide", "narrow"), None),
        P(("groups", "wide", "narrow"), None),
        P(),
        P(),
        P(),
        P(),
        P(("groups", "wide", "narrow"), None, None, None),
        P(None, "narrow"),
        P(("wide", "narrow"), None, None),
        P(("wide", "narrow"), None, None),
        P(("groups", "wide", "narrow"), None),
        P(("groups", "wide", "narrow"), None),
    )
    return jax.shard_map(
        body,
        mesh=mesh,
        in_specs=placed,
        out_specs=(
            P(("groups", "wide", "narrow"), None),
            P(("groups", "wide", "narrow"), None, None, None),
        ),
        check_vma=False,
    )
```

```python
import functools

import jax
import jax.numpy as jnp
from jax import lax
from jax.experimental import pallas as pl
from jax.experimental.pallas import tpu as pltpu
from jax.sharding import PartitionSpec as P

epsilon = 1e-05


CHUNK = 8
NT = (((1,), (1,)), ((), ()))
TN = (((0,), (0,)), ((), ()))


def column_of(row_ref):
    count = row_ref.shape[1]
    i = lax.broadcasted_iota(jnp.int32, (count, count), 0)
    j = lax.broadcasted_iota(jnp.int32, (count, count), 1)
    return jnp.sum(jnp.where(i == j, row_ref[...], 0.0), axis=1, keepdims=True)


def decays(dt_ref, bias_ref, a_ref, step_ref, decay_ref):
    frames = dt_ref.shape[1]
    step_size = jax.nn.softplus(dt_ref[...] + column_of(bias_ref))
    rise = step_size * -jnp.exp(column_of(a_ref))
    s = lax.broadcasted_iota(jnp.int32, (frames, frames), 0)
    t = lax.broadcasted_iota(jnp.int32, (frames, frames), 1)
    upto = jnp.where(s <= t, 1.0, 0.0)
    step_ref[...] = step_size
    decay_ref[...] = jnp.dot(
        rise, upto, precision=lax.Precision.HIGHEST, preferred_element_type=jnp.float32
    )


def mixer_kernel(
    skip_ref,
    x_ref,
    z_ref,
    b_ref,
    c_ref,
    dt_ref,
    bias_ref,
    a_ref,
    gain_ref,
    state_ref,
    top_ref,
    bottom_ref,
    g_ref,
    ss_ref,
    step_ref,
    decay_ref,
):
    i = pl.program_id(0)
    frames, width = x_ref.shape
    head = width // CHUNK
    pl.when(i == 0)(lambda: decays(dt_ref, bias_ref, a_ref, step_ref, decay_ref))
    chunk = pl.ds(pl.multiple_of(i * CHUNK, CHUNK), CHUNK)
    step_size, decay = step_ref[chunk, :], decay_ref[chunk, :]
    decay_col = decay.T
    carry_col = jnp.exp(decay_col)
    t = lax.broadcasted_iota(jnp.int32, (frames, frames), 0)
    s = lax.broadcasted_iota(jnp.int32, (frames, frames), 1)
    c = c_ref[...]
    scores = lax.dot_general(c, b_ref[...], NT, preferred_element_type=jnp.float32)
    scores = jnp.where(s <= t, scores, 0.0)
    cc = jnp.concatenate([c, c], axis=1)
    left = lax.broadcasted_iota(jnp.int32, (frames, 2 * head), 1) < head
    squares = None
    for pair in range(CHUNK // 2):
        mixes = []
        for h in (2 * pair, 2 * pair + 1):
            spread = jnp.exp(jnp.minimum(decay_col[:, h : h + 1] - decay[h : h + 1, :], 0.0))
            mixes.append((spread * (scores * step_size[h : h + 1, :])).astype(jnp.bfloat16))
        at = slice(2 * head * pair, 2 * head * (pair + 1))
        x = x_ref[:, at]
        zero = jnp.zeros_like(x)
        y = jnp.dot(
            jnp.concatenate(mixes, axis=1),
            jnp.concatenate([jnp.where(left, x, zero), jnp.where(left, zero, x)], axis=0),
            preferred_element_type=jnp.float32,
        )
        state = state_ref[at, :]
        high = state.astype(jnp.bfloat16)
        low = (state - high.astype(jnp.float32)).astype(jnp.bfloat16)
        carried = lax.dot_general(
            cc, jnp.concatenate([high, low], axis=1), NT, preferred_element_type=jnp.float32
        )
        factor = jnp.where(
            left, carry_col[:, 2 * pair : 2 * pair + 1], carry_col[:, 2 * pair + 1 : 2 * pair + 2]
        )
        skip = jnp.where(left[:1], skip_ref[i * CHUNK + 2 * pair], skip_ref[i * CHUNK + 2 * pair + 1])
        mixed = y + factor * carried + skip * x.astype(jnp.float32)
        z = z_ref[:, at].astype(jnp.float32)
        g = mixed * jax.nn.silu(z)
        g_ref[i, :, at] = g
        squares = g * g if squares is None else squares + g * g

    @pl.when(i == 0)
    def _():
        ss_ref[...] = squares

    @pl.when(i > 0)
    def _():
        ss_ref[...] += squares

    steps = g_ref.shape[0]

    @pl.when(i == steps - 1)
    def _():
        mean = jnp.sum(ss_ref[...], axis=1, keepdims=True) / (steps * width)
        scale = lax.rsqrt(mean + epsilon)
        for j in range(steps):
            at = slice(j * width, (j + 1) * width)
            normed = (g_ref[j] * scale * gain_ref[:, at]).astype(jnp.bfloat16)
            top_ref[:, at] = normed[: frames // 2]
            bottom_ref[:, at] = normed[frames // 2 :]


def state_kernel(x_ref, b_ref, dt_ref, bias_ref, a_ref, state_ref, out_ref, step_ref, decay_ref):
    i = pl.program_id(0)
    frames, width = x_ref.shape
    head = width // CHUNK
    pl.when(i == 0)(lambda: decays(dt_ref, bias_ref, a_ref, step_ref, decay_ref))
    chunk = pl.ds(pl.multiple_of(i * CHUNK, CHUNK), CHUNK)
    step_size, decay = step_ref[chunk, :], decay_ref[chunk, :]
    end = decay[:, frames - 1 : frames]
    tail = (jnp.exp(end - decay) * step_size).T
    kept = jnp.exp(end)
    left = lax.broadcasted_iota(jnp.int32, (frames, 2 * head), 1) < head
    upper = lax.broadcasted_iota(jnp.int32, (2 * head, b_ref.shape[1]), 0) < head
    for pair in range(CHUNK // 2):
        at = slice(2 * head * pair, 2 * head * (pair + 1))
        factor = jnp.where(left, tail[:, 2 * pair : 2 * pair + 1], tail[:, 2 * pair + 1 : 2 * pair + 2])
        scaled = (x_ref[:, at].astype(jnp.float32) * factor).astype(jnp.bfloat16)
        added = lax.dot_general(scaled, b_ref[...], TN, preferred_element_type=jnp.float32)
        keep = jnp.where(upper, kept[2 * pair : 2 * pair + 1, :], kept[2 * pair + 1 : 2 * pair + 2, :])
        out_ref[at, :] = keep * state_ref[at, :] + added


def ssm_mixer(
    ssm_input, gate_input, b_proj, c_proj, dt_raw, a_log, dt_bias, d_skip, norm_gain, state_in
):
    frames, width = ssm_input.shape
    heads, head, inner = state_in.shape
    steps = heads // CHUNK
    part = width // steps
    state = state_in.reshape(width, inner)
    dt = dt_raw.T
    column = pl.BlockSpec((frames, part), lambda i: (0, i))
    whole = pl.BlockSpec((frames, inner), lambda i: (0, 0))
    per_head = pl.BlockSpec((heads, frames), lambda i: (0, 0))
    scalar = pl.BlockSpec((1, heads), lambda i: (0, 0))
    rows = pl.BlockSpec((part, inner), lambda i: (i, 0))
    full_row = pl.BlockSpec((1, width), lambda i: (0, 0))
    tables = [pltpu.VMEM((heads, frames), jnp.float32)] * 2
    normed = pl.pallas_call(
        mixer_kernel,
        grid=(steps,),
        in_specs=[
            pl.BlockSpec(memory_space=pltpu.SMEM),
            column,
            column,
            whole,
            whole,
            per_head,
            scalar,
            scalar,
            full_row,
            rows,
        ],
        out_specs=[pl.BlockSpec((frames // 2, width), lambda i: (0, 0))] * 2,
        out_shape=[jax.ShapeDtypeStruct((frames // 2, width), jnp.bfloat16)] * 2,
        scratch_shapes=[
            pltpu.VMEM((steps, frames, part), jnp.float32),
            pltpu.VMEM((frames, 2 * head), jnp.float32),
            *tables,
        ],
        compiler_params=pltpu.CompilerParams(vmem_limit_bytes=56 << 20),
        cost_estimate=pl.CostEstimate(flops=400_000_000, bytes_accessed=6_000_000, transcendentals=2_000_000),
        name="mixer",
    )(
        d_skip,
        ssm_input,
        gate_input,
        b_proj,
        c_proj,
        dt,
        dt_bias[None, :],
        a_log[None, :],
        norm_gain[None, :],
        state,
    )

    def state_next(ssm_input):
        out = pl.pallas_call(
            state_kernel,
            grid=(steps,),
            in_specs=[column, whole, per_head, scalar, scalar, rows],
            out_specs=rows,
            out_shape=jax.ShapeDtypeStruct((width, inner), jnp.float32),
            scratch_shapes=tables,
            compiler_params=pltpu.CompilerParams(vmem_limit_bytes=16 << 20),
            cost_estimate=pl.CostEstimate(flops=70_000_000, bytes_accessed=3_000_000, transcendentals=20_000),
            name="state",
        )(ssm_input, b_proj, dt, dt_bias[None, :], a_log[None, :], state)
        return out.reshape(heads, head, inner)

    return (normed, state_next)


def slot_positions(route_ids, experts):
    flat_ids = route_ids.reshape(-1)
    onehot = (flat_ids[:, None] == jnp.arange(experts, dtype=jnp.int32)[None, :]).astype(jnp.int32)
    earlier = jnp.cumsum(onehot, axis=0) - onehot
    return (flat_ids, jnp.sum(earlier * onehot, axis=1))


def body(
    ssm_input,
    gate_input,
    b_proj,
    c_proj,
    dt_raw,
    a_log,
    dt_bias,
    d_skip,
    norm_gain,
    state_in,
    out_proj,
    expert_in,
    expert_out,
    route_ids,
    route_weights,
):
    normed, state_next = ssm_mixer(
        ssm_input,
        gate_input,
        b_proj,
        c_proj,
        dt_raw,
        a_log,
        dt_bias,
        d_skip,
        norm_gain,
        state_in[0],
    )
    frames_here, topk_count = route_ids.shape
    local_experts = expert_in.shape[0]
    experts = local_experts * lax.axis_size(("wide", "narrow"))
    wide, narrow = lax.axis_size("wide"), lax.axis_size("narrow")
    if experts <= 4 * topk_count and narrow == 4 and wide & (wide - 1) == 0 and local_experts == 1:
        layer_out, state = dense_experts(
            normed,
            out_proj,
            expert_in[0],
            expert_out[0],
            route_ids,
            route_weights,
            lambda tie: state_next(after(ssm_input, tie)),
        )
    else:
        normed = jnp.concatenate(normed)
        layer_out = routed_experts(normed, out_proj, expert_in, expert_out, route_ids, route_weights)
        state = state_next(ssm_input)
    return (layer_out, state[None])


def routes(wide, move):
    pairs = []
    for z in range(wide):
        for x in range(2):
            for core in range(2):
                to = move(z, x, core)
                pairs.append(((z * 2 + x) * 2 + core, (to[0] * 2 + to[1]) * 2 + to[2]))
    return pairs


def after(value, *others):
    return lax.optimization_barrier((value, *others))[0]


def dense_experts(normed, out_proj, expert_in, expert_out, route_ids, route_weights, state_next):
    frames = route_ids.shape[0]
    wide = lax.axis_size("wide")
    ring = 2 * wide
    z = lax.axis_index("wide")
    x, core = lax.axis_index("narrow") // 2, lax.axis_index("narrow") % 2
    place = jnp.where(x == 0, z, ring - 1 - z)
    axes = ("wide", "narrow")

    def send(value, move):
        return lax.ppermute(value, axes, routes(wide, move))

    def to_core(value):
        return send(value, lambda z, x, c: (z, x, 1 - c))

    def to_x(value):
        return send(value, lambda z, x, c: (z, 1 - x, c))

    def along(value, step):
        def move(z, x, c):
            p = ((z if x == 0 else ring - 1 - z) + step) % ring
            return (p, 0, c) if p < wide else (ring - 1 - p, 1, c)

        return send(value, move)

    out_other, in_other, down_other = to_core(out_proj), to_core(expert_in), to_core(expert_out)

    experts = wide * 4
    gates = jnp.sum(
        jnp.where(route_ids[:, :, None] == jnp.arange(experts), route_weights[:, :, None], 0.0), axis=1
    )
    normed_top, normed_bottom, other = lax.optimization_barrier((*normed, to_x(gates)))
    gates = jnp.where(x == 0, jnp.stack([gates, other]), jnp.stack([other, gates]))[:, None]

    halves = range(2)
    size = frames // 2
    hidden_width = expert_out.shape[0]
    sent = [to_x(normed_top), to_x(normed_bottom)]

    step = 1
    while step < wide:
        other = send(gates, lambda z, x, c: (z ^ step, x, c))
        gates = jnp.where(
            z & step == 0,
            jnp.concatenate([gates, other], axis=1),
            jnp.concatenate([other, gates], axis=1),
        )
        step *= 2
    sent[1], gates = lax.optimization_barrier((sent[1], gates))
    mine = (z * 2 + x) * 2 + core
    pair = jnp.stack([mine, mine + 1 - 2 * core])
    gates = jnp.sum(
        jnp.where(pair[:, None] == jnp.arange(experts), gates[..., None, :], 0.0), axis=-1
    )
    gates = jnp.concatenate([gates[0], gates[1, ::-1]])
    gates = lax.dynamic_slice_in_dim(jnp.concatenate([gates, gates]), place, ring, 0)

    columns = lax.optimization_barrier(
        jnp.where(
            core == 0,
            jnp.concatenate([out_proj, out_other], axis=1),
            jnp.concatenate([out_other, out_proj], axis=1),
        )
    )

    def project(rows):
        return jnp.dot(rows, columns, preferred_element_type=jnp.float32).astype(jnp.bfloat16)

    own = [project(normed_top), project(normed_bottom)]
    rows, peer = [], None
    for h in halves:
        arrived = sent[h]
        if peer is not None:
            arrived = after(arrived, peer)
        peer = project(arrived)
        back = to_x(peer)
        rows.append(
            jnp.where(
                x == 0,
                jnp.concatenate([own[h], back], axis=1),
                jnp.concatenate([back, own[h]], axis=1),
            )
        )

    rows[1], expert_in, expert_out = lax.optimization_barrier((rows[1], expert_in, expert_out))
    gate_in, up_in = expert_in[:, :hidden_width], expert_in[:, hidden_width:]

    far = ring // 2
    fore_at, back_at = {0: rows}, {0: rows}
    for k in range(1, far):
        fore_at[k] = [along(fore_at[k - 1][h], 1) for h in halves]
        back_at[k] = [along(back_at[k - 1][h], -1) for h in halves]
    last = [along(fore_at[far - 1][0], 1), along(back_at[far - 1][1], -1)]

    joined_in = jnp.concatenate(
        [gate_in, in_other[:, :hidden_width], up_in, in_other[:, hidden_width:]], axis=1
    )
    joined_down = jnp.concatenate([expert_out, down_other], axis=0)
    joined_in, joined_down = lax.optimization_barrier((joined_in, joined_down))
    is_first = jnp.arange(2 * hidden_width)[None, :] < hidden_width

    def run_experts(parts, gate):
        v = jnp.dot(jnp.concatenate(parts), joined_in, preferred_element_type=jnp.float32)
        hidden = jax.nn.silu(v[:, : 2 * hidden_width]) * v[:, 2 * hidden_width :]
        hidden = (hidden * jnp.where(is_first, gate[:, :1], gate[:, 1:])).astype(jnp.bfloat16)
        return jnp.dot(hidden, joined_down, preferred_element_type=jnp.float32)

    def hop_experts(k, tie):
        parts = rows if k == 0 else [*back_at[k], *fore_at[k]]
        gate = gates[0] if k == 0 else jnp.concatenate([gates[k], gates[ring - k]])
        parts = [after(part, tie) for part in parts]
        total = run_experts(parts, gate)
        cut = [total[i * size : (i + 1) * size] for i in range(len(parts))]
        return cut[:2], cut[2:]

    total = run_experts(last, gates[far]).astype(jnp.bfloat16)
    fore, back = [along(total[:size], 1), None], [None, along(total[size:], -1)]
    ahead, behind = hop_experts(far - 1, total)
    tie = total
    for k in range(far - 1, 0, -1):
        if k > 1:
            coming = hop_experts(k - 1, tie)
        before = ()
        groups = [((fore, 1, ahead, h), (back, -1, behind, h)) for h in halves]
        if k == far - 1:
            groups = [((fore, 1, ahead, 1), (back, -1, behind, 0)), ((fore, 1, ahead, 0), (back, -1, behind, 1))]
        for group in groups:
            loads = []
            for way, step, totals, h in group:
                load = totals[h]
                if way[h] is not None:
                    load = load + after(way[h], *before).astype(jnp.float32)
                loads.append(load.astype(jnp.bfloat16))
            before = loads
            for (way, step, totals, h), load in zip(group, loads):
                way[h] = along(load, step)
        tie = loads[0]
        if k == 1:
            coming = hop_experts(0, tie)
            state = state_next(tie)
        ahead, behind = coming
    out = []
    for h in halves:
        total = ahead[h] + fore[h].astype(jnp.float32) + back[h].astype(jnp.float32)
        out.append((rows[h].astype(jnp.float32) + total).astype(jnp.bfloat16))
    return jnp.concatenate(out), state


def routed_experts(normed, out_proj, expert_in, expert_out, route_ids, route_weights):
    mixer_rows = jnp.dot(
        normed,
        lax.all_gather(out_proj, "narrow", axis=1, tiled=True),
        preferred_element_type=jnp.float32,
    ).astype(jnp.bfloat16)
    frames_here = mixer_rows.shape[0]
    model_width = mixer_rows.shape[1]
    topk_count = route_ids.shape[1]
    local_experts = expert_in.shape[0]
    devices = lax.axis_size(("wide", "narrow"))
    experts = local_experts * devices
    capacity = max(2, frames_here * topk_count * 5 // (4 * experts))
    flat_ids, positions = slot_positions(route_ids, experts)
    owners = jnp.arange(frames_here * topk_count, dtype=jnp.int32) // topk_count
    slot_table = (
        jnp.full((experts, capacity), frames_here, jnp.int32).at[flat_ids, positions].set(owners)
    )
    padded = jnp.concatenate([mixer_rows, jnp.zeros((1, model_width), jnp.bfloat16)], axis=0)
    outgoing = padded[slot_table]
    hidden_width = expert_out.shape[1]
    projected = jnp.einsum(
        "nlcd,ldf->nlcf",
        lax.all_to_all(
            outgoing.reshape(devices, local_experts, capacity, model_width),
            ("wide", "narrow"),
            split_axis=0,
            concat_axis=0,
            tiled=True,
        ),
        expert_in,
        preferred_element_type=jnp.float32,
    )
    hidden = (jax.nn.silu(projected[..., :hidden_width]) * projected[..., hidden_width:]).astype(
        jnp.bfloat16
    )
    returned = lax.all_to_all(
        jnp.einsum("nlcf,lfd->nlcd", hidden, expert_out, preferred_element_type=jnp.float32).astype(
            jnp.bfloat16
        ),
        ("wide", "narrow"),
        split_axis=0,
        concat_axis=0,
        tiled=True,
    )
    returned = returned.reshape(experts, capacity, model_width)
    picked = returned[flat_ids, positions].reshape(frames_here, topk_count, model_width)
    expert_sum = jnp.einsum("tk,tkd->td", route_weights, picked.astype(jnp.float32))
    layer_out = (mixer_rows.astype(jnp.float32) + expert_sum).astype(jnp.bfloat16)
    return layer_out


def solution(mesh):
    placed = (
        P(("groups", "wide", "narrow"), None),
        P(("groups", "wide", "narrow"), None),
        P(("groups", "wide", "narrow"), None),
        P(("groups", "wide", "narrow"), None),
        P(("groups", "wide", "narrow"), None),
        P(),
        P(),
        P(),
        P(),
        P(("groups", "wide", "narrow"), None, None, None),
        P(None, "narrow"),
        P(("wide", "narrow"), None, None),
        P(("wide", "narrow"), None, None),
        P(("groups", "wide", "narrow"), None),
        P(("groups", "wide", "narrow"), None),
    )
    return jax.shard_map(
        body,
        mesh=mesh,
        in_specs=placed,
        out_specs=(
            P(("groups", "wide", "narrow"), None),
            P(("groups", "wide", "narrow"), None, None, None),
        ),
        check_vma=False,
    )
```
